32 devices in a mesh: dp: 8 (over y, x, core), tm: 4 (over z).
Axes of the slice: x: 2, y: 2, z: 4, core: 2. Of those that a mesh axis runs over, the one named last changes fastest.
Arguments:
- tokens: bfloat16 [32, 2048, 512], P('dp', 'tm'), may hold values from -6 to 6
- lengths: int32 [32, 3], P('dp'), may hold values from 128 to 1791, as said below
- style: bfloat16 [32, 3, 128], P('dp'), may hold values from -6 to 6
- fc1_weight: bfloat16 [128, 1024], replicated, may hold values from -0.375 to 0.375
- fc1_bias: bfloat16 [1024], replicated, may hold values from -3 to 3
- conv1_kernel: bfloat16 [3, 512, 512], replicated, may hold values from -0.15625 to 0.15625
- fc2_weight: bfloat16 [128, 1024], replicated, may hold values from -0.375 to 0.375
- fc2_bias: bfloat16 [1024], replicated, may hold values from -3 to 3
- conv2_kernel: bfloat16 [3, 512, 512], replicated, may hold values from -0.15625 to 0.15625
- conv2_bias: bfloat16 [512], replicated, may hold values from -3 to 3
- out_grad: bfloat16 [32, 2048, 512], P('dp', 'tm'), may hold values from -6 to 6
Outputs:
- block_out: bfloat16 [32, 2048, 512], P('dp', 'tm')
- input_grad: bfloat16 [32, 2048, 512], P('dp', 'tm')
- style_grad: float32 [32, 3, 128], P('dp')
- fc1_weight_grad: float32 [128, 1024], replicated
- fc1_bias_grad: float32 [1024], replicated
- conv1_kernel_grad: float32 [3, 512, 512], replicated
- fc2_weight_grad: float32 [128, 1024], replicated
- fc2_bias_grad: float32 [1024], replicated
- conv2_kernel_grad: float32 [3, 512, 512], replicated
- conv2_bias_grad: float32 [512], replicated
The draws below stay inside these ranges and needn't reach their ends.
Inputs may be any that keep to these rules, and one draw needn't show every extreme that they name: `lengths`: every row ends in at least one frame of padding. Of each row's 3 utterances all but one have 512 // 4 to 170 frames, one of them exactly 128; the remaining one begins among the row's first 512 frames and ends among its last 512 frames.
All inputs are finite; a program needn't handle non-finite values.
Results may differ from the reference program's by a relative error of at most 0.0078.
Values may be sent and summed in bfloat16 or wider, within the bound.
No kernel may reach another device: no remote copies, remote signals or barrier semaphores. Data moves between devices by JAX's collectives and lax.ppermute only.
A program may use at most 128 MiB of HBM per device.

```python
import jax
import jax.numpy as jnp
from jax import lax

C = 512
STYLE = 128
KERNEL = 3
SEGS = 3
F_DEV = 512
FRAMES = 2048
ROWS = 32


def draw_lengths(key, part):
    key = jax.random.fold_in(key, 7)
    streams = jax.random.split(key, 4)
    row_ids = jnp.arange(ROWS, dtype=jnp.int32)[:, None]
    shorts = jax.random.randint(streams[0], (ROWS, SEGS), F_DEV // 4, F_DEV // 3 + 1)
    shorts = jnp.where(row_ids == 0, F_DEV // 4, shorts)
    long_at = jax.random.randint(streams[1], (ROWS, 1), 0, SEGS)
    least_at = (long_at + jax.random.randint(streams[2], (ROWS, 1), 1, SEGS)) % SEGS
    padding = jax.random.randint(streams[3], (ROWS, 1), 1, F_DEV // 8 + 1)
    padding = jnp.where(row_ids == 0, 1, padding)
    columns = jnp.arange(SEGS, dtype=jnp.int32)[None, :]
    shorts = jnp.where(columns == least_at, F_DEV // 4, shorts)
    shorts = jnp.where(columns == long_at, 0, shorts)
    longest = FRAMES - padding - jnp.sum(shorts, axis=1, keepdims=True)
    return jnp.where(columns == long_at, longest, shorts).astype(jnp.int32)


def steps_of(own_key, shape, cuts, low, largest):
    level, own = 1.0, jax.random.fold_in(own_key, 6)
    for position, shards_of in cuts:
        steps = jnp.exp(jax.random.uniform(jax.random.fold_in(own, position), (shards_of,), jnp.float32, low / len(cuts), largest / len(cuts)))
        level = level * jnp.repeat(steps, shape[position] // shards_of).reshape([-1 if axis == position else 1 for axis in range(len(shape))])
    return level


def noise(stream_key, extent, scale, bound, cuts=(), held_as=jnp.bfloat16):
    values = jax.random.normal(stream_key, extent, jnp.float32) * scale
    if len(cuts) > 0:
        values = steps_of(stream_key, extent, cuts, -0.22, 0.18) * values
    return jnp.clip(values, min=-bound, max=bound).astype(held_as)


def setup_inputs(seed: int = 0) -> dict:
    key_of = jax.random.split(jax.random.key(seed), 12)
    tokens = noise(key_of[0], (ROWS, FRAMES, C), 1.0, 6.0, ((0, 8), (1, 4)))
    lengths = draw_lengths(jax.random.fold_in(key_of[11], 71), 0)
    style = noise(key_of[2], (ROWS, SEGS, STYLE), 1.0, 6.0, ((0, 8),))
    fc1_weight = noise(key_of[3], (STYLE, 2 * C), (2 * STYLE) ** -0.5, 0.375)
    fc1_bias = noise(key_of[4], (2 * C,), 0.5, 3.0)
    conv1_kernel = noise(key_of[5], (KERNEL, C, C), (KERNEL * C) ** -0.5, 0.15625)
    fc2_weight = noise(key_of[6], (STYLE, 2 * C), (2 * STYLE) ** -0.5, 0.375)
    fc2_bias = noise(key_of[7], (2 * C,), 0.5, 3.0)
    conv2_kernel = noise(key_of[8], (KERNEL, C, C), (KERNEL * C) ** -0.5, 0.15625)
    conv2_bias = noise(key_of[9], (C,), 0.5, 3.0)
    out_grad = noise(key_of[10], (ROWS, FRAMES, C), 1.0, 6.0, ((0, 8), (1, 4)))
    return dict(tokens=tokens, lengths=lengths, style=style, fc1_weight=fc1_weight, fc1_bias=fc1_bias, conv1_kernel=conv1_kernel, fc2_weight=fc2_weight, fc2_bias=fc2_bias, conv2_kernel=conv2_kernel, conv2_bias=conv2_bias, out_grad=out_grad)


@jax.custom_vjp
def low(v):
    return lax.optimization_barrier(v.astype(jnp.bfloat16)).astype(jnp.float32)

@jax.custom_vjp
def low_back(v):
    return v

def low_keep(v):
    return (low(v), None)

def low_pass(kept, grad):
    return (grad,)

def back_keep(v):
    return (v, None)

def back_low(kept, grad):
    return (low(grad),)
low.defvjp(low_keep, low_pass)
low_back.defvjp(back_keep, back_low)
EPSILON = 1e-05
ROOT_HALF = 0.7071067811865476
HIGHEST_PREC = lax.Precision.HIGHEST

def row_tables(lengths_row):
    seg_ends = jnp.cumsum(lengths_row).astype(jnp.int32)
    starts = (seg_ends - lengths_row).astype(jnp.int32)
    frame_index = jnp.arange(-1, FRAMES + 1, dtype=jnp.int32)
    segment = lax.optimization_barrier(jnp.sum((frame_index[:, None] >= seg_ends[None, :]).astype(jnp.int32), axis=1))
    centre = segment[1:-1]
    keep_prev = (segment[:-2] == centre).astype(jnp.float32)[:, None]
    keep_next = (segment[2:] == centre).astype(jnp.float32)[:, None]
    inner_index = frame_index[1:-1]
    onehot = ((inner_index[:, None] >= starts[None, :]) & (inner_index[:, None] < seg_ends[None, :])).astype(jnp.float32)
    live_mask = lax.optimization_barrier(jnp.sum(onehot, axis=1, keepdims=True))
    counts = lengths_row.astype(jnp.float32)[:, None]
    return (onehot, live_mask, counts, keep_prev, keep_next)

def adain_norm(signal, style_row, weight, bias, onehot, counts):
    seg_sums = jnp.dot(onehot.T, signal, precision=HIGHEST_PREC)
    seg_squares = jnp.dot(onehot.T, signal * signal, precision=HIGHEST_PREC)
    seg_mean = seg_sums / counts
    seg_rstd = lax.rsqrt(seg_squares / counts - seg_mean * seg_mean + EPSILON)
    affine = jnp.dot(style_row, weight, precision=HIGHEST_PREC) + bias
    gamma_seg = affine[:, :C]
    beta_seg = affine[:, C:]
    normed = (signal - jnp.dot(onehot, seg_mean, precision=HIGHEST_PREC)) * jnp.dot(onehot, seg_rstd, precision=HIGHEST_PREC)
    return (1.0 + jnp.dot(onehot, gamma_seg, precision=HIGHEST_PREC)) * normed + jnp.dot(onehot, beta_seg, precision=HIGHEST_PREC)

def convolve(lowered, kernel, keep_prev, keep_next):
    zero_row = jnp.zeros((1, lowered.shape[1]), jnp.float32)
    before = jnp.concatenate([zero_row, lowered[:-1]], axis=0) * keep_prev
    after_rows = jnp.concatenate([lowered[1:], zero_row], axis=0) * keep_next
    return jnp.dot(before, kernel[0], precision=HIGHEST_PREC) + jnp.dot(lowered, kernel[1], precision=HIGHEST_PREC) + jnp.dot(after_rows, kernel[2], precision=HIGHEST_PREC)

def res_block(signal, style_row, weights, tables):
    fc1_weight, fc1_bias, conv1_kernel, fc2_weight, fc2_bias, conv2_kernel, conv2_bias = weights
    onehot, live_mask, counts, keep_prev, keep_next = tables
    low1 = low(live_mask * jax.nn.silu(adain_norm(signal, style_row, fc1_weight, fc1_bias, onehot, counts)))
    hidden = low_back(convolve(low1, conv1_kernel, keep_prev, keep_next))
    low2 = low(live_mask * jax.nn.silu(adain_norm(hidden, style_row, fc2_weight, fc2_bias, onehot, counts)))
    branch = live_mask * low_back(convolve(low2, conv2_kernel, keep_prev, keep_next) + conv2_bias)
    return (signal + branch) * ROOT_HALF

def reference(tokens, lengths, style, fc1_weight, fc1_bias, conv1_kernel, fc2_weight, fc2_bias, conv2_kernel, conv2_bias, out_grad):
    weights = tuple((weight.astype(jnp.float32) for weight in (fc1_weight, fc1_bias, conv1_kernel, fc2_weight, fc2_bias, conv2_kernel, conv2_bias)))

    def one_row(totals, row_data):
        tokens_row, lengths_row, style_row, grad_row = row_data
        tables = row_tables(lengths_row)

        def apply_block(signal, style_value, *params):
            return res_block(signal, style_value, params, tables)
        result, pull_back = jax.vjp(apply_block, tokens_row.astype(jnp.float32), style_row.astype(jnp.float32), *weights)
        gradients = pull_back(grad_row.astype(jnp.float32))
        totals = tuple((total + extra for total, extra in zip(totals, gradients[2:])))
        return (totals, (result.astype(jnp.bfloat16), gradients[0].astype(jnp.bfloat16), gradients[1]))
    initial = tuple((jnp.zeros(weight.shape, jnp.float32) for weight in weights))
    totals, stacked_rows = lax.scan(one_row, initial, (tokens, lengths, style, out_grad))
    return (stacked_rows[0], stacked_rows[1], stacked_rows[2], totals[0], totals[1], totals[2], totals[3], totals[4], totals[5], totals[6])
```

```python
import functools

import jax
import jax.numpy as jnp
from jax import lax
from jax.experimental import pallas as pl
from jax.experimental.pallas import tpu as pltpu
from jax.sharding import Mesh, PartitionSpec as P

EPSILON = 1e-05
ROOT_HALF = 0.7071067811865476
SEGS = 3
PAD = 16
CHUNK = 64
EDGE = 8 + 16
F32 = jnp.float32
BF16 = jnp.bfloat16
VMEM_MIB = 32


class Row:
    def __init__(self, len_ref, r, frames):
        self.frames = frames
        self.z = lax.axis_index("tm")
        self.counts = [len_ref[r, s] for s in range(SEGS)]
        l0, l1, l2 = self.counts
        start = -self.z * frames
        e0 = start + l0
        e1 = e0 + l1
        e2 = e1 + l2
        self.begins = [start, e0, e1]
        self.ends = [e0, e1, e2]
        self.long_at = jnp.where(l0 >= jnp.maximum(l1, l2), 0, jnp.where(l1 >= l2, 1, 2))
        self.long_begin = self.of_long(self.begins)
        self.long_end = self.of_long(self.ends)

    def of_long(self, values):
        return jnp.where(
            self.long_at == 0, values[0], jnp.where(self.long_at == 1, values[1], values[2])
        )

    def segment(self, t):
        return sum((t >= e).astype(jnp.int32) for e in self.ends)

    def chunks(self, uniform_fn, mixed_fn):
        def body(i, carry):
            t0 = pl.multiple_of(i * CHUNK, CHUNK)
            first, last = self.segment(t0), self.segment(t0 + CHUNK - 1)
            uniform = jnp.logical_and(first == last, first < SEGS)

            @pl.when(uniform)
            def _():
                uniform_fn(t0, first)

            @pl.when(jnp.logical_not(uniform))
            def _():
                mixed_fn(t0)

            return carry

        lax.fori_loop(0, self.frames // CHUNK, body, 0)


def frame_ids(t0, rows, width):
    return t0 + lax.broadcasted_iota(jnp.int32, (rows, width), 0)


def pick(tab_ref, base, t, row):
    value = jnp.where(t >= row.ends[0], tab_ref[base + 1 : base + 2, :], tab_ref[base : base + 1, :])
    return jnp.where(t >= row.ends[1], tab_ref[base + 2 : base + 3, :], value)


def row_of(tab_ref, base, s):
    return tab_ref[pl.ds(base + s, 1), :]


def fold(x):
    return jnp.sum(x.reshape(x.shape[0] // 8, 8, x.shape[1]), axis=0)


def add_sums(acc_ref, s, first, second):
    acc_ref[s] += fold(first)
    acc_ref[4 + s] += fold(second)


def add_masked_sums(acc_ref, t, row, first, second):
    for s in range(SEGS):
        inside = jnp.logical_and(t >= row.begins[s], t < row.ends[s])
        add_sums(acc_ref, s, jnp.where(inside, first, 0.0), jnp.where(inside, second, 0.0))


def put_sums(acc_ref, st_ref, msg_ref, row, r):
    for s in range(SEGS):
        st_ref[s : s + 1, :] = jnp.sum(acc_ref[s], axis=0, keepdims=True)
        st_ref[SEGS + s : SEGS + s + 1, :] = jnp.sum(acc_ref[4 + s], axis=0, keepdims=True)
    st_ref[6:8, :] = jnp.zeros((2, st_ref.shape[1]), F32)
    for k in range(2):
        value = jnp.sum(acc_ref[4 * k + row.long_at], axis=0, keepdims=True)
        for d in range(msg_ref.shape[0]):
            msg_ref[d, pl.ds(2 * r + k, 1), :] = value


def sums_of(row, r, st_ref, rx_ref, s):
    out = []
    for k in range(2):
        total = rx_ref[0, pl.ds(2 * r + k, 1), :]
        for d in range(1, rx_ref.shape[0]):
            total = total + rx_ref[d, pl.ds(2 * r + k, 1), :]
        local = st_ref[SEGS * k + s : SEGS * k + s + 1, :]
        out.append(jnp.where(row.long_at == s, total, local))
    return out


def norm_of(row, r, st_ref, rx_ref, aff_ref, s):
    width = st_ref.shape[1]
    first, second = sums_of(row, r, st_ref, rx_ref, s)
    count = jnp.full((1, width), row.counts[s].astype(F32))
    mean = first / count
    rstd = lax.rsqrt(second / count - mean * mean + EPSILON)
    affine = aff_ref[pl.ds(SEGS * r + s, 1), :]
    return mean, rstd, 1.0 + affine[:, :width], affine[:, width:], count


def put_forward(row, r, st_ref, rx_ref, aff_ref, tab_ref):
    scales, shifts = [], []
    for s in range(SEGS):
        mean, rstd, gain, beta, _ = norm_of(row, r, st_ref, rx_ref, aff_ref, s)
        scales.append(gain * rstd)
        shifts.append(beta - mean * scales[-1])
        tab_ref[s : s + 1, :] = scales[s]
        tab_ref[SEGS + s : SEGS + s + 1, :] = shifts[s]
    tab_ref[6:7, :] = row.of_long(scales)
    tab_ref[7:8, :] = row.of_long(shifts)


def put_backward(row, r, st_ref, rx_ref, gst_ref, grx_ref, aff_ref, tab_ref):
    parts = [[], [], []]
    for s in range(SEGS):
        mean, rstd, gain, _, count = norm_of(row, r, st_ref, rx_ref, aff_ref, s)
        shift, scale = sums_of(row, r, gst_ref, grx_ref, s)
        scale = rstd * (scale - mean * shift)
        mean_g = gain * shift / count
        slope = rstd * rstd * (gain * scale / count)
        parts[0].append(gain * rstd)
        parts[1].append(-slope)
        parts[2].append(slope * mean - rstd * mean_g)
    for k in range(3):
        for s in range(SEGS):
            tab_ref[SEGS * k + s : SEGS * k + s + 1, :] = parts[k][s]
        tab_ref[9 + k : 10 + k, :] = row.of_long(parts[k])


def put_affine_grads(row, r, st_ref, rx_ref, gst_ref, aff_ref, out_ref, at):
    width = st_ref.shape[1]
    for s in range(SEGS):
        mean, rstd, _, _, _ = norm_of(row, r, st_ref, rx_ref, aff_ref, s)
        shift = gst_ref[s : s + 1, :]
        scale = rstd * (gst_ref[SEGS + s : SEGS + s + 1, :] - mean * shift)
        out_ref[pl.ds(4 * r + s, 1), at : at + width] = scale
        out_ref[pl.ds(4 * r + s, 1), at + width : at + 2 * width] = shift


def silu(a):
    half = 0.5 * a
    return half + half * jnp.tanh(half)


def silu_and_slope(a):
    gate = 0.5 + 0.5 * jnp.tanh(0.5 * a)
    low = a * gate
    return low, gate + low * (1.0 - gate)


def halo_tile(row, frames, width, left):
    t = frame_ids(-PAD if left else frames, PAD, width)
    near = jnp.logical_and(t >= -2, t < frames + 2)
    inside = jnp.logical_and(t >= row.long_begin, t < row.long_end)
    return t, jnp.logical_and(near, inside)


def edge_tile(rx_ref, row, r, t, at, left):
    last = rx_ref.shape[0] - 1
    source = jnp.maximum(row.z - 1, 0) if left else jnp.minimum(row.z + 1, last)
    e0 = rx_ref[source, pl.ds(8 + 4 * r + at, 1), :]
    e1 = rx_ref[source, pl.ds(8 + 4 * r + at + 1, 1), :]
    second = -1 if left else row.frames + 1
    return jnp.where(t == second, e1, e0)


def stack_taps(buf_ref, xs_ref, row, frames, forward, halo, low_ref=None):
    width = buf_ref.shape[1]
    before_at, after_at = (0, 2 * width) if forward else (2 * width, 0)
    base = PAD if halo else 0
    for i in range(frames // CHUNK):
        o, d = PAD + i * CHUNK, base + i * CHUNK
        centre = buf_ref[o : o + CHUNK, :].astype(BF16)
        xs_ref[d : d + CHUNK, width : 2 * width] = centre
        xs_ref[d : d + CHUNK, before_at : before_at + width] = buf_ref[o - 1 : o - 1 + CHUNK, :].astype(BF16)
        xs_ref[d : d + CHUNK, after_at : after_at + width] = buf_ref[o + 1 : o + 1 + CHUNK, :].astype(BF16)
        if low_ref is not None:
            low_ref[0, i * CHUNK : (i + 1) * CHUNK, :] = centre
    if halo:
        end = PAD + frames
        left, right = buf_ref[0:PAD, :], buf_ref[end : end + PAD, :]
        xs_ref[0:PAD, width : 2 * width] = left.astype(BF16)
        xs_ref[end : end + PAD, width : 2 * width] = right.astype(BF16)
        xs_ref[0:PAD, before_at : before_at + width] = pltpu.roll(left, 1, 0).astype(BF16)
        xs_ref[end : end + PAD, before_at : before_at + width] = buf_ref[end - 1 : end - 1 + PAD, :].astype(BF16)
        xs_ref[0:PAD, after_at : after_at + width] = buf_ref[1 : 1 + PAD, :].astype(BF16)
        xs_ref[end : end + PAD, after_at : after_at + width] = pltpu.roll(right, PAD - 1, 0).astype(BF16)
    for end in row.ends[:2]:
        for at, t in ((before_at, end), (after_at, end - 1)):

            @pl.when(jnp.logical_and(t >= 0, t < frames))
            def _(at=at, t=t):
                tile = pl.multiple_of((t // PAD) * PAD, PAD)
                rows = pl.ds(base + tile, PAD)
                value = xs_ref[rows, at : at + width].astype(F32)
                keep = frame_ids(tile, PAD, width) != t
                xs_ref[rows, at : at + width] = jnp.where(keep, value, 0.0).astype(BF16)


def times_transposed(xs, w_ref, width):
    out = None
    for k in range(3):
        part = lax.dot_general(
            xs[:, k * width : (k + 1) * width],
            w_ref[k * width : (k + 1) * width, :],
            (((1,), (1,)), ((), ())),
            preferred_element_type=F32,
        )
        out = part if out is None else out + part
    return out


def token_sums_kernel(len_ref, tok_ref, tok_head, tok_tail, og_head, og_tail, st_ref, msg_ref, acc_ref):
    r = pl.program_id(0)
    frames, width = tok_ref.shape[1:]
    row = Row(len_ref, r, frames)
    acc_ref[...] = jnp.zeros_like(acc_ref)

    def uniform(t0, s):
        v = tok_ref[0, pl.ds(t0, CHUNK), :].astype(F32)
        add_sums(acc_ref, s, v, v * v)

    def mixed(t0):
        v = tok_ref[0, pl.ds(t0, CHUNK), :].astype(F32)
        add_masked_sums(acc_ref, frame_ids(t0, CHUNK, width), row, v, v * v)

    row.chunks(uniform, mixed)
    put_sums(acc_ref, st_ref, msg_ref, row, r)
    for j, (head, tail) in enumerate(((tok_head, tok_tail), (og_head, og_tail))):
        first, last = head[0].astype(F32), tail[0].astype(F32)
        for i in range(2):
            to_left, to_right = first[i : i + 1, :], last[PAD - 2 + i : PAD - 1 + i, :]
            for d in range(msg_ref.shape[0]):
                msg_ref[d, pl.ds(8 + 4 * r + 2 * j + i, 1), :] = jnp.where(row.z < d, to_right, to_left)


def first_half_kernel(len_ref, tok_ref, st_ref, rx_ref, aff_ref, w_ref, low_ref, hid_ref, st2_ref, msg_ref,
                      buf_ref, xs_ref, tab_ref, acc_ref):
    r = pl.program_id(0)
    frames, width = tok_ref.shape[1:]
    row = Row(len_ref, r, frames)
    put_forward(row, r, st_ref, rx_ref, aff_ref, tab_ref)

    def uniform(t0, s):
        v = tok_ref[0, pl.ds(t0, CHUNK), :].astype(F32)
        buf_ref[pl.ds(PAD + t0, CHUNK), :] = silu(v * row_of(tab_ref, 0, s) + row_of(tab_ref, SEGS, s))

    def mixed(t0):
        t = frame_ids(t0, CHUNK, width)
        v = tok_ref[0, pl.ds(t0, CHUNK), :].astype(F32)
        low = silu(v * pick(tab_ref, 0, t, row) + pick(tab_ref, SEGS, t, row))
        buf_ref[pl.ds(PAD + t0, CHUNK), :] = jnp.where(t < row.ends[2], low, 0.0)

    row.chunks(uniform, mixed)
    for left in (True, False):
        t, valid = halo_tile(row, frames, width, left)
        low = silu(edge_tile(rx_ref, row, r, t, 0, left) * tab_ref[6:7, :] + tab_ref[7:8, :])
        at = 0 if left else PAD + frames
        buf_ref[at : at + PAD, :] = jnp.where(valid, low, 0.0)
    stack_taps(buf_ref, xs_ref, row, frames, True, True, low_ref)
    hid_ref[0] = jnp.dot(xs_ref[...], w_ref[...], preferred_element_type=F32)

    acc_ref[...] = jnp.zeros_like(acc_ref)

    def uniform_sums(t0, s):
        v = hid_ref[0, pl.ds(PAD + t0, CHUNK), :]
        add_sums(acc_ref, s, v, v * v)

    def mixed_sums(t0):
        v = hid_ref[0, pl.ds(PAD + t0, CHUNK), :]
        add_masked_sums(acc_ref, frame_ids(t0, CHUNK, width), row, v, v * v)

    row.chunks(uniform_sums, mixed_sums)
    put_sums(acc_ref, st2_ref, msg_ref, row, r)


def branch_grad_kernel(len_ref, og_ref, rx_ref, w_ref, gs_ref, q_ref, bias_ref, buf_ref, xs_ref):
    r = pl.program_id(0)
    frames, width = og_ref.shape[1:]
    row = Row(len_ref, r, frames)

    @pl.when(r == 0)
    def _():
        bias_ref[...] = jnp.zeros_like(bias_ref)

    def put(t0, g):
        g = g.astype(BF16).astype(F32)
        buf_ref[pl.ds(PAD + t0, CHUNK), :] = g
        bias_ref[...] += fold(g)

    def uniform(t0, s):
        put(t0, og_ref[0, pl.ds(t0, CHUNK), :].astype(F32) * ROOT_HALF)

    def mixed(t0):
        t = frame_ids(t0, CHUNK, width)
        g = og_ref[0, pl.ds(t0, CHUNK), :].astype(F32) * ROOT_HALF
        put(t0, jnp.where(t < row.ends[2], g, 0.0))

    row.chunks(uniform, mixed)
    for left in (True, False):
        t, valid = halo_tile(row, frames, width, left)
        at = 0 if left else PAD + frames
        g = edge_tile(rx_ref, row, r, t, 2, left) * ROOT_HALF
        buf_ref[at : at + PAD, :] = jnp.where(valid, g, 0.0)
    stack_taps(buf_ref, xs_ref, row, frames, False, True)
    gs_ref[0] = xs_ref[PAD : PAD + frames, :]
    q_ref[0] = times_transposed(xs_ref[...], w_ref, width).astype(BF16)


def second_norm_kernel(len_ref, hid_ref, q_ref, st_ref, rx_ref, aff_ref, low_ref, da_ref, gst_ref, msg_ref,
                       tab_ref, acc_ref):
    r = pl.program_id(0)
    padded, width = hid_ref.shape[1:]
    frames = padded - 2 * PAD
    row = Row(len_ref, r, frames)
    put_forward(row, r, st_ref, rx_ref, aff_ref, tab_ref)
    acc_ref[...] = jnp.zeros_like(acc_ref)

    def uniform(t0, s):
        rows = pl.ds(PAD + t0, CHUNK)
        v = hid_ref[0, rows, :]
        low, slope = silu_and_slope(v * row_of(tab_ref, 0, s) + row_of(tab_ref, SEGS, s))
        da = slope * q_ref[0, rows, :].astype(F32)
        low_ref[0, rows, :] = low.astype(BF16)
        da_ref[0, rows, :] = da.astype(BF16)
        add_sums(acc_ref, s, da, da * v)

    def mixed(t0):
        rows = pl.ds(PAD + t0, CHUNK)
        t = frame_ids(t0, CHUNK, width)
        live = t < row.ends[2]
        v = hid_ref[0, rows, :]
        low, slope = silu_and_slope(v * pick(tab_ref, 0, t, row) + pick(tab_ref, SEGS, t, row))
        da = slope * q_ref[0, rows, :].astype(F32)
        low_ref[0, rows, :] = jnp.where(live, low, 0.0).astype(BF16)
        da_ref[0, rows, :] = jnp.where(live, da, 0.0).astype(BF16)
        add_masked_sums(acc_ref, t, row, da, da * v)

    row.chunks(uniform, mixed)
    for left in (True, False):
        t, valid = halo_tile(row, frames, width, left)
        at = 0 if left else PAD + frames
        v = hid_ref[0, at : at + PAD, :]
        low, slope = silu_and_slope(v * tab_ref[6:7, :] + tab_ref[7:8, :])
        da = slope * q_ref[0, at : at + PAD, :].astype(F32)
        low_ref[0, at : at + PAD, :] = jnp.where(valid, low, 0.0).astype(BF16)
        da_ref[0, at : at + PAD, :] = jnp.where(valid, da, 0.0).astype(BF16)
    put_sums(acc_ref, gst_ref, msg_ref, row, r)


def block_out_kernel(len_ref, low_ref, tok_ref, w_ref, bias_ref, out_ref, buf_ref, xs_ref):
    r = pl.program_id(0)
    frames, width = tok_ref.shape[1:]
    row = Row(len_ref, r, frames)
    buf_ref[...] = low_ref[0].astype(F32)
    stack_taps(buf_ref, xs_ref, row, frames, True, False)
    branch = jnp.dot(xs_ref[...], w_ref[...], preferred_element_type=F32) + bias_ref[...].astype(F32)
    live = frame_ids(0, frames, width) < row.ends[2]
    out = (tok_ref[0].astype(F32) + jnp.where(live, branch, 0.0)) * ROOT_HALF
    out_ref[0] = out.astype(BF16)


def add_kernel_grad(r, u, gs, acc_ref, send_ref, keep_ref):
    width = u.shape[1]
    part = lax.dot_general(u, gs, (((0,), (0,)), ((), ())), preferred_element_type=F32)

    @pl.when(r == 0)
    def _():
        acc_ref[...] = part

    @pl.when(r > 0)
    def _():
        acc_ref[...] += part

    @pl.when(r == pl.num_programs(0) - 1)
    def _():
        core, half = lax.axis_index("core"), width // 2
        for ref, which in ((send_ref, 1 - core), (keep_ref, core)):
            rows = pl.ds(pl.multiple_of(which * half, half), half)
            for k in range(3):
                ref[k * half : (k + 1) * half, :] = acc_ref[rows, k * width : (k + 1) * width].astype(BF16)


def second_kernel_grad_kernel(low_ref, gs_ref, send_ref, keep_ref, acc_ref):
    frames = gs_ref.shape[1]
    add_kernel_grad(pl.program_id(0), low_ref[0, PAD : PAD + frames, :], gs_ref[0], acc_ref, send_ref, keep_ref)


def hidden_grad_kernel(len_ref, low_ref, da_ref, hid_ref, st_ref, rx_ref, gst_ref, grx_ref, aff_ref,
                       gs_ref, send_ref, keep_ref, part_ref, buf_ref, tab_ref, acc_ref):
    r = pl.program_id(0)
    frames, width = low_ref.shape[1:]
    row = Row(len_ref, r, frames)

    @pl.when(r == 0)
    def _():
        part_ref[...] = jnp.zeros_like(part_ref)

    put_affine_grads(row, r, st_ref, rx_ref, gst_ref, aff_ref, part_ref, 0)
    put_backward(row, r, st_ref, rx_ref, gst_ref, grx_ref, aff_ref, tab_ref)

    def uniform(t0, s):
        rows = pl.ds(PAD + t0, CHUNK)
        buf_ref[rows, :] = (
            da_ref[0, rows, :].astype(F32) * row_of(tab_ref, 0, s)
            + hid_ref[0, rows, :] * row_of(tab_ref, SEGS, s)
            + row_of(tab_ref, 2 * SEGS, s)
        )

    def mixed(t0):
        rows = pl.ds(PAD + t0, CHUNK)
        t = frame_ids(t0, CHUNK, width)
        grad = (
            da_ref[0, rows, :].astype(F32) * pick(tab_ref, 0, t, row)
            + hid_ref[0, rows, :] * pick(tab_ref, SEGS, t, row)
            + pick(tab_ref, 2 * SEGS, t, row)
        )
        buf_ref[rows, :] = jnp.where(t < row.ends[2], grad, 0.0)

    row.chunks(uniform, mixed)
    for left in (True, False):
        t, valid = halo_tile(row, frames, width, left)
        at = 0 if left else PAD + frames
        grad = (
            da_ref[0, at : at + PAD, :].astype(F32) * tab_ref[9:10, :]
            + hid_ref[0, at : at + PAD, :] * tab_ref[10:11, :]
            + tab_ref[11:12, :]
        )
        buf_ref[at : at + PAD, :] = jnp.where(valid, grad, 0.0)
    stack_taps(buf_ref, gs_ref.at[0], row, frames, False, False)
    add_kernel_grad(r, low_ref[0], gs_ref[0], acc_ref, send_ref, keep_ref)


def first_norm_grad_kernel(len_ref, gs_ref, w_ref, tok_ref, st_ref, rx_ref, aff_ref, part2_ref, bias_ref,
                           da_ref, gst_ref, msg_ref, part_ref, q_ref, tab_ref, acc_ref, sums_ref):
    r = pl.program_id(0)
    frames, width = tok_ref.shape[1:]
    row = Row(len_ref, r, frames)

    @pl.when(r == 0)
    def _():
        sums_ref[:, : 2 * width] = jnp.zeros((sums_ref.shape[0], 2 * width), F32)
        sums_ref[:, 2 * width :] = part2_ref[...]
        sums_ref[SEGS : SEGS + 1, :width] = jnp.sum(bias_ref[...], axis=0, keepdims=True)

    put_forward(row, r, st_ref, rx_ref, aff_ref, tab_ref)
    q_ref[...] = times_transposed(gs_ref[0], w_ref, width)
    acc_ref[...] = jnp.zeros_like(acc_ref)

    def uniform(t0, s):
        rows = pl.ds(t0, CHUNK)
        v = tok_ref[0, rows, :].astype(F32)
        _, slope = silu_and_slope(v * row_of(tab_ref, 0, s) + row_of(tab_ref, SEGS, s))
        da = slope * q_ref[rows, :]
        da_ref[0, rows, :] = da.astype(BF16)
        add_sums(acc_ref, s, da, da * v)

    def mixed(t0):
        rows = pl.ds(t0, CHUNK)
        t = frame_ids(t0, CHUNK, width)
        v = tok_ref[0, rows, :].astype(F32)
        _, slope = silu_and_slope(v * pick(tab_ref, 0, t, row) + pick(tab_ref, SEGS, t, row))
        da = slope * q_ref[rows, :]
        da_ref[0, rows, :] = jnp.where(t < row.ends[2], da, 0.0).astype(BF16)
        add_masked_sums(acc_ref, t, row, da, da * v)

    row.chunks(uniform, mixed)
    put_sums(acc_ref, gst_ref, msg_ref, row, r)
    put_affine_grads(row, r, st_ref, rx_ref, gst_ref, aff_ref, sums_ref, 0)

    @pl.when(r == pl.num_programs(0) - 1)
    def _():
        for d in range(part_ref.shape[0]):
            part_ref[d] = sums_ref[...].astype(BF16)


def input_grad_kernel(len_ref, og_ref, da_ref, tok_ref, st_ref, rx_ref, gst_ref, grx_ref, aff_ref, out_ref, tab_ref):
    r = pl.program_id(0)
    frames, width = tok_ref.shape[1:]
    row = Row(len_ref, r, frames)
    put_backward(row, r, st_ref, rx_ref, gst_ref, grx_ref, aff_ref, tab_ref)

    def uniform(t0, s):
        rows = pl.ds(t0, CHUNK)
        out = (
            og_ref[0, rows, :].astype(F32) * ROOT_HALF
            + da_ref[0, rows, :].astype(F32) * row_of(tab_ref, 0, s)
            + tok_ref[0, rows, :].astype(F32) * row_of(tab_ref, SEGS, s)
            + row_of(tab_ref, 2 * SEGS, s)
        )
        out_ref[0, rows, :] = out.astype(BF16)

    def mixed(t0):
        rows = pl.ds(t0, CHUNK)
        t = frame_ids(t0, CHUNK, width)
        grad = (
            da_ref[0, rows, :].astype(F32) * pick(tab_ref, 0, t, row)
            + tok_ref[0, rows, :].astype(F32) * pick(tab_ref, SEGS, t, row)
            + pick(tab_ref, 2 * SEGS, t, row)
        )
        out = og_ref[0, rows, :].astype(F32) * ROOT_HALF + jnp.where(t < row.ends[2], grad, 0.0)
        out_ref[0, rows, :] = out.astype(BF16)

    row.chunks(uniform, mixed)


def per_row(*shape):
    return pl.BlockSpec((1, *shape), lambda r, *_: (r,) + (0,) * len(shape))


def sums_block(width):
    return pl.BlockSpec((8, width), lambda r, *_: (r, 0))


def whole(*shape):
    return pl.BlockSpec(shape, lambda r, *_: (0,) * len(shape))


def call(kernel, rows, lengths, arrays, in_specs, outs, out_specs, scratch, flops=0, nbytes=8 << 20):
    prefetch = () if lengths is None else (lengths,)
    return pl.pallas_call(
        kernel,
        out_shape=[jax.ShapeDtypeStruct(s, d) for s, d in outs],
        grid_spec=pltpu.PrefetchScalarGridSpec(
            num_scalar_prefetch=len(prefetch),
            grid=(rows,),
            in_specs=in_specs,
            out_specs=out_specs,
            scratch_shapes=[pltpu.VMEM(s, d) for s, d in scratch],
        ),
        compiler_params=pltpu.CompilerParams(
            dimension_semantics=("arbitrary",), vmem_limit_bytes=VMEM_MIB << 20
        ),
        cost_estimate=pl.CostEstimate(flops=flops, bytes_accessed=nbytes, transcendentals=0),
    )(*prefetch, *arrays)


def exchange(message):
    return lax.all_to_all(message, "tm", 0, 0)


def spread(block, axis):
    count = lax.axis_size(axis)
    return lax.all_to_all(jnp.broadcast_to(block[None], (count, *block.shape)), axis, 0, 0)


def scatter_sum(blocks, axis):
    count = lax.axis_size(axis)
    got = lax.all_to_all(blocks.reshape(count, -1, blocks.shape[1]), axis, 0, 0)
    return jnp.sum(got.astype(F32), axis=0).astype(BF16)


def swap_cores(block):
    return lax.ppermute(block, "core", [(0, 1), (1, 0)])


def total(send, keep):
    width = send.shape[1]
    mine = (swap_cores(send).astype(F32) + keep.astype(F32)).astype(BF16)
    part = scatter_sum(scatter_sum(mine, "chip"), "tm")
    mine = spread(spread(part, "tm").reshape(-1, width), "chip").reshape(-1, width)
    other = swap_cores(mine)
    first = lax.axis_index("core") == 0
    low = jnp.where(first, mine, other).reshape(3, -1, width)
    high = jnp.where(first, other, mine).reshape(3, -1, width)
    return jnp.concatenate([low, high], axis=1).astype(F32)


def per_device(tokens, lengths, style, fc1_weight, fc1_bias, conv1_kernel, fc2_weight, fc2_bias, conv2_kernel,
               conv2_bias, out_grad):
    rows, frames, width = tokens.shape
    count = lax.axis_size("tm")
    padded = frames + 2 * PAD
    style_rows = style.reshape(rows * SEGS, -1)
    affine1 = jnp.dot(style_rows, fc1_weight, preferred_element_type=F32) + fc1_bias.astype(F32)
    affine2 = jnp.dot(style_rows, fc2_weight, preferred_element_type=F32) + fc2_bias.astype(F32)
    kernel1 = conv1_kernel.reshape(3 * width, width)
    kernel2 = conv2_kernel.reshape(3 * width, width)

    own, wide = per_row(frames, width), per_row(padded, width)
    taps = per_row(frames, 3 * width)
    head = pl.BlockSpec((1, PAD, width), lambda r, *_: (r, 0, 0))
    tail = pl.BlockSpec((1, PAD, width), lambda r, *_: (r, frames // PAD - 1, 0))
    sums, affine, kernel = sums_block(width), whole(rows * SEGS, 2 * width), whole(3 * width, width)
    msg, msg_edges = whole(count, 2 * rows, width), whole(count, EDGE, width)
    halves = whole(3 * width // 2, width)
    sums_shape = ((8 * rows, width), F32)
    msg_shape = ((count, 2 * rows, width), F32)
    half_shape = ((3 * width // 2, width), BF16)
    acc, tab = ((8, 8, width), F32), ((16, width), F32)
    buf, xs_wide, xs_own = ((padded, width), F32), ((padded, 3 * width), BF16), ((frames, 3 * width), BF16)
    flops = 2 * rows * frames * 3 * width * width

    st1, msg1 = call(
        token_sums_kernel, rows, lengths, (tokens, tokens, tokens, out_grad, out_grad),
        [own, head, tail, head, tail], [sums_shape, ((count, EDGE, width), F32)], [sums, msg_edges], [acc],
    )
    rx1 = exchange(msg1)
    low1, hidden, st2, msg2 = call(
        first_half_kernel, rows, lengths, (tokens, st1, rx1, affine1, kernel1),
        [own, sums, msg_edges, affine, kernel],
        [((rows, frames, width), BF16), ((rows, padded, width), F32), sums_shape, msg_shape],
        [own, wide, sums, msg], [buf, xs_wide, tab, acc], flops,
    )
    rx2 = exchange(msg2)
    gs2, grad_low2, bias_part = call(
        branch_grad_kernel, rows, lengths, (out_grad, rx1, kernel2), [own, msg_edges, kernel],
        [((rows, frames, 3 * width), BF16), ((rows, padded, width), BF16), ((8, width), F32)],
        [taps, wide, whole(8, width)], [buf, xs_wide], flops,
    )
    low2, da2, gst2, msg3 = call(
        second_norm_kernel, rows, lengths, (hidden, grad_low2, st2, rx2, affine2), [wide, wide, sums, msg, affine],
        [((rows, padded, width), BF16), ((rows, padded, width), BF16), sums_shape, msg_shape],
        [wide, wide, sums, msg], [tab, acc],
    )
    rx3 = exchange(msg3)
    send2, keep2 = call(
        second_kernel_grad_kernel, rows, None, (low2, gs2), [wide, taps], [half_shape, half_shape], [halves, halves],
        [((width, 3 * width), F32)], flops,
    )
    gs1, send1, keep1, part2 = call(
        hidden_grad_kernel, rows, lengths, (low1, da2, hidden, st2, rx2, gst2, rx3, affine2),
        [own, wide, wide, sums, msg, sums, msg, affine],
        [((rows, frames, 3 * width), BF16), half_shape, half_shape, ((4 * rows, 2 * width), F32)],
        [taps, halves, halves, whole(4 * rows, 2 * width)], [buf, tab, ((width, 3 * width), F32)], flops,
    )
    da1, gst1, msg4, parts = call(
        first_norm_grad_kernel, rows, lengths, (gs1, kernel1, tokens, st1, rx1, affine1, part2, bias_part),
        [taps, kernel, own, sums, msg_edges, affine, whole(4 * rows, 2 * width), whole(8, width)],
        [((rows, frames, width), BF16), sums_shape, msg_shape, ((count, 4 * rows, 4 * width), BF16)],
        [own, sums, msg, whole(count, 4 * rows, 4 * width)],
        [((frames, width), F32), tab, acc, ((4 * rows, 4 * width), F32)], flops,
    )
    rx4 = exchange(msg4)
    (block_out,) = call(
        block_out_kernel, rows, lengths, (low2, tokens, kernel2, conv2_bias.reshape(1, width)),
        [wide, own, kernel, whole(1, width)], [((rows, frames, width), BF16)], [own], [buf, xs_own], flops,
    )
    (input_grad,) = call(
        input_grad_kernel, rows, lengths, (out_grad, da1, tokens, st1, rx1, gst1, rx4, affine1),
        [own, own, own, sums, msg_edges, sums, msg, affine], [((rows, frames, width), BF16)], [own], [tab],
    )

    conv2_sum, conv1_sum = total(send2, keep2), total(send1, keep1)

    affine_grads = jnp.sum(exchange(parts).astype(F32), axis=0).astype(BF16)
    mine = affine_grads.reshape(rows, 4, 4 * width)[:, :SEGS].reshape(rows * SEGS, 4 * width)
    style_grad = lax.dot_general(
        mine[:, : 2 * width], fc1_weight, (((1,), (1,)), ((), ())), preferred_element_type=F32
    ) + lax.dot_general(mine[:, 2 * width :], fc2_weight, (((1,), (1,)), ((), ())), preferred_element_type=F32)
    style_pad = jnp.pad(style, ((0, 0), (0, 1), (0, 0))).reshape(rows * 4, -1)
    gathered = spread(jnp.concatenate([affine_grads, style_pad], axis=1), ("chip", "core"))
    gathered = gathered.reshape(-1, gathered.shape[-1])
    grads, styles = gathered[:, : 4 * width], gathered[:, 4 * width :]
    fc_grads = lax.dot_general(styles, grads, (((0,), (0,)), ((), ())), preferred_element_type=F32)
    by_segment = jnp.sum(grads.reshape(-1, 4, 4 * width).astype(F32), axis=0)
    fc_bias_grads = jnp.sum(by_segment[:SEGS], axis=0)
    return (
        block_out,
        input_grad,
        style_grad.reshape(style.shape),
        fc_grads[:, : 2 * width],
        fc_bias_grads[: 2 * width],
        conv1_sum,
        fc_grads[:, 2 * width :],
        fc_bias_grads[2 * width :],
        conv2_sum,
        by_segment[SEGS, :width],
    )


def solution(mesh):
    chips = mesh.shape["dp"] // 2
    mesh = Mesh(mesh.devices.reshape(chips, 2, mesh.shape["tm"]), ("chip", "core", "tm"))
    dp = ("chip", "core")
    return jax.shard_map(
        per_device,
        mesh=mesh,
        in_specs=(
            P(dp, "tm", None),
            P(dp, None),
            P(dp, None, None),
            P(),
            P(),
            P(),
            P(),
            P(),
            P(),
            P(),
            P(dp, "tm", None),
        ),
        out_specs=(
            P(dp, "tm", None),
            P(dp, "tm", None),
            P(dp, None, None),
            P(),
            P(),
            P(),
            P(),
            P(),
            P(),
            P(),
        ),
        check_vma=False,
    )
```

```python
import functools

import jax
import jax.numpy as jnp
from jax import lax
from jax.experimental import pallas as pl
from jax.experimental.pallas import tpu as pltpu
from jax.sharding import Mesh, PartitionSpec as P

EPSILON = 1e-05
ROOT_HALF = 0.7071067811865476
SEGS = 3
PAD = 16
CHUNK = 64
EDGE = 8 + 16
F32 = jnp.float32
BF16 = jnp.bfloat16
SMALL, LARGE = 20, 30


class Row:
    def __init__(self, len_ref, r, frames):
        self.frames = frames
        self.z = lax.axis_index("tm")
        self.counts = [len_ref[r, s] for s in range(SEGS)]
        l0, l1, l2 = self.counts
        start = -self.z * frames
        e0 = start + l0
        e1 = e0 + l1
        e2 = e1 + l2
        self.begins = [start, e0, e1]
        self.ends = [e0, e1, e2]
        self.long_at = jnp.where(l0 >= jnp.maximum(l1, l2), 0, jnp.where(l1 >= l2, 1, 2))
        self.long_begin = self.of_long(self.begins)
        self.long_end = self.of_long(self.ends)

    def of_long(self, values):
        return jnp.where(
            self.long_at == 0, values[0], jnp.where(self.long_at == 1, values[1], values[2])
        )

    def segment(self, t):
        return sum((t >= e).astype(jnp.int32) for e in self.ends)

    def chunks(self, uniform_fn, mixed_fn):
        def body(i, carry):
            t0 = pl.multiple_of(i * CHUNK, CHUNK)
            first, last = self.segment(t0), self.segment(t0 + CHUNK - 1)
            uniform = jnp.logical_and(first == last, first < SEGS)

            @pl.when(uniform)
            def _():
                uniform_fn(t0, first)

            @pl.when(jnp.logical_not(uniform))
            def _():
                mixed_fn(t0)

            return carry

        lax.fori_loop(0, self.frames // CHUNK, body, 0)


def frame_ids(t0, rows, width):
    return t0 + lax.broadcasted_iota(jnp.int32, (rows, width), 0)


def pick(tab_ref, base, t, row):
    value = jnp.where(t >= row.ends[0], tab_ref[base + 1 : base + 2, :], tab_ref[base : base + 1, :])
    return jnp.where(t >= row.ends[1], tab_ref[base + 2 : base + 3, :], value)


def row_of(tab_ref, base, s):
    return tab_ref[pl.ds(base + s, 1), :]


def fold(x):
    return jnp.sum(x.reshape(x.shape[0] // 8, 8, x.shape[1]), axis=0)


def add_sums(acc_ref, s, first, second):
    acc_ref[s] += fold(first)
    acc_ref[4 + s] += fold(second)


def add_masked_sums(acc_ref, t, row, first, second):
    for s in range(SEGS):
        inside = jnp.logical_and(t >= row.begins[s], t < row.ends[s])
        add_sums(acc_ref, s, jnp.where(inside, first, 0.0), jnp.where(inside, second, 0.0))


def put_sums(acc_ref, st_ref, msg_refs, row, r):
    for s in range(SEGS):
        for k in range(2):
            st_ref[r, pl.ds(SEGS * k + s, 1), :] = jnp.sum(acc_ref[4 * k + s], axis=0, keepdims=True)
    for k in range(2):
        value = jnp.sum(acc_ref[4 * k + row.long_at], axis=0, keepdims=True)
        for ref in msg_refs:
            ref[pl.ds(2 * r + k, 1), :] = value


def sums_of(row, r, st_ref, rx_refs, s):
    out = []
    for k in range(2):
        total = sum(ref[pl.ds(2 * r + k, 1), :] for ref in rx_refs)
        local = st_ref[r, SEGS * k + s : SEGS * k + s + 1, :]
        out.append(jnp.where(row.long_at == s, total, local))
    return out


def norm_of(row, r, st_ref, rx_ref, aff_ref, s):
    width = st_ref.shape[2]
    first, second = sums_of(row, r, st_ref, rx_ref, s)
    count = jnp.full((1, width), row.counts[s].astype(F32))
    mean = first / count
    rstd = lax.rsqrt(second / count - mean * mean + EPSILON)
    affine = aff_ref[r, s : s + 1, :]
    return mean, rstd, 1.0 + affine[:, :width], affine[:, width:], count


def put_forward(row, r, st_ref, rx_ref, aff_ref, tab_ref):
    scales, shifts = [], []
    for s in range(SEGS):
        mean, rstd, gain, beta, _ = norm_of(row, r, st_ref, rx_ref, aff_ref, s)
        scales.append(gain * rstd)
        shifts.append(beta - mean * scales[-1])
        tab_ref[s : s + 1, :] = scales[s]
        tab_ref[SEGS + s : SEGS + s + 1, :] = shifts[s]
    tab_ref[6:7, :] = row.of_long(scales)
    tab_ref[7:8, :] = row.of_long(shifts)


def put_backward(row, r, st_ref, rx_ref, gst_ref, grx_ref, aff_ref, tab_ref):
    parts = [[], [], []]
    for s in range(SEGS):
        mean, rstd, gain, _, count = norm_of(row, r, st_ref, rx_ref, aff_ref, s)
        shift, scale = sums_of(row, r, gst_ref, grx_ref, s)
        scale = rstd * (scale - mean * shift)
        mean_g = gain * shift / count
        slope = rstd * rstd * (gain * scale / count)
        parts[0].append(gain * rstd)
        parts[1].append(-slope)
        parts[2].append(slope * mean - rstd * mean_g)
    for k in range(3):
        for s in range(SEGS):
            tab_ref[SEGS * k + s : SEGS * k + s + 1, :] = parts[k][s]
        tab_ref[9 + k : 10 + k, :] = row.of_long(parts[k])


def put_affine_grads(row, r, st_ref, rx_ref, gst_ref, aff_ref, out_ref, at):
    width = st_ref.shape[2]
    for s in range(SEGS):
        mean, rstd, _, _, _ = norm_of(row, r, st_ref, rx_ref, aff_ref, s)
        shift = gst_ref[r, s : s + 1, :]
        scale = rstd * (gst_ref[r, SEGS + s : SEGS + s + 1, :] - mean * shift)
        out_ref[pl.ds(4 * r + s, 1), at : at + width] = scale
        out_ref[pl.ds(4 * r + s, 1), at + width : at + 2 * width] = shift


def silu(a):
    half = 0.5 * a
    return half + half * jnp.tanh(half)


def silu_and_slope(a):
    gate = 0.5 + 0.5 * jnp.tanh(0.5 * a)
    low = a * gate
    return low, gate + low * (1.0 - gate)


def halo_tile(row, frames, width, left):
    t = frame_ids(-PAD if left else frames, PAD, width)
    near = jnp.logical_and(t >= -2, t < frames + 2)
    inside = jnp.logical_and(t >= row.long_begin, t < row.long_end)
    return t, jnp.logical_and(near, inside)


def edge_tile(rx_refs, row, r, t, at, left):
    last = len(rx_refs) - 1
    neighbour = jnp.maximum(row.z - 1, 0) if left else jnp.minimum(row.z + 1, last)
    edges = []
    for i in range(2):
        value, k = rx_refs[1][pl.ds(8 + 4 * r + at + i, 1), :], 3
        while k <= last:
            value = jnp.where((row.z ^ neighbour) == k, rx_refs[k][pl.ds(8 + 4 * r + at + i, 1), :], value)
            k = 2 * k + 1
        edges.append(value)
    second = -1 if left else row.frames + 1
    return jnp.where(t == second, edges[1], edges[0])


def stack_taps(buf_ref, xs_ref, row, frames, forward, halo, low_ref=None, r=None):
    width = buf_ref.shape[1]
    before_at, after_at = (0, 2 * width) if forward else (2 * width, 0)
    base = PAD if halo else 0
    for i in range(frames // CHUNK):
        o, d = PAD + i * CHUNK, base + i * CHUNK
        centre = buf_ref[o : o + CHUNK, :].astype(BF16)
        xs_ref[d : d + CHUNK, width : 2 * width] = centre
        xs_ref[d : d + CHUNK, before_at : before_at + width] = buf_ref[o - 1 : o - 1 + CHUNK, :].astype(BF16)
        xs_ref[d : d + CHUNK, after_at : after_at + width] = buf_ref[o + 1 : o + 1 + CHUNK, :].astype(BF16)
        if low_ref is not None:
            low_ref[r, i * CHUNK : (i + 1) * CHUNK, :] = centre
    if halo:
        end = PAD + frames
        left, right = buf_ref[0:PAD, :], buf_ref[end : end + PAD, :]
        xs_ref[0:PAD, width : 2 * width] = left.astype(BF16)
        xs_ref[end : end + PAD, width : 2 * width] = right.astype(BF16)
        xs_ref[0:PAD, before_at : before_at + width] = pltpu.roll(left, 1, 0).astype(BF16)
        xs_ref[end : end + PAD, before_at : before_at + width] = buf_ref[end - 1 : end - 1 + PAD, :].astype(BF16)
        xs_ref[0:PAD, after_at : after_at + width] = buf_ref[1 : 1 + PAD, :].astype(BF16)
        xs_ref[end : end + PAD, after_at : after_at + width] = pltpu.roll(right, PAD - 1, 0).astype(BF16)
    for end in row.ends[:2]:
        for at, t in ((before_at, end), (after_at, end - 1)):

            @pl.when(jnp.logical_and(t >= 0, t < frames))
            def _(at=at, t=t):
                tile = pl.multiple_of((t // PAD) * PAD, PAD)
                rows = pl.ds(base + tile, PAD)
                value = xs_ref[rows, at : at + width].astype(F32)
                keep = frame_ids(tile, PAD, width) != t
                xs_ref[rows, at : at + width] = jnp.where(keep, value, 0.0).astype(BF16)


def times_transposed(xs, w_ref, width):
    out = None
    for k in range(3):
        part = lax.dot_general(
            xs[:, k * width : (k + 1) * width],
            w_ref[k * width : (k + 1) * width, :],
            (((1,), (1,)), ((), ())),
            preferred_element_type=F32,
        )
        out = part if out is None else out + part
    return out


def for_rows(len_ref, rows, frames, body):
    def step(r, carry):
        body(r, Row(len_ref, r, frames))
        return carry

    lax.fori_loop(0, rows, step, 0)


def token_sums_kernel(len_ref, tok_hbm, og_hbm, w_hbm, tok_ref, w_ref, st_ref, msg_refs, head_ref, tail_ref, acc_ref,
                      sems, row_sems):
    rows, frames, width = tok_ref.shape

    def row_copy(r):
        return pltpu.make_async_copy(tok_hbm.at[r], tok_ref.at[r], row_sems.at[r])

    for r in range(rows):
        row_copy(r).start()
    edges = (
        pltpu.make_async_copy(og_hbm.at[:, pl.ds(0, PAD), :], head_ref, sems.at[0]),
        pltpu.make_async_copy(og_hbm.at[:, pl.ds(frames - PAD, PAD), :], tail_ref, sems.at[1]),
    )
    for copy in edges:
        copy.start()
    kernel_copy = pltpu.make_async_copy(w_hbm, w_ref, sems.at[2])
    kernel_copy.start()
    for copy in edges:
        copy.wait()

    def body(r, row):
        row_copy(r).wait()
        acc_ref[...] = jnp.zeros_like(acc_ref)

        def uniform(t0, s):
            v = tok_ref[r, pl.ds(t0, CHUNK), :].astype(F32)
            add_sums(acc_ref, s, v, v * v)

        def mixed(t0):
            v = tok_ref[r, pl.ds(t0, CHUNK), :].astype(F32)
            add_masked_sums(acc_ref, frame_ids(t0, CHUNK, width), row, v, v * v)

        row.chunks(uniform, mixed)
        put_sums(acc_ref, st_ref, msg_refs, row, r)
        for j, (head, tail) in enumerate(
            ((tok_ref[r, 0:PAD, :], tok_ref[r, frames - PAD : frames, :]), (head_ref[r], tail_ref[r]))
        ):
            first, last = head.astype(F32), tail.astype(F32)
            for i in range(2):
                to_left, to_right = first[i : i + 1, :], last[PAD - 2 + i : PAD - 1 + i, :]
                for k, ref in enumerate(msg_refs):
                    value = jnp.where(row.z < row.z ^ k, to_right, to_left)
                    ref[pl.ds(8 + 4 * r + 2 * j + i, 1), :] = value

    for_rows(len_ref, rows, frames, body)
    kernel_copy.wait()


def first_half_kernel(len_ref, tok_ref, st_ref, rx_ref, aff_ref, w_ref, og_hbm, w2_hbm, low_hbm, hid_hbm,
                      hid_ref, st2_ref, msg_ref, og_ref, w2_ref, low_ref, buf_ref, xs_ref, tab_ref, acc_ref,
                      sems, row_sems):
    rows, frames, width = tok_ref.shape

    def row_copies(r):
        return (
            pltpu.make_async_copy(low_ref.at[r], low_hbm.at[r], row_sems.at[r]),
            pltpu.make_async_copy(hid_ref.at[r], hid_hbm.at[r], row_sems.at[rows + r]),
        )

    copies = (
        pltpu.make_async_copy(og_hbm, og_ref, sems.at[0]),
        pltpu.make_async_copy(w2_hbm, w2_ref, sems.at[1]),
    )
    for copy in copies:
        copy.start()

    def body(r, row):
        put_forward(row, r, st_ref, rx_ref, aff_ref, tab_ref)

        def uniform(t0, s):
            v = tok_ref[r, pl.ds(t0, CHUNK), :].astype(F32)
            buf_ref[pl.ds(PAD + t0, CHUNK), :] = silu(v * row_of(tab_ref, 0, s) + row_of(tab_ref, SEGS, s))

        def mixed(t0):
            t = frame_ids(t0, CHUNK, width)
            v = tok_ref[r, pl.ds(t0, CHUNK), :].astype(F32)
            low = silu(v * pick(tab_ref, 0, t, row) + pick(tab_ref, SEGS, t, row))
            buf_ref[pl.ds(PAD + t0, CHUNK), :] = jnp.where(t < row.ends[2], low, 0.0)

        row.chunks(uniform, mixed)
        for left in (True, False):
            t, valid = halo_tile(row, frames, width, left)
            low = silu(edge_tile(rx_ref, row, r, t, 0, left) * tab_ref[6:7, :] + tab_ref[7:8, :])
            at = 0 if left else PAD + frames
            buf_ref[at : at + PAD, :] = jnp.where(valid, low, 0.0)
        stack_taps(buf_ref, xs_ref, row, frames, True, True, low_ref, r)
        hid_ref[r] = jnp.dot(xs_ref[...], w_ref[...], preferred_element_type=F32)
        for copy in row_copies(r):
            copy.start()

        acc_ref[...] = jnp.zeros_like(acc_ref)

        def uniform_sums(t0, s):
            v = hid_ref[r, pl.ds(PAD + t0, CHUNK), :]
            add_sums(acc_ref, s, v, v * v)

        def mixed_sums(t0):
            v = hid_ref[r, pl.ds(PAD + t0, CHUNK), :]
            add_masked_sums(acc_ref, frame_ids(t0, CHUNK, width), row, v, v * v)

        row.chunks(uniform_sums, mixed_sums)
        put_sums(acc_ref, st2_ref, [msg_ref], row, r)

    for_rows(len_ref, rows, frames, body)
    for r in range(rows):
        copies += row_copies(r)
    for copy in copies:
        copy.wait()


def branch_grad_kernel(len_ref, og_ref, rx_ref, w_ref, gs_ref, q_ref, bias_ref, buf_ref, xs_ref):
    rows, frames, width = og_ref.shape
    bias_ref[...] = jnp.zeros_like(bias_ref)

    def body(r, row):
        def put(t0, g):
            g = g.astype(BF16).astype(F32)
            buf_ref[pl.ds(PAD + t0, CHUNK), :] = g
            bias_ref[...] += fold(g)

        def uniform(t0, s):
            put(t0, og_ref[r, pl.ds(t0, CHUNK), :].astype(F32) * ROOT_HALF)

        def mixed(t0):
            t = frame_ids(t0, CHUNK, width)
            g = og_ref[r, pl.ds(t0, CHUNK), :].astype(F32) * ROOT_HALF
            put(t0, jnp.where(t < row.ends[2], g, 0.0))

        row.chunks(uniform, mixed)
        for left in (True, False):
            t, valid = halo_tile(row, frames, width, left)
            at = 0 if left else PAD + frames
            g = edge_tile(rx_ref, row, r, t, 2, left) * ROOT_HALF
            buf_ref[at : at + PAD, :] = jnp.where(valid, g, 0.0)
        stack_taps(buf_ref, xs_ref, row, frames, False, True)
        gs_ref[r] = xs_ref[PAD : PAD + frames, :]
        q_ref[r] = times_transposed(xs_ref[...], w_ref, width).astype(BF16)

    for_rows(len_ref, rows, frames, body)


def second_norm_kernel(len_ref, hid_ref, q_ref, st_ref, rx_ref, aff_ref, low_ref, low_hbm, da_hbm, gst_ref, msg_ref,
                       da_ref, tab_ref, acc_ref, row_sems):
    rows, padded, width = hid_ref.shape
    frames = padded - 2 * PAD

    def row_copies(r):
        return (
            pltpu.make_async_copy(low_ref.at[r], low_hbm.at[r], row_sems.at[r]),
            pltpu.make_async_copy(da_ref.at[r], da_hbm.at[r], row_sems.at[rows + r]),
        )

    def body(r, row):
        put_forward(row, r, st_ref, rx_ref, aff_ref, tab_ref)
        acc_ref[...] = jnp.zeros_like(acc_ref)

        def uniform(t0, s):
            at = pl.ds(PAD + t0, CHUNK)
            v = hid_ref[r, at, :]
            low, slope = silu_and_slope(v * row_of(tab_ref, 0, s) + row_of(tab_ref, SEGS, s))
            da = slope * q_ref[r, at, :].astype(F32)
            low_ref[r, at, :] = low.astype(BF16)
            da_ref[r, at, :] = da.astype(BF16)
            add_sums(acc_ref, s, da, da * v)

        def mixed(t0):
            at = pl.ds(PAD + t0, CHUNK)
            t = frame_ids(t0, CHUNK, width)
            live = t < row.ends[2]
            v = hid_ref[r, at, :]
            low, slope = silu_and_slope(v * pick(tab_ref, 0, t, row) + pick(tab_ref, SEGS, t, row))
            da = slope * q_ref[r, at, :].astype(F32)
            low_ref[r, at, :] = jnp.where(live, low, 0.0).astype(BF16)
            da_ref[r, at, :] = jnp.where(live, da, 0.0).astype(BF16)
            add_masked_sums(acc_ref, t, row, da, da * v)

        row.chunks(uniform, mixed)
        for left in (True, False):
            t, valid = halo_tile(row, frames, width, left)
            at = 0 if left else PAD + frames
            v = hid_ref[r, at : at + PAD, :]
            low, slope = silu_and_slope(v * tab_ref[6:7, :] + tab_ref[7:8, :])
            da = slope * q_ref[r, at : at + PAD, :].astype(F32)
            low_ref[r, at : at + PAD, :] = jnp.where(valid, low, 0.0).astype(BF16)
            da_ref[r, at : at + PAD, :] = jnp.where(valid, da, 0.0).astype(BF16)
        for copy in row_copies(r):
            copy.start()
        put_sums(acc_ref, gst_ref, [msg_ref], row, r)

    for_rows(len_ref, rows, frames, body)
    for r in range(rows):
        for copy in row_copies(r):
            copy.wait()


class Loads:
    def __init__(self, rows, sems, whole, by_row):
        count = len(whole)
        self.whole = [pltpu.make_async_copy(a, b, sems.at[i]) for i, (a, b) in enumerate(whole)]
        self.row = lambda r: [
            pltpu.make_async_copy(a.at[r], b.at[r], sems.at[count + i * rows + r]) for i, (a, b) in enumerate(by_row)
        ]
        for r in range(rows):
            for copy in self.row(r):
                copy.start()
            if r == 0:
                for copy in self.whole:
                    copy.start()

    def wait(self, r):
        for copy in self.row(r):
            copy.wait()

        @pl.when(r == 0)
        def _():
            for copy in self.whole:
                copy.wait()


def block_out_kernel(len_ref, low_hbm, tok_hbm, w_hbm, bias_ref, out_hbm, low_ref, tok_ref, w_ref, buf_ref, xs_ref,
                     out_ref, sems, row_sems):
    rows, frames, width = tok_ref.shape
    loads = Loads(rows, sems, [(w_hbm, w_ref)], [(low_hbm, low_ref), (tok_hbm, tok_ref)])

    def row_copy(r):
        return pltpu.make_async_copy(out_ref.at[r], out_hbm.at[r], row_sems.at[r])

    def body(r, row):
        loads.wait(r)
        buf_ref[...] = low_ref[r].astype(F32)
        stack_taps(buf_ref, xs_ref, row, frames, True, False)
        branch = jnp.dot(xs_ref[...], w_ref[...], preferred_element_type=F32) + bias_ref[...].astype(F32)
        live = frame_ids(0, frames, width) < row.ends[2]
        out = (tok_ref[r].astype(F32) + jnp.where(live, branch, 0.0)) * ROOT_HALF
        out_ref[r] = out.astype(BF16)
        row_copy(r).start()

    for_rows(len_ref, rows, frames, body)
    for r in range(rows):
        row_copy(r).wait()


def half_of_grad(low_ref, gs_ref, r, half, first_frame):
    frames, width = gs_ref.shape[1], low_ref.shape[2] // 2
    u = low_ref[r, first_frame : first_frame + frames, pl.ds(pl.multiple_of(half * width, width), width)]
    return lax.dot_general(u, gs_ref[r], (((0,), (0,)), ((), ())), preferred_element_type=F32)


def put_half(acc_ref, out_ref):
    half, width = acc_ref.shape[0], acc_ref.shape[1] // 3
    for k in range(3):
        out_ref[k * half : (k + 1) * half, :] = acc_ref[:, k * width : (k + 1) * width].astype(BF16)


def kernel_grad_kernel(own, first_frame, low_ref, gs_ref, out_ref, acc_ref):
    core = lax.axis_index("core")
    half = core if own else 1 - core
    acc_ref[...] = half_of_grad(low_ref, gs_ref, 0, half, first_frame)

    def step(r, carry):
        acc_ref[...] += half_of_grad(low_ref, gs_ref, r, half, first_frame)
        return carry

    lax.fori_loop(1, low_ref.shape[0], step, 0)
    put_half(acc_ref, out_ref)


def hidden_grad_kernel(len_ref, low_hbm, da_hbm, hid_hbm, st_ref, rx_ref, gst_ref, grx_ref, aff_ref,
                       gs_hbm, send_ref, keep_ref, part_ref, low_ref, da_ref, hid_ref, gs_ref, buf_ref, tab_ref, acc_ref,
                       sems, row_sems):
    rows, frames, width = low_ref.shape
    loads = Loads(rows, sems, [], [(da_hbm, da_ref), (hid_hbm, hid_ref), (low_hbm, low_ref)])
    part_ref[...] = jnp.zeros_like(part_ref)
    acc_ref[...] = jnp.zeros_like(acc_ref)

    def row_copy(r):
        return pltpu.make_async_copy(gs_ref.at[r], gs_hbm.at[r], row_sems.at[r])

    def body(r, row):
        put_affine_grads(row, r, st_ref, rx_ref, gst_ref, aff_ref, part_ref, 0)
        put_backward(row, r, st_ref, rx_ref, gst_ref, grx_ref, aff_ref, tab_ref)
        loads.wait(r)

        def uniform(t0, s):
            at = pl.ds(PAD + t0, CHUNK)
            buf_ref[at, :] = (
                da_ref[r, at, :].astype(F32) * row_of(tab_ref, 0, s)
                + hid_ref[r, at, :] * row_of(tab_ref, SEGS, s)
                + row_of(tab_ref, 2 * SEGS, s)
            )

        def mixed(t0):
            at = pl.ds(PAD + t0, CHUNK)
            t = frame_ids(t0, CHUNK, width)
            grad = (
                da_ref[r, at, :].astype(F32) * pick(tab_ref, 0, t, row)
                + hid_ref[r, at, :] * pick(tab_ref, SEGS, t, row)
                + pick(tab_ref, 2 * SEGS, t, row)
            )
            buf_ref[at, :] = jnp.where(t < row.ends[2], grad, 0.0)

        row.chunks(uniform, mixed)
        for left in (True, False):
            t, valid = halo_tile(row, frames, width, left)
            at = 0 if left else PAD + frames
            grad = (
                da_ref[r, at : at + PAD, :].astype(F32) * tab_ref[9:10, :]
                + hid_ref[r, at : at + PAD, :] * tab_ref[10:11, :]
                + tab_ref[11:12, :]
            )
            buf_ref[at : at + PAD, :] = jnp.where(valid, grad, 0.0)
        stack_taps(buf_ref, gs_ref.at[r], row, frames, False, False)
        row_copy(r).start()
        acc_ref[...] += lax.dot_general(
            low_ref[r], gs_ref[r], (((0,), (0,)), ((), ())), preferred_element_type=F32
        )

    for_rows(len_ref, rows, frames, body)
    core, half = lax.axis_index("core"), width // 2
    for ref, which in ((send_ref, 1 - core), (keep_ref, core)):
        put_half(acc_ref.at[pl.ds(pl.multiple_of(which * half, half), half), :], ref)
    for r in range(rows):
        row_copy(r).wait()


def first_norm_grad_kernel(len_ref, gs_hbm, w_hbm, tok_hbm, st_ref, rx_ref, aff_ref, part2_ref, bias_ref,
                           da_hbm, gst_ref, msg_ref, out_ref, gs_ref, w_ref, tok_ref, da_ref, q_ref, tab_ref, acc_ref,
                           part_ref, sems, row_sems):
    rows, frames, width = tok_ref.shape
    loads = Loads(rows, sems, [(w_hbm, w_ref)], [(gs_hbm, gs_ref), (tok_hbm, tok_ref)])
    part_ref[:, : 2 * width] = jnp.zeros((part_ref.shape[0], 2 * width), F32)
    part_ref[:, 2 * width :] = part2_ref[...]
    part_ref[SEGS : SEGS + 1, :width] = jnp.sum(bias_ref[...], axis=0, keepdims=True)

    def row_copy(r):
        return pltpu.make_async_copy(da_ref.at[r], da_hbm.at[r], row_sems.at[r])

    def body(r, row):
        put_forward(row, r, st_ref, rx_ref, aff_ref, tab_ref)
        loads.wait(r)
        q_ref[...] = times_transposed(gs_ref[r], w_ref, width)
        acc_ref[...] = jnp.zeros_like(acc_ref)

        def uniform(t0, s):
            at = pl.ds(t0, CHUNK)
            v = tok_ref[r, at, :].astype(F32)
            _, slope = silu_and_slope(v * row_of(tab_ref, 0, s) + row_of(tab_ref, SEGS, s))
            da = slope * q_ref[at, :]
            da_ref[r, at, :] = da.astype(BF16)
            add_sums(acc_ref, s, da, da * v)

        def mixed(t0):
            at = pl.ds(t0, CHUNK)
            t = frame_ids(t0, CHUNK, width)
            v = tok_ref[r, at, :].astype(F32)
            _, slope = silu_and_slope(v * pick(tab_ref, 0, t, row) + pick(tab_ref, SEGS, t, row))
            da = slope * q_ref[at, :]
            da_ref[r, at, :] = jnp.where(t < row.ends[2], da, 0.0).astype(BF16)
            add_masked_sums(acc_ref, t, row, da, da * v)

        row.chunks(uniform, mixed)
        row_copy(r).start()
        put_sums(acc_ref, gst_ref, [msg_ref], row, r)
        put_affine_grads(row, r, st_ref, rx_ref, gst_ref, aff_ref, part_ref, 0)

    for_rows(len_ref, rows, frames, body)
    out_ref[...] = part_ref[...].astype(BF16)
    for r in range(rows):
        row_copy(r).wait()


def input_grad_kernel(len_ref, og_hbm, da_hbm, tok_hbm, st_ref, rx_ref, gst_ref, grx_ref, aff_ref, out_hbm,
                      og_ref, da_ref, tok_ref, tab_ref, out_ref, sems, row_sems):
    rows, frames, width = tok_ref.shape
    loads = Loads(rows, sems, [], [(og_hbm, og_ref), (da_hbm, da_ref), (tok_hbm, tok_ref)])

    def row_copy(r):
        return pltpu.make_async_copy(out_ref.at[r], out_hbm.at[r], row_sems.at[r])

    def body(r, row):
        put_backward(row, r, st_ref, rx_ref, gst_ref, grx_ref, aff_ref, tab_ref)
        loads.wait(r)

        def uniform(t0, s):
            at = pl.ds(t0, CHUNK)
            out = (
                og_ref[r, at, :].astype(F32) * ROOT_HALF
                + da_ref[r, at, :].astype(F32) * row_of(tab_ref, 0, s)
                + tok_ref[r, at, :].astype(F32) * row_of(tab_ref, SEGS, s)
                + row_of(tab_ref, 2 * SEGS, s)
            )
            out_ref[r, at, :] = out.astype(BF16)

        def mixed(t0):
            at = pl.ds(t0, CHUNK)
            t = frame_ids(t0, CHUNK, width)
            grad = (
                da_ref[r, at, :].astype(F32) * pick(tab_ref, 0, t, row)
                + tok_ref[r, at, :].astype(F32) * pick(tab_ref, SEGS, t, row)
                + pick(tab_ref, 2 * SEGS, t, row)
            )
            out = og_ref[r, at, :].astype(F32) * ROOT_HALF + jnp.where(t < row.ends[2], grad, 0.0)
            out_ref[r, at, :] = out.astype(BF16)

        row.chunks(uniform, mixed)
        row_copy(r).start()

    for_rows(len_ref, rows, frames, body)
    for r in range(rows):
        row_copy(r).wait()


def assemble_kernel(mine_ref, other_ref, out2_hbm, out1_hbm, buf_ref, sems):
    chips, count, _, rows, width = mine_ref.shape
    half = chips * count * rows // 3
    first = lax.axis_index("core") == 0
    copies = []
    for which, out_hbm in enumerate((out2_hbm, out1_hbm)):
        for b in range(chips * count):
            for j in range(rows // PAD):
                at = b * rows + j * PAD
                tap, channel = at // half, at % half
                block = (b // count, b % count, which, slice(j * PAD, (j + 1) * PAD))
                mine, other = mine_ref[block].astype(F32), other_ref[block].astype(F32)
                buf_ref[which, tap, channel : channel + PAD, :] = jnp.where(first, mine, other)
                buf_ref[which, tap, half + channel : half + channel + PAD, :] = jnp.where(first, other, mine)
        copies.append(pltpu.make_async_copy(buf_ref.at[which], out_hbm, sems.at[which]))
        copies[-1].start()
    for copy in copies:
        copy.wait()


SPACES = {"s": pltpu.SMEM, "v": pltpu.VMEM, "h": pltpu.HBM}


def call(kernel, spaces, arrays, outs, scratch, vmem_mib, flops=0, nbytes=8 << 20):
    arrays = [
        pltpu.with_memory_space_constraint(a, pltpu.HBM) if c == "h" else a for c, a in zip(spaces, arrays)
    ]
    letters = list(zip(spaces, [*arrays, *outs]))
    specs = [jax.tree.map(lambda _, c=c: pl.BlockSpec(memory_space=SPACES[c]), a) for c, a in letters[: len(arrays)]]

    def shape_of(c, out):
        return pltpu.HBM(*out) if c == "h" else jax.ShapeDtypeStruct(*out)

    def spec_of(c, out):
        return pl.BlockSpec(memory_space=SPACES[c])

    shapes, out_specs = (
        [[f(c, o) for o in out] if isinstance(out, list) else f(c, out) for c, out in letters[len(arrays) :]]
        for f in (shape_of, spec_of)
    )
    return pl.pallas_call(
        kernel,
        out_shape=shapes,
        in_specs=specs,
        out_specs=out_specs,
        scratch_shapes=[pltpu.SemaphoreType.DMA(s) if len(s) == 1 else pltpu.VMEM(*s) for s in scratch],
        compiler_params=pltpu.CompilerParams(vmem_limit_bytes=vmem_mib << 20),
        cost_estimate=pl.CostEstimate(flops=flops, bytes_accessed=nbytes, transcendentals=0),
    )(*arrays)


def after(x, *others):
    return lax.optimization_barrier((x, *others))[0]


def exchange(messages):
    return [messages[0]] + [swap(m, "tm", k) for k, m in enumerate(messages) if k > 0]


def scatter_sum(blocks, axis):
    return jnp.sum(lax.all_to_all(blocks, axis, 0, 0).astype(F32), axis=0).astype(BF16)


def spread(block, axis):
    return lax.all_to_all(jnp.broadcast_to(block[None], (lax.axis_size(axis), *block.shape)), axis, 0, 0)


def swap(x, axis, bit):
    return lax.ppermute(x, axis, [(i, i ^ bit) for i in range(lax.axis_size(axis))])


def sum_over_tm(x):
    count = lax.axis_size("tm")
    parts = [x.astype(F32)] + [swap(x, "tm", k).astype(F32) for k in range(1, count)]
    while len(parts) > 1:
        half = len(parts) // 2
        parts = [a + b for a, b in zip(parts[:half], parts[half:])]
    return parts[0]


def gather_rows(x):
    steps = [("core", 1)] + [("chip", 1 << b) for b in range((lax.axis_size("chip") - 1).bit_length())]
    for axis, bit in steps:
        other = swap(x, axis, bit)
        upper = (lax.axis_index(axis) & bit) != 0
        x = jnp.where(upper, jnp.concatenate([other, x]), jnp.concatenate([x, other]))
    return x


def per_device(tokens, lengths, style, fc1_weight, fc1_bias, conv1_kernel, fc2_weight, fc2_bias, conv2_kernel,
               conv2_bias, out_grad):
    rows, frames, width = tokens.shape
    count, chips = lax.axis_size("tm"), lax.axis_size("chip")
    padded = frames + 2 * PAD
    affine1 = jnp.einsum("rsk,kc->rsc", style, fc1_weight, preferred_element_type=F32) + fc1_bias.astype(F32)
    affine2 = jnp.einsum("rsk,kc->rsc", style, fc2_weight, preferred_element_type=F32) + fc2_bias.astype(F32)
    kernel1, kernel2 = (k.reshape(3 * width, width) for k in (conv1_kernel, conv2_kernel))

    own, wide = ((rows, frames, width), BF16), ((rows, padded, width), BF16)
    hid, taps, kernel = ((rows, padded, width), F32), ((rows, frames, 3 * width), BF16), ((3 * width, width), BF16)
    sums, msg, half = ((rows, 8, width), F32), ((2 * rows, width), F32), ((3 * width // 2, width), BF16)
    acc, tab = ((8, 8, width), F32), ((16, width), F32)
    buf, xs = ((padded, width), F32), ((padded, 3 * width), BF16)
    flops = 2 * rows * frames * 3 * width * width

    tok, w1, st1, msg1 = call(
        token_sums_kernel, "shhh" + "vvvv", (lengths, tokens, out_grad, kernel1),
        [own, kernel, sums, [((EDGE, width), F32)] * count],
        [((rows, PAD, width), BF16), ((rows, PAD, width), BF16), acc, (3,), (rows,)], SMALL,
    )
    rx1 = exchange(msg1)
    low1, hidden_hbm, hidden, st2, msg2, og, w2 = call(
        first_half_kernel, "svvvvvhh" + "hhvvvvv", (lengths, tok, st1, rx1, affine1, w1, out_grad, kernel2),
        [own, hid, hid, sums, msg, own, kernel], [own, buf, xs, tab, acc, (2,), (2 * rows,)], SMALL, flops,
    )
    rx2 = exchange([msg2] * count)
    gs2, grad_low2, bias_part = call(
        branch_grad_kernel, "svvv" + "vvv", (lengths, og, rx1, w2), [taps, wide, ((8, width), F32)], [buf, xs],
        SMALL, flops,
    )
    low2, low2_hbm, da2, gst2, msg3 = call(
        second_norm_kernel, "svvvvv" + "vhhvv", (lengths, hidden, grad_low2, st2, rx2, affine2),
        [wide, wide, wide, sums, msg], [wide, tab, acc, (2 * rows,)], SMALL,
    )
    rx3 = exchange([msg3] * count)

    def kernel_grad(own_half, first_frame, low, gs):
        return call(
            functools.partial(kernel_grad_kernel, own_half, first_frame), "vvv", (low, gs), [half],
            [((width // 2, 3 * width), F32)], SMALL, flops // 2,
        )[0]

    send2 = kernel_grad(False, PAD, low2, gs2)
    got2 = swap(send2, "core", 1)
    keep2 = kernel_grad(True, PAD, low2, after(gs2, send2, *rx3))
    half2 = (got2.astype(F32) + keep2.astype(F32)).astype(BF16)
    part2 = scatter_sum(half2.reshape(chips, -1, width), "chip")

    gs1, send1, keep1, affine_part2 = call(
        hidden_grad_kernel, "shhhvvvvv" + "hvvv",
        (lengths, low1, after(da2, half2), hidden_hbm, st2, rx2, gst2, rx3, affine2),
        [taps, half, half, ((4 * rows, 2 * width), F32)],
        [own, wide, hid, taps, buf, tab, ((width, 3 * width), F32), (3 * rows,), (rows,)], LARGE, flops,
    )
    got1 = swap(after(send1, part2), "core", 1)
    half1 = (got1.astype(F32) + keep1.astype(F32)).astype(BF16)
    part1 = scatter_sum(half1.reshape(chips, -1, width), "chip")

    da1, gst1, msg4, affine_part = call(
        first_norm_grad_kernel, "shhhvvvvv" + "hvvv",
        (lengths, after(gs1, half1), kernel1, tokens, st1, rx1, affine1, affine_part2, bias_part),
        [own, sums, msg, ((4 * rows, 4 * width), BF16)],
        [taps, kernel, own, own, ((frames, width), F32), tab, acc, ((4 * rows, 4 * width), F32), (1 + 2 * rows,), (rows,)],
        LARGE, flops,
    )
    both = jnp.concatenate([part2.reshape(count, -1, width), part1.reshape(count, -1, width)], axis=1)
    both = scatter_sum(after(both, da1), "tm")
    rx4 = exchange([after(msg4, part1)] * count)
    affine_grads = sum_over_tm(after(affine_part, part1)).astype(BF16)
    (block_out,) = call(
        block_out_kernel, "shhhv" + "h", (lengths, low2_hbm, after(tokens, da1), kernel2, conv2_bias.reshape(1, width)), [own],
        [wide, own, kernel, buf, ((frames, 3 * width), BF16), own, (1 + 2 * rows,), (rows,)], LARGE, flops,
    )
    both = spread(after(both, block_out), "tm")
    (input_grad,) = call(
        input_grad_kernel, "shhhvvvvv" + "h", (lengths, out_grad, da1, tokens, st1, rx1, gst1, rx4, affine1), [own],
        [own, own, own, tab, own, (3 * rows,), (rows,)], LARGE,
    )
    both = spread(after(both, input_grad), "chip")

    mine = affine_grads.reshape(rows, 4, 4 * width)[:, :SEGS].reshape(rows * SEGS, 4 * width)
    style_grad = lax.dot_general(
        mine[:, : 2 * width], fc1_weight, (((1,), (1,)), ((), ())), preferred_element_type=F32
    ) + lax.dot_general(mine[:, 2 * width :], fc2_weight, (((1,), (1,)), ((), ())), preferred_element_type=F32)
    style_pad = jnp.pad(style, ((0, 0), (0, 1), (0, 0))).reshape(rows * 4, -1)
    gathered = gather_rows(jnp.concatenate([affine_grads, style_pad], axis=1))
    grads, styles = gathered[:, : 4 * width], gathered[:, 4 * width :]
    fc_grads = lax.dot_general(styles, grads, (((0,), (0,)), ((), ())), preferred_element_type=F32)
    by_segment = jnp.sum(grads.reshape(-1, 4, 4 * width).astype(F32), axis=0)
    fc_bias_grads = jnp.sum(by_segment[:SEGS], axis=0)

    both = both.reshape(chips, count, 2, -1, width)
    other = swap(after(both, fc_grads, fc_bias_grads, style_grad), "core", 1)
    if both.shape[3] % PAD == 0:
        conv_shape = ((3, width, width), F32)
        conv2_sum, conv1_sum = call(
            assemble_kernel, "vv" + "hh", (both, other), [conv_shape, conv_shape], [((2, 3, width, width), F32), (2,)], SMALL,
        )
    else:
        first = lax.axis_index("core") == 0
        halves = [jnp.where(first, both, other), jnp.where(first, other, both)]
        halves = [jnp.moveaxis(h, 2, 0).reshape(2, 3, width // 2, width) for h in halves]
        conv2_sum, conv1_sum = jnp.concatenate(halves, axis=2).astype(F32)
    return (
        block_out,
        input_grad,
        style_grad.reshape(style.shape),
        fc_grads[:, : 2 * width],
        fc_bias_grads[: 2 * width],
        conv1_sum,
        fc_grads[:, 2 * width :],
        fc_bias_grads[2 * width :],
        conv2_sum,
        by_segment[SEGS, :width],
    )


def solution(mesh):
    chips = mesh.shape["dp"] // 2
    mesh = Mesh(mesh.devices.reshape(chips, 2, mesh.shape["tm"]), ("chip", "core", "tm"))
    dp = ("chip", "core")
    return jax.shard_map(
        per_device,
        mesh=mesh,
        in_specs=(
            P(dp, "tm", None),
            P(dp, None),
            P(dp, None, None),
            P(),
            P(),
            P(),
            P(),
            P(),
            P(),
            P(),
            P(dp, "tm", None),
        ),
        out_specs=(
            P(dp, "tm", None),
            P(dp, "tm", None),
            P(dp, None, None),
            P(),
            P(),
            P(),
            P(),
            P(),
            P(),
            P(),
        ),
        check_vma=False,
    )
```

```python
import functools

import jax
import jax.numpy as jnp
from jax import lax
from jax.experimental import pallas as pl
from jax.experimental.pallas import tpu as pltpu
from jax.sharding import Mesh, PartitionSpec as P

EPSILON = 1e-05
ROOT_HALF = 0.7071067811865476
SEGS = 3
PAD = 16
CHUNK = 32
EDGE = 8 + 16
F32 = jnp.float32
BF16 = jnp.bfloat16
SMALL, LARGE = 20, 30


class Row:
    def __init__(self, len_ref, r, frames):
        self.frames = frames
        self.z = lax.axis_index("tm")
        self.counts = [len_ref[r, s] for s in range(SEGS)]
        l0, l1, l2 = self.counts
        start = -self.z * frames
        e0 = start + l0
        e1 = e0 + l1
        e2 = e1 + l2
        self.begins = [start, e0, e1]
        self.ends = [e0, e1, e2]
        self.long_at = jnp.where(l0 >= jnp.maximum(l1, l2), 0, jnp.where(l1 >= l2, 1, 2))
        self.long_begin = self.of_long(self.begins)
        self.long_end = self.of_long(self.ends)

    def of_long(self, values):
        return jnp.where(
            self.long_at == 0, values[0], jnp.where(self.long_at == 1, values[1], values[2])
        )

    def segment(self, t):
        return sum((t >= e).astype(jnp.int32) for e in self.ends)

    def slot(self, t0):
        first, last = self.segment(t0), self.segment(t0 + CHUNK - 1)
        return jnp.where(first == last, first, SEGS)

    def mixed(self, fn):
        for end in self.ends:

            @pl.when(jnp.logical_and(jnp.logical_and(end > 0, end < self.frames), end % CHUNK != 0))
            def _(end=end):
                fn(pl.multiple_of((end // CHUNK) * CHUNK, CHUNK))


def frame_ids(t0, rows, width):
    return t0 + lax.broadcasted_iota(jnp.int32, (rows, width), 0)


def pick(tab_ref, base, t, row):
    value = tab_ref[base : base + 1, :]
    for s in range(SEGS):
        value = jnp.where(t >= row.ends[s], tab_ref[base + s + 1 : base + s + 2, :], value)
    return value


def row_of(tab_ref, base, s):
    return tab_ref[pl.ds(base + s, 1), :]


def put_table(tab_ref, base, values):
    for s in range(SEGS):
        tab_ref[base + s : base + s + 1, :] = values[s]
    tab_ref[base + SEGS : base + SEGS + 1, :] = jnp.zeros_like(values[0])


def fold(x):
    return jnp.sum(x.reshape(x.shape[0] // 8, 8, x.shape[1]), axis=0)


def add_sums(acc_ref, s, first, second):
    acc_ref[s] += fold(first)
    acc_ref[4 + s] += fold(second)


def add_masked_sums(acc_ref, t, row, first, second):
    for s in range(SEGS):
        inside = jnp.logical_and(t >= row.begins[s], t < row.ends[s])
        add_sums(acc_ref, s, jnp.where(inside, first, 0.0), jnp.where(inside, second, 0.0))


def put_sums(acc_ref, st_ref, msg_refs, row, r):
    for s in range(SEGS):
        for k in range(2):
            st_ref[r, pl.ds(SEGS * k + s, 1), :] = jnp.sum(acc_ref[4 * k + s], axis=0, keepdims=True)
    for k in range(2):
        value = jnp.sum(acc_ref[4 * k + row.long_at], axis=0, keepdims=True)
        for ref in msg_refs:
            ref[pl.ds(2 * r + k, 1), :] = value


def sums_of(row, r, st_ref, rx_refs, s):
    out = []
    for k in range(2):
        total = sum(ref[pl.ds(2 * r + k, 1), :] for ref in rx_refs)
        local = st_ref[r, SEGS * k + s : SEGS * k + s + 1, :]
        out.append(jnp.where(row.long_at == s, total, local))
    return out


def norm_of(row, r, st_ref, rx_ref, aff_ref, s):
    width = st_ref.shape[2]
    first, second = sums_of(row, r, st_ref, rx_ref, s)
    count = jnp.full((1, width), row.counts[s].astype(F32))
    mean = first / count
    rstd = lax.rsqrt(second / count - mean * mean + EPSILON)
    affine = aff_ref[r, s : s + 1, :]
    return mean, rstd, 1.0 + affine[:, :width], affine[:, width:], count


def put_forward(row, r, st_ref, rx_ref, aff_ref, tab_ref):
    scales, shifts = [], []
    for s in range(SEGS):
        mean, rstd, gain, beta, _ = norm_of(row, r, st_ref, rx_ref, aff_ref, s)
        scales.append(gain * rstd)
        shifts.append(beta - mean * scales[-1])
    put_table(tab_ref, 0, scales)
    put_table(tab_ref, 4, shifts)
    tab_ref[12:13, :] = row.of_long(scales)
    tab_ref[13:14, :] = row.of_long(shifts)


def put_backward(row, r, st_ref, rx_ref, gst_ref, grx_ref, aff_ref, tab_ref):
    parts = [[], [], []]
    for s in range(SEGS):
        mean, rstd, gain, _, count = norm_of(row, r, st_ref, rx_ref, aff_ref, s)
        if isinstance(grx_ref, (list, tuple)):
            shift, scale = sums_of(row, r, gst_ref, grx_ref, s)
            scale = rstd * (scale - mean * shift)
        else:
            width = mean.shape[1]
            total = grx_ref[pl.ds(4 * r + s, 1), : 2 * width] + grx_ref[pl.ds(4 * r + SEGS, 1), 2 * width :]
            shift, local = gst_ref[r, s : s + 1, :], gst_ref[r, SEGS + s : SEGS + s + 1, :]
            scale = jnp.where(row.long_at == s, total[:, :width], rstd * (local - mean * shift))
            shift = jnp.where(row.long_at == s, total[:, width:], shift)
        mean_g = gain * shift / count
        slope = rstd * rstd * (gain * scale / count)
        parts[0].append(gain * rstd)
        parts[1].append(-slope)
        parts[2].append(slope * mean - rstd * mean_g)
    for k in range(3):
        put_table(tab_ref, 4 * k, parts[k])
        tab_ref[12 + k : 13 + k, :] = row.of_long(parts[k])


def put_affine_grads(row, r, st_ref, rx_ref, gst_ref, aff_ref, out_ref, at):
    width = st_ref.shape[2]
    for s in range(SEGS):
        mean, rstd, _, _, _ = norm_of(row, r, st_ref, rx_ref, aff_ref, s)
        shift = gst_ref[r, s : s + 1, :]
        scale = rstd * (gst_ref[r, SEGS + s : SEGS + s + 1, :] - mean * shift)
        out_ref[pl.ds(4 * r + s, 1), at : at + width] = scale
        out_ref[pl.ds(4 * r + s, 1), at + width : at + 2 * width] = shift


def silu(a):
    half = 0.5 * a
    return half + half * jnp.tanh(half)


def silu_and_slope(a):
    gate = 0.5 + 0.5 * jnp.tanh(0.5 * a)
    low = a * gate
    return low, gate + low * (1.0 - gate)


def halo_tile(row, frames, width, left):
    t = frame_ids(-PAD if left else frames, PAD, width)
    near = jnp.logical_and(t >= -2, t < frames + 2)
    inside = jnp.logical_and(t >= row.long_begin, t < row.long_end)
    return t, jnp.logical_and(near, inside)


def edge_tile(rx_refs, row, r, t, at, left):
    last = len(rx_refs) - 1
    neighbour = jnp.maximum(row.z - 1, 0) if left else jnp.minimum(row.z + 1, last)
    edges = []
    for i in range(2):
        value, k = rx_refs[1][pl.ds(8 + 4 * r + at + i, 1), :], 3
        while k <= last:
            value = jnp.where((row.z ^ neighbour) == k, rx_refs[k][pl.ds(8 + 4 * r + at + i, 1), :], value)
            k = 2 * k + 1
        edges.append(value)
    second = -1 if left else row.frames + 1
    return jnp.where(t == second, edges[1], edges[0])


def chunks(frames):
    return range(0, frames, CHUNK)


def tap_blocks(ref, at, rows, step):
    if at - step < 0 or at + rows - step > ref.shape[0]:
        return pltpu.roll(ref[at : at + rows, :], step % rows, 0)
    return ref[at - step : at - step + rows, :]


def tap_sum(z_ref, at, rows, before, after):
    return tap_blocks(z_ref.at[before], at, rows, 1) + z_ref[1, at : at + rows, :] + tap_blocks(z_ref.at[after], at, rows, -1)


def cut_products(z_ref, row, before, after):
    for end in row.ends:

        @pl.when(jnp.logical_and(end >= 0, end <= row.frames))
        def _(end=end):
            zero = jnp.zeros((1, z_ref.shape[2]), F32)
            z_ref[before, pl.ds(PAD + end - 1, 1), :] = zero
            z_ref[after, pl.ds(PAD + end, 1), :] = zero


def put_products(x_ref, w_ref, z_ref, transposed):
    width = x_ref.shape[1]
    for k in range(3):
        tap = w_ref[k * width : (k + 1) * width, :]
        z_ref[k] = lax.dot_general(
            x_ref[...], tap, (((1,), (1 if transposed else 0,)), ((), ())), preferred_element_type=F32
        )


def put_taps(buf_ref, gs_ref, frames):
    width = buf_ref.shape[1]
    for t0 in chunks(frames):
        o = PAD + t0
        for k, step in enumerate((-1, 0, 1)):
            gs_ref[t0 : t0 + CHUNK, k * width : (k + 1) * width] = buf_ref[o - step : o - step + CHUNK, :].astype(BF16)


def cut_taps(gs_ref, row):
    width = gs_ref.shape[1] // 3
    for end in row.ends[:2]:
        for at, t in ((2 * width, end), (0, end - 1)):

            @pl.when(jnp.logical_and(t >= 0, t < row.frames))
            def _(at=at, t=t):
                tile = pl.multiple_of((t // PAD) * PAD, PAD)
                value = gs_ref[pl.ds(tile, PAD), at : at + width].astype(F32)
                keep = frame_ids(tile, PAD, width) != t
                gs_ref[pl.ds(tile, PAD), at : at + width] = jnp.where(keep, value, 0.0).astype(BF16)


def pipeline(rows, *stages):
    for i in range(rows + len(stages) - 1):
        live = [(stage, i - k) for k, stage in enumerate(stages) if 0 <= i - k < rows]
        for (work, _), r in live:
            work(r)
        for (_, then), r in live:
            then(r)


class Loads:
    def __init__(self, rows, sems, whole, by_row):
        count = len(whole)
        self.whole = [pltpu.make_async_copy(a, b, sems.at[i]) for i, (a, b) in enumerate(whole)]
        self.rows = [
            [pltpu.make_async_copy(a.at[r], b.at[r], sems.at[count + i * rows + r]) for i, (a, b) in enumerate(by_row)]
            for r in range(rows)
        ]
        for r in range(rows):
            for copy in self.rows[r]:
                copy.start()
            if r == 0:
                for copy in self.whole:
                    copy.start()

    def wait(self, r):
        for copy in self.rows[r]:
            copy.wait()
        if r == 0:
            self.wait_whole()

    def wait_whole(self):
        for copy in self.whole:
            copy.wait()
        self.whole = []


class Stores:
    def __init__(self, sems, *pairs):
        self.sems, self.pairs, self.copies = sems, pairs, []

    def start(self, r):
        for a, b in self.pairs:
            self.copies.append(pltpu.make_async_copy(a(r), b.at[r], self.sems.at[len(self.copies)]))
            self.copies[-1].start()

    def wait(self):
        for copy in self.copies:
            copy.wait()


def token_sums_kernel(len_ref, tok_hbm, og_hbm, w_hbm, tok_ref, w_ref, st_ref, msg_refs, head_ref, tail_ref, acc_ref,
                      sems, row_sems):
    rows, frames, width = tok_ref.shape
    tokens = Loads(rows, row_sems, [], [(tok_hbm, tok_ref)])
    edges = Loads(
        0, sems, [], []
    )
    edges.whole = [
        pltpu.make_async_copy(og_hbm.at[:, pl.ds(0, PAD), :], head_ref, sems.at[0]),
        pltpu.make_async_copy(og_hbm.at[:, pl.ds(frames - PAD, PAD), :], tail_ref, sems.at[1]),
    ]
    kernel_copy = pltpu.make_async_copy(w_hbm, w_ref, sems.at[2])
    for copy in (*edges.whole, kernel_copy):
        copy.start()
    edges.wait_whole()
    row_at = [Row(len_ref, r, frames) for r in range(rows)]

    def sums(r):
        tokens.wait(r)
        acc_ref[r] = jnp.zeros(acc_ref.shape[1:], F32)
        for t0 in chunks(frames):
            v = tok_ref[r, t0 : t0 + CHUNK, :].astype(F32)
            add_sums(acc_ref.at[r], row_at[r].slot(t0), v, v * v)

    def sums_then(r):
        row = row_at[r]

        def mixed(t0):
            v = tok_ref[r, pl.ds(t0, CHUNK), :].astype(F32)
            add_masked_sums(acc_ref.at[r], frame_ids(t0, CHUNK, width), row, v, v * v)

        row.mixed(mixed)
        put_sums(acc_ref.at[r], st_ref, msg_refs, row, r)
        for j, (head, tail) in enumerate(
            ((tok_ref[r, 0:PAD, :], tok_ref[r, frames - PAD : frames, :]), (head_ref[r], tail_ref[r]))
        ):
            first, last = head.astype(F32), tail.astype(F32)
            for k, ref in enumerate(msg_refs):
                value = jnp.where(row.z < row.z ^ k, last[PAD - 2 :, :], first[:2, :])
                ref[8 + 4 * r + 2 * j : 10 + 4 * r + 2 * j, :] = value

    pipeline(rows, (sums, sums_then))
    kernel_copy.wait()


def first_half_kernel(len_ref, tok_ref, st_ref, rx_refs, aff_ref, w_ref, og_hbm, w2_hbm, low_hbm, hid_hbm,
                      hid_ref, st2_ref, msg_ref, og_ref, w2_ref, low_refs, z_refs, tab_ref, acc_ref, sems, row_sems):
    rows, frames, width = tok_ref.shape
    following = [
        pltpu.make_async_copy(og_hbm, og_ref, sems.at[0]),
        pltpu.make_async_copy(w2_hbm, w2_ref, sems.at[1]),
    ]
    for copy in following:
        copy.start()
    low_out = Stores(row_sems, (lambda r: low_refs[r].at[pl.ds(PAD, frames), :], low_hbm))
    hid_out = Stores(row_sems.at[pl.ds(rows, rows)], (lambda r: hid_ref.at[r], hid_hbm))
    row_at = [Row(len_ref, r, frames) for r in range(rows)]

    def norm(r):
        row, tab = row_at[r], tab_ref.at[r]
        put_forward(row, r, st_ref, rx_refs, aff_ref, tab)
        for t0 in chunks(frames):
            s = row.segment(t0)
            v = tok_ref[r, t0 : t0 + CHUNK, :].astype(F32)
            low = silu(v * row_of(tab, 0, s) + row_of(tab, 4, s))
            low_refs[r][PAD + t0 : PAD + t0 + CHUNK, :] = low.astype(BF16)
        for left in (True, False):
            t, valid = halo_tile(row, frames, width, left)
            low = silu(edge_tile(rx_refs, row, r, t, 0, left) * tab[12:13, :] + tab[13:14, :])
            at = 0 if left else PAD + frames
            low_refs[r][at : at + PAD, :] = jnp.where(valid, low, 0.0).astype(BF16)

    def norm_then(r):
        row, tab = row_at[r], tab_ref.at[r]

        def mixed(t0):
            t = frame_ids(t0, CHUNK, width)
            v = tok_ref[r, pl.ds(t0, CHUNK), :].astype(F32)
            low = silu(v * pick(tab, 0, t, row) + pick(tab, 4, t, row))
            low_refs[r][pl.ds(PAD + t0, CHUNK), :] = low.astype(BF16)

        row.mixed(mixed)
        low_out.start(r)

    def conv(r):
        put_products(low_refs[r], w_ref, z_refs[r % 2], False)

    def conv_then(r):
        cut_products(z_refs[r % 2], row_at[r], 0, 2)

    def sums(r):
        row, z = row_at[r], z_refs[r % 2]
        acc_ref[r] = jnp.zeros(acc_ref.shape[1:], F32)
        for t0 in chunks(frames):
            v = tap_sum(z, PAD + t0, CHUNK, 0, 2)
            hid_ref[r, PAD + t0 : PAD + t0 + CHUNK, :] = v
            add_sums(acc_ref.at[r], row.slot(t0), v, v * v)
        for at in (0, PAD + frames):
            hid_ref[r, at : at + PAD, :] = tap_sum(z, at, PAD, 0, 2)

    def sums_then(r):
        row = row_at[r]

        def mixed(t0):
            v = hid_ref[r, pl.ds(PAD + t0, CHUNK), :]
            add_masked_sums(acc_ref.at[r], frame_ids(t0, CHUNK, width), row, v, v * v)

        hid_out.start(r)
        row.mixed(mixed)
        put_sums(acc_ref.at[r], st2_ref, [msg_ref], row, r)

    pipeline(rows, (norm, norm_then), (conv, conv_then), (sums, sums_then))
    for copy in following:
        copy.wait()
    low_out.wait()
    hid_out.wait()


def branch_grad_kernel(len_ref, og_ref, rx_refs, w_ref, gs_ref, q_ref, bias_ref, buf_refs, g_refs, z_refs, acc_ref):
    rows, frames, width = og_ref.shape
    row_at = [Row(len_ref, r, frames) for r in range(rows)]
    acc_ref[...] = jnp.zeros_like(acc_ref)

    def put(r, at, rows_at, g):
        low = g.astype(BF16)
        g_refs[r % 2][at, :] = low
        buf_refs[r % 2][at, :] = low.astype(F32)
        return low.astype(F32)

    def grad(r):
        row = row_at[r]
        for t0 in chunks(frames):
            scale = jnp.where(row.segment(t0) < SEGS, ROOT_HALF, 0.0)
            g = og_ref[r, t0 : t0 + CHUNK, :].astype(F32) * scale
            g = put(r, slice(PAD + t0, PAD + t0 + CHUNK), CHUNK, g)
            acc_ref[jnp.where(row.slot(t0) < SEGS, 0, 1)] += fold(g)
        for left in (True, False):
            t, valid = halo_tile(row, frames, width, left)
            at = 0 if left else PAD + frames
            g = edge_tile(rx_refs, row, r, t, 2, left) * ROOT_HALF
            put(r, slice(at, at + PAD), PAD, jnp.where(valid, g, 0.0))

    def grad_then(r):
        row = row_at[r]

        def mixed(t0):
            t = frame_ids(t0, CHUNK, width)
            g = og_ref[r, pl.ds(t0, CHUNK), :].astype(F32) * ROOT_HALF
            acc_ref[0] += fold(put(r, pl.ds(PAD + t0, CHUNK), CHUNK, jnp.where(t < row.ends[2], g, 0.0)))

        row.mixed(mixed)

    def conv(r):
        put_products(g_refs[r % 2], w_ref, z_refs[r % 2], True)
        put_taps(buf_refs[r % 2], gs_ref.at[r], frames)

    def conv_then(r):
        cut_products(z_refs[r % 2], row_at[r], 2, 0)
        cut_taps(gs_ref.at[r], row_at[r])

    def combine(r):
        z = z_refs[r % 2]
        for t0 in chunks(frames):
            at = PAD + t0
            q_ref[r, at : at + CHUNK, :] = tap_sum(z, at, CHUNK, 2, 0).astype(BF16)
        for at in (0, PAD + frames):
            q_ref[r, at : at + PAD, :] = tap_sum(z, at, PAD, 2, 0).astype(BF16)

    pipeline(rows, (grad, grad_then), (conv, conv_then), (combine, lambda r: None))
    bias_ref[...] = acc_ref[0]


def second_norm_kernel(len_ref, hid_ref, q_ref, st_ref, rx_refs, aff_ref, low_ref, low_hbm, da_hbm, gst_ref, msg_ref,
                       da_ref, tab_ref, acc_ref, row_sems):
    rows, padded, width = hid_ref.shape
    frames = padded - 2 * PAD
    row_at = [Row(len_ref, r, frames) for r in range(rows)]
    out = Stores(row_sems, (lambda r: low_ref.at[r], low_hbm), (lambda r: da_ref.at[r], da_hbm))

    def both(r, at, scale, shift):
        v = hid_ref[r, at, :]
        low, slope = silu_and_slope(v * scale + shift)
        return v, low, slope * q_ref[r, at, :].astype(F32)

    def norm(r):
        row, tab = row_at[r], tab_ref.at[r]
        put_forward(row, r, st_ref, rx_refs, aff_ref, tab)
        acc_ref[r] = jnp.zeros(acc_ref.shape[1:], F32)
        for t0 in chunks(frames):
            at, s = slice(PAD + t0, PAD + t0 + CHUNK), row.segment(t0)
            v, low, da = both(r, at, row_of(tab, 0, s), row_of(tab, 4, s))
            low_ref[r, at, :] = low.astype(BF16)
            da_ref[r, at, :] = da.astype(BF16)
            add_sums(acc_ref.at[r], row.slot(t0), da, da * v)
        for left in (True, False):
            t, valid = halo_tile(row, frames, width, left)
            at = slice(0, PAD) if left else slice(PAD + frames, padded)
            _, low, da = both(r, at, tab[12:13, :], tab[13:14, :])
            low_ref[r, at, :] = jnp.where(valid, low, 0.0).astype(BF16)
            da_ref[r, at, :] = jnp.where(valid, da, 0.0).astype(BF16)

    def norm_then(r):
        row, tab = row_at[r], tab_ref.at[r]

        def mixed(t0):
            at, t = pl.ds(PAD + t0, CHUNK), frame_ids(t0, CHUNK, width)
            v, low, da = both(r, at, pick(tab, 0, t, row), pick(tab, 4, t, row))
            low_ref[r, at, :] = low.astype(BF16)
            da_ref[r, at, :] = da.astype(BF16)
            add_masked_sums(acc_ref.at[r], t, row, da, da * v)

        row.mixed(mixed)
        out.start(r)
        put_sums(acc_ref.at[r], gst_ref, [msg_ref], row, r)

    pipeline(rows, (norm, norm_then))
    out.wait()


def block_out_kernel(len_ref, low_hbm, tok_hbm, w_hbm, bias_ref, out_hbm, low_ref, tok_ref, w_ref, z_refs, out_ref,
                     sems, row_sems):
    rows, frames, width = tok_ref.shape
    loads = Loads(rows, sems, [(w_hbm, w_ref)], [(low_hbm, low_ref), (tok_hbm, tok_ref)])
    out = Stores(row_sems, (lambda r: out_ref.at[r], out_hbm))
    row_at = [Row(len_ref, r, frames) for r in range(rows)]
    bias = bias_ref[...].astype(F32)

    def conv(r):
        loads.wait(r)
        put_products(low_ref.at[r], w_ref, z_refs[r % 2], False)

    def conv_then(r):
        cut_products(z_refs[r % 2], row_at[r], 0, 2)

    def combine(r):
        for t0 in chunks(frames):
            at, t = slice(t0, t0 + CHUNK), frame_ids(t0, CHUNK, width)
            branch = tap_sum(z_refs[r % 2], PAD + t0, CHUNK, 0, 2) + jnp.where(t < row_at[r].ends[2], bias, 0.0)
            out_ref[r, at, :] = ((tok_ref[r, at, :].astype(F32) + branch) * ROOT_HALF).astype(BF16)

    pipeline(rows, (conv, conv_then), (combine, out.start))
    out.wait()


def half_of_grad(low_ref, gs_ref, r, half, first_frame):
    frames, width = gs_ref.shape[1], low_ref.shape[2] // 2
    u = low_ref[r, first_frame : first_frame + frames, pl.ds(pl.multiple_of(half * width, width), width)]
    return lax.dot_general(u, gs_ref[r], (((0,), (0,)), ((), ())), preferred_element_type=F32)


def put_half(acc_ref, out_ref):
    half, width = acc_ref.shape[0], acc_ref.shape[1] // 3
    for k in range(3):
        out_ref[k * half : (k + 1) * half, :] = acc_ref[:, k * width : (k + 1) * width].astype(BF16)


def kernel_grad_kernel(own, first_frame, low_ref, gs_ref, out_ref, acc_ref):
    core = lax.axis_index("core")
    half = core if own else 1 - core
    acc_ref[...] = half_of_grad(low_ref, gs_ref, 0, half, first_frame)

    def step(r, carry):
        acc_ref[...] += half_of_grad(low_ref, gs_ref, r, half, first_frame)
        return carry

    lax.fori_loop(1, low_ref.shape[0], step, 0)
    put_half(acc_ref, out_ref)


def hidden_grad_kernel(len_ref, low_hbm, da_hbm, hid_hbm, st_ref, rx_refs, gst_ref, grx_refs, aff_ref,
                       g_hbm, send_ref, keep_ref, part_ref, low_ref, da_ref, hid_ref, g_ref, buf_refs, gs_refs, tab_ref,
                       acc_ref, sems, row_sems):
    rows, frames, width = low_ref.shape
    loads = Loads(rows, sems, [], [(da_hbm, da_ref), (hid_hbm, hid_ref), (low_hbm, low_ref)])
    out = Stores(row_sems, (lambda r: g_ref.at[r], g_hbm))
    row_at = [Row(len_ref, r, frames) for r in range(rows)]
    part_ref[...] = jnp.zeros_like(part_ref)

    def grad_at(r, at, tab, picked):
        return da_ref[r, at, :].astype(F32) * picked(0) + hid_ref[r, at, :] * picked(4) + picked(8)

    def put(r, at, grad):
        g_ref[r, at, :] = grad.astype(BF16)
        buf_refs[r % 2][at, :] = grad

    def grad(r):
        row, tab = row_at[r], tab_ref.at[r]
        put_affine_grads(row, r, st_ref, rx_refs, gst_ref, aff_ref, part_ref, 0)
        put_backward(row, r, st_ref, rx_refs, gst_ref, grx_refs, aff_ref, tab)
        loads.wait(r)
        for t0 in chunks(frames):
            at, s = slice(PAD + t0, PAD + t0 + CHUNK), row.segment(t0)
            put(r, at, grad_at(r, at, tab, lambda base: row_of(tab, base, s)))
        for left in (True, False):
            t, valid = halo_tile(row, frames, width, left)
            at = slice(0, PAD) if left else slice(PAD + frames, 2 * PAD + frames)
            grad = grad_at(r, at, tab, lambda base: tab[12 + base // 4 : 13 + base // 4, :])
            put(r, at, jnp.where(valid, grad, 0.0))

    def grad_then(r):
        row, tab = row_at[r], tab_ref.at[r]

        def mixed(t0):
            at, t = pl.ds(PAD + t0, CHUNK), frame_ids(t0, CHUNK, width)
            put(r, at, grad_at(r, at, tab, lambda base: pick(tab, base, t, row)))

        row.mixed(mixed)
        out.start(r)

    def taps(r):
        put_taps(buf_refs[r % 2], gs_refs[r % 2], frames)

    def taps_then(r):
        cut_taps(gs_refs[r % 2], row_at[r])

    def product(r):
        part = lax.dot_general(low_ref[r], gs_refs[r % 2][...], (((0,), (0,)), ((), ())), preferred_element_type=F32)
        acc_ref[...] = part if r == 0 else acc_ref[...] + part

    pipeline(rows, (grad, grad_then), (taps, taps_then), (product, lambda r: None))
    core, half = lax.axis_index("core"), width // 2
    for ref, which in ((send_ref, 1 - core), (keep_ref, core)):
        put_half(acc_ref.at[pl.ds(pl.multiple_of(which * half, half), half), :], ref)
    out.wait()


def first_norm_grad_kernel(len_ref, g_hbm, w_hbm, tok_hbm, st_ref, rx_refs, aff_ref, part2_ref, bias_ref,
                           da_hbm, gst_ref, out_ref, g_ref, w_ref, tok_ref, da_ref, z_refs, q_ref, tab_ref, acc_ref,
                           part_ref, sems, row_sems):
    rows, frames, width = tok_ref.shape
    loads = Loads(rows, sems, [(w_hbm, w_ref)], [(g_hbm, g_ref), (tok_hbm, tok_ref)])
    out = Stores(row_sems, (lambda r: da_ref.at[r], da_hbm))
    row_at = [Row(len_ref, r, frames) for r in range(rows)]
    part_ref[:, : 2 * width] = jnp.zeros((part_ref.shape[0], 2 * width), F32)
    part_ref[:, 2 * width :] = part2_ref[...]
    part_ref[SEGS : SEGS + 1, :width] = jnp.sum(bias_ref[...], axis=0, keepdims=True)

    def conv(r):
        put_forward(row_at[r], r, st_ref, rx_refs, aff_ref, tab_ref.at[r])
        loads.wait(r)
        put_products(g_ref.at[r], w_ref, z_refs[r % 2], True)

    def conv_then(r):
        cut_products(z_refs[r % 2], row_at[r], 2, 0)

    def back(r):
        row, tab = row_at[r], tab_ref.at[r]
        acc_ref[r] = jnp.zeros(acc_ref.shape[1:], F32)
        for t0 in chunks(frames):
            at, s = slice(t0, t0 + CHUNK), row.segment(t0)
            v = tok_ref[r, at, :].astype(F32)
            q = tap_sum(z_refs[r % 2], PAD + t0, CHUNK, 2, 0)
            q_ref[at, :] = q
            da = silu_and_slope(v * row_of(tab, 0, s) + row_of(tab, 4, s))[1] * q
            da_ref[r, at, :] = da.astype(BF16)
            add_sums(acc_ref.at[r], row.slot(t0), da, da * v)

    def back_then(r):
        row, tab = row_at[r], tab_ref.at[r]

        def mixed(t0):
            at, t = pl.ds(t0, CHUNK), frame_ids(t0, CHUNK, width)
            v = tok_ref[r, at, :].astype(F32)
            da = silu_and_slope(v * pick(tab, 0, t, row) + pick(tab, 4, t, row))[1] * q_ref[at, :]
            da_ref[r, at, :] = da.astype(BF16)
            add_masked_sums(acc_ref.at[r], t, row, da, da * v)

        row.mixed(mixed)
        out.start(r)
        put_sums(acc_ref.at[r], gst_ref, [], row, r)
        put_affine_grads(row, r, st_ref, rx_refs, gst_ref, aff_ref, part_ref, 0)
        value = part_ref[pl.ds(4 * r + row.long_at, 1), : 2 * width]
        part_ref[pl.ds(4 * r + SEGS, 1), 2 * width :] = value - value.astype(BF16).astype(F32)

    pipeline(rows, (conv, conv_then), (back, back_then))
    out_ref[...] = part_ref[...].astype(BF16)
    out.wait()


def input_grad_kernel(len_ref, og_hbm, da_hbm, tok_hbm, st_ref, rx_refs, gst_ref, grx_ref, aff_ref, out_hbm,
                      og_ref, da_ref, tok_ref, tab_ref, out_ref, sems, row_sems):
    rows, frames, width = tok_ref.shape
    loads = Loads(rows, sems, [], [(og_hbm, og_ref), (da_hbm, da_ref), (tok_hbm, tok_ref)])
    out = Stores(row_sems, (lambda r: out_ref.at[r], out_hbm))
    row_at = [Row(len_ref, r, frames) for r in range(rows)]

    def put(r, at, picked):
        out_ref[r, at, :] = (
            og_ref[r, at, :].astype(F32) * ROOT_HALF
            + da_ref[r, at, :].astype(F32) * picked(0)
            + tok_ref[r, at, :].astype(F32) * picked(4)
            + picked(8)
        ).astype(BF16)

    def grad(r):
        row, tab = row_at[r], tab_ref.at[r]
        put_backward(row, r, st_ref, rx_refs, gst_ref, grx_ref, aff_ref, tab)
        loads.wait(r)
        for t0 in chunks(frames):
            s = row.segment(t0)
            put(r, slice(t0, t0 + CHUNK), lambda base, s=s: row_of(tab, base, s))

    def grad_then(r):
        row, tab = row_at[r], tab_ref.at[r]

        def mixed(t0):
            t = frame_ids(t0, CHUNK, width)
            put(r, pl.ds(t0, CHUNK), lambda base: pick(tab, base, t, row))

        row.mixed(mixed)
        out.start(r)

    pipeline(rows, (grad, grad_then))
    out.wait()


def projection_grad_kernel(all_ref, fc1_hbm, fc2_hbm, bias1_ref, bias2_ref, conv_bias_ref, rows_ref, grad_ref, sems):
    device = lax.axis_index("chip") * 2 + lax.axis_index("core")
    width = conv_bias_ref.shape[1]
    for i in range(all_ref.shape[0] // PAD):
        block = pl.ds(pl.multiple_of((device ^ i) * PAD, PAD), PAD)
        rows_ref[i * PAD : (i + 1) * PAD, :] = all_ref[block, :]
    grads, styles = rows_ref[:, : 4 * width], rows_ref[:, 4 * width :]
    grad_ref[...] = lax.dot_general(styles, grads, (((0,), (0,)), ((), ())), preferred_element_type=F32)
    copies = [
        pltpu.make_async_copy(grad_ref.at[:, pl.ds(i * 2 * width, 2 * width)], out, sems.at[i])
        for i, out in enumerate((fc1_hbm, fc2_hbm))
    ]
    for copy in copies:
        copy.start()
    values = grads.astype(F32)
    of_segment = frame_ids(0, values.shape[0], values.shape[1]) % 4 < SEGS
    bias = jnp.sum(jnp.where(of_segment, values, 0.0), axis=0, keepdims=True)
    bias1_ref[...] = bias[:, : 2 * width]
    bias2_ref[...] = bias[:, 2 * width :]
    rest = jnp.where(of_segment[:, :width], 0.0, values[:, :width])
    conv_bias_ref[...] = jnp.sum(rest, axis=0, keepdims=True)
    for copy in copies:
        copy.wait()


def assemble_kernel(mine_ref, other_ref, out2_hbm, out1_hbm, buf_ref, sems):
    chips, count, _, rows, width = mine_ref.shape
    half = chips * count * rows // 3
    first = lax.axis_index("core") == 0
    copies = []
    for which, out_hbm in enumerate((out2_hbm, out1_hbm)):
        for b in range(chips * count):
            for j in range(rows // PAD):
                at = b * rows + j * PAD
                tap, channel = at // half, at % half
                block = (b // count, b % count, which, slice(j * PAD, (j + 1) * PAD))
                mine, other = mine_ref[block].astype(F32), other_ref[block].astype(F32)
                buf_ref[which, tap, channel : channel + PAD, :] = jnp.where(first, mine, other)
                buf_ref[which, tap, half + channel : half + channel + PAD, :] = jnp.where(first, other, mine)
        copies.append(pltpu.make_async_copy(buf_ref.at[which], out_hbm, sems.at[which]))
        copies[-1].start()
    for copy in copies:
        copy.wait()


SPACES = {"s": pltpu.SMEM, "v": pltpu.VMEM, "h": pltpu.HBM}


def call(kernel, spaces, arrays, outs, scratch, vmem_mib, flops=0, nbytes=8 << 20):
    arrays = [
        pltpu.with_memory_space_constraint(a, pltpu.HBM) if c == "h" else a for c, a in zip(spaces, arrays)
    ]
    letters = list(zip(spaces, [*arrays, *outs]))
    specs = [jax.tree.map(lambda _, c=c: pl.BlockSpec(memory_space=SPACES[c]), a) for c, a in letters[: len(arrays)]]

    def shape_of(c, out):
        return pltpu.HBM(*out) if c == "h" else jax.ShapeDtypeStruct(*out)

    def spec_of(c, out):
        return pl.BlockSpec(memory_space=SPACES[c])

    shapes, out_specs = (
        [[f(c, o) for o in out] if isinstance(out, list) else f(c, out) for c, out in letters[len(arrays) :]]
        for f in (shape_of, spec_of)
    )
    return pl.pallas_call(
        kernel,
        out_shape=shapes,
        in_specs=specs,
        out_specs=out_specs,
        scratch_shapes=jax.tree.map(
            lambda s: pltpu.SemaphoreType.DMA(s) if len(s) == 1 else pltpu.VMEM(*s),
            list(scratch),
            is_leaf=lambda s: isinstance(s, tuple),
        ),
        compiler_params=pltpu.CompilerParams(vmem_limit_bytes=vmem_mib << 20),
        cost_estimate=pl.CostEstimate(flops=flops, bytes_accessed=nbytes, transcendentals=0),
    )(*arrays)


def after(x, *others):
    return lax.optimization_barrier((x, *others))[0]


def exchange(messages):
    return [messages[0]] + [swap(m, "tm", k) for k, m in enumerate(messages) if k > 0]


def scatter_sum(blocks, axis):
    return jnp.sum(lax.all_to_all(blocks, axis, 0, 0).astype(F32), axis=0).astype(BF16)


def spread(block, axis):
    return lax.all_to_all(jnp.broadcast_to(block[None], (lax.axis_size(axis), *block.shape)), axis, 0, 0)


def swap(x, axis, bit):
    return lax.ppermute(x, axis, [(i, i ^ bit) for i in range(lax.axis_size(axis))])


def sum_over_tm(x):
    count = lax.axis_size("tm")
    parts = [x.astype(F32)] + [swap(x, "tm", k).astype(F32) for k in range(1, count)]
    while len(parts) > 1:
        half = len(parts) // 2
        parts = [a + b for a, b in zip(parts[:half], parts[half:])]
    return parts[0]


def gather_rows(x):
    steps = [("core", 1)] + [("chip", 1 << b) for b in range((lax.axis_size("chip") - 1).bit_length())]
    for axis, bit in steps:
        x = jnp.concatenate([x, swap(x, axis, bit)])
    return x


def per_device(tokens, lengths, style, fc1_weight, fc1_bias, conv1_kernel, fc2_weight, fc2_bias, conv2_kernel,
               conv2_bias, out_grad):
    rows, frames, width = tokens.shape
    count, chips = lax.axis_size("tm"), lax.axis_size("chip")
    padded = frames + 2 * PAD
    affine1 = jnp.einsum("rsk,kc->rsc", style, fc1_weight, preferred_element_type=F32) + fc1_bias.astype(F32)
    affine2 = jnp.einsum("rsk,kc->rsc", style, fc2_weight, preferred_element_type=F32) + fc2_bias.astype(F32)
    kernel1, kernel2 = (k.reshape(3 * width, width) for k in (conv1_kernel, conv2_kernel))

    own, wide = ((rows, frames, width), BF16), ((rows, padded, width), BF16)
    hid, taps, kernel = ((rows, padded, width), F32), ((rows, frames, 3 * width), BF16), ((3 * width, width), BF16)
    sums, msg, half = ((rows, 8, width), F32), ((2 * rows, width), F32), ((3 * width // 2, width), BF16)
    acc, tab = ((rows, 8, 8, width), F32), ((rows, 16, width), F32)
    products, buf = [((3, padded, width), F32)] * 2, [((padded, width), F32)] * 2
    flops = 2 * rows * frames * 3 * width * width

    tok, w1, st1, msg1 = call(
        token_sums_kernel, "shhh" + "vvvv", (lengths, tokens, out_grad, kernel1),
        [own, kernel, sums, [((EDGE, width), F32)] * count],
        [((rows, PAD, width), BF16), ((rows, PAD, width), BF16), acc, (3,), (rows,)], SMALL,
    )
    rx1 = exchange(msg1)
    low1, hidden_hbm, hidden, st2, msg2, og, w2 = call(
        first_half_kernel, "svvvvvhh" + "hhvvvvv", (lengths, tok, st1, rx1, affine1, w1, out_grad, kernel2),
        [own, hid, hid, sums, msg, own, kernel],
        [[((padded, width), BF16)] * rows, products, tab, acc, (2,), (2 * rows,)], SMALL, flops,
    )
    rx2 = exchange([msg2] * count)
    gs2, grad_low2, bias_part = call(
        branch_grad_kernel, "svvv" + "vvv", (lengths, og, rx1, w2), [taps, wide, ((8, width), F32)],
        [buf, [((padded, width), BF16)] * 2, products, ((2, 8, width), F32)], SMALL, flops,
    )
    low2, low2_hbm, da2, gst2, msg3 = call(
        second_norm_kernel, "svvvvv" + "vhhvv", (lengths, hidden, grad_low2, st2, rx2, affine2),
        [wide, wide, wide, sums, msg], [wide, tab, acc, (2 * rows,)], SMALL,
    )
    rx3 = exchange([msg3] * count)

    def kernel_grad(own_half, first_frame, low, gs):
        return call(
            functools.partial(kernel_grad_kernel, own_half, first_frame), "vvv", (low, gs), [half],
            [((width // 2, 3 * width), F32)], SMALL, flops // 2,
        )[0]

    send2 = kernel_grad(False, PAD, low2, gs2)
    got2 = swap(send2, "core", 1)
    keep2 = kernel_grad(True, PAD, low2, after(gs2, send2))
    half2 = (got2.astype(F32) + after(keep2, *rx3).astype(F32)).astype(BF16)
    part2 = scatter_sum(half2.reshape(chips, -1, width), "chip")

    grad_hidden, send1, keep1, affine_part2 = call(
        hidden_grad_kernel, "shhhvvvvv" + "hvvv",
        (lengths, low1, after(da2, half2), hidden_hbm, st2, rx2, gst2, rx3, affine2),
        [wide, half, half, ((4 * rows, 2 * width), F32)],
        [own, wide, hid, wide, buf, [((frames, 3 * width), BF16)] * 2, tab, ((width, 3 * width), F32), (3 * rows,), (rows,)],
        LARGE, flops,
    )
    got1 = swap(after(send1, part2), "core", 1)
    half1 = (got1.astype(F32) + keep1.astype(F32)).astype(BF16)
    part1 = scatter_sum(half1.reshape(chips, -1, width), "chip")

    da1, gst1, last_part = call(
        first_norm_grad_kernel, "shhhvvvvv" + "hvv",
        (lengths, after(grad_hidden, half1), kernel1, tokens, st1, rx1, affine1, affine_part2, bias_part),
        [own, sums, ((4 * rows, 4 * width), BF16)],
        [wide, kernel, own, own, products, ((frames, width), F32), tab, acc, ((4 * rows, 4 * width), F32), (1 + 2 * rows,),
         (rows,)],
        LARGE, flops,
    )
    both = jnp.concatenate([part2.reshape(count, -1, width), part1.reshape(count, -1, width)], axis=1)
    both = after(both, da1)
    last_part = after(last_part, both)
    both = scatter_sum(both, "tm")
    (block_out,) = call(
        block_out_kernel, "shhhv" + "h", (lengths, low2_hbm, after(tokens, both), kernel2, conv2_bias.reshape(1, width)), [own],
        [wide, own, kernel, products, own, (1 + 2 * rows,), (rows,)], LARGE, flops,
    )
    last = sum_over_tm(last_part)
    affine_grads = after(last, both).astype(BF16)
    both = spread(both, "tm")
    (input_grad,) = call(
        input_grad_kernel, "shhhvvvvv" + "h", (lengths, out_grad, after(da1, both), tokens, st1, rx1, gst1, last, affine1), [own],
        [own, own, own, tab, own, (3 * rows,), (rows,)], LARGE,
    )
    mine = affine_grads.reshape(rows, 4, 4 * width)[:, :SEGS].reshape(rows * SEGS, 4 * width)
    style_grad = lax.dot_general(
        mine[:, : 2 * width], fc1_weight, (((1,), (1,)), ((), ())), preferred_element_type=F32
    ) + lax.dot_general(mine[:, 2 * width :], fc2_weight, (((1,), (1,)), ((), ())), preferred_element_type=F32)
    style_grad = style_grad.reshape(style.shape)
    style_pad = jnp.pad(style, ((0, 0), (0, 1), (0, 0))).reshape(rows * 4, -1)
    gathered = gather_rows(jnp.concatenate([affine_grads, style_pad], axis=1))
    both = spread(after(both, block_out, gathered), "chip")
    fc_shape, bias_shape = ((style.shape[2], 2 * width), F32), ((1, 2 * width), F32)
    fc1_grad, fc2_grad, fc1_bias_grad, fc2_bias_grad, conv2_bias_grad = call(
        projection_grad_kernel, "v" + "hhvvv", (gathered,), [fc_shape, fc_shape, bias_shape, bias_shape, ((1, width), F32)],
        [(gathered.shape, BF16), ((style.shape[2], 4 * width), F32), (2,)], SMALL,
    )
    fc1_bias_grad, fc2_bias_grad, conv2_bias_grad = (
        b.reshape(b.shape[1]) for b in (fc1_bias_grad, fc2_bias_grad, conv2_bias_grad)
    )

    both = both.reshape(chips, count, 2, -1, width)
    both, input_grad, *small = lax.optimization_barrier(
        (both, input_grad, style_grad, fc1_grad, fc2_grad, fc1_bias_grad, fc2_bias_grad, conv2_bias_grad)
    )
    style_grad, fc1_grad, fc2_grad, fc1_bias_grad, fc2_bias_grad, conv2_bias_grad = small
    other = swap(both, "core", 1)
    if both.shape[3] % PAD == 0:
        conv_shape = ((3, width, width), F32)
        conv2_sum, conv1_sum = call(
            assemble_kernel, "vv" + "hh", (both, other), [conv_shape, conv_shape], [((2, 3, width, width), F32), (2,)], SMALL,
        )
    else:
        first = lax.axis_index("core") == 0
        halves = [jnp.where(first, both, other), jnp.where(first, other, both)]
        halves = [jnp.moveaxis(h, 2, 0).reshape(2, 3, width // 2, width) for h in halves]
        conv2_sum, conv1_sum = jnp.concatenate(halves, axis=2).astype(F32)
    return (
        block_out, input_grad, style_grad, fc1_grad, fc1_bias_grad, conv1_sum, fc2_grad, fc2_bias_grad, conv2_sum,
        conv2_bias_grad,
    )


def solution(mesh):
    chips = mesh.shape["dp"] // 2
    mesh = Mesh(mesh.devices.reshape(chips, 2, mesh.shape["tm"]), ("chip", "core", "tm"))
    dp = ("chip", "core")
    return jax.shard_map(
        per_device,
        mesh=mesh,
        in_specs=(
            P(dp, "tm", None),
            P(dp, None),
            P(dp, None, None),
            P(),
            P(),
            P(),
            P(),
            P(),
            P(),
            P(),
            P(dp, "tm", None),
        ),
        out_specs=(
            P(dp, "tm", None),
            P(dp, "tm", None),
            P(dp, None, None),
            P(),
            P(),
            P(),
            P(),
            P(),
            P(),
            P(),
        ),
        check_vma=False,
    )
```

```python
import functools

import jax
import jax.numpy as jnp
from jax import lax
from jax.experimental import pallas as pl
from jax.experimental.pallas import tpu as pltpu
from jax.sharding import Mesh, PartitionSpec as P

EPSILON = 1e-05
ROOT_HALF = 0.7071067811865476
SEGS = 3
PAD = 16
CHUNK = 32
EDGE = 8 + 16
F32 = jnp.float32
BF16 = jnp.bfloat16
SMALL, LARGE = 20, 30


class Row:
    def __init__(self, len_ref, r, frames):
        self.frames = frames
        self.z = lax.axis_index("tm")
        self.counts = [len_ref[r, s] for s in range(SEGS)]
        l0, l1, l2 = self.counts
        start = -self.z * frames
        e0 = start + l0
        e1 = e0 + l1
        e2 = e1 + l2
        self.begins = [start, e0, e1]
        self.ends = [e0, e1, e2]
        self.long_at = jnp.where(l0 >= jnp.maximum(l1, l2), 0, jnp.where(l1 >= l2, 1, 2))
        self.long_begin = self.of_long(self.begins)
        self.long_end = self.of_long(self.ends)

    def of_long(self, values):
        return jnp.where(
            self.long_at == 0, values[0], jnp.where(self.long_at == 1, values[1], values[2])
        )

    def segment(self, t):
        return sum((t >= e).astype(jnp.int32) for e in self.ends)

    def chunks(self, uniform_fn, mixed_fn, sums=None, acc_ref=None, ends=None):
        for t0 in range(0, self.frames, CHUNK):
            uniform_fn(t0, self.segment(t0))
        if sums is not None:
            sums.put(acc_ref)
        self.mixed(mixed_fn, ends)

    def mixed(self, fn, ends=None):
        for end in ends or self.ends:

            @pl.when(jnp.logical_and(jnp.logical_and(end > 0, end < self.frames), end % CHUNK != 0))
            def _(end=end):
                fn(pl.multiple_of((end // CHUNK) * CHUNK, CHUNK))


def frame_ids(t0, rows, width):
    return t0 + lax.broadcasted_iota(jnp.int32, (rows, width), 0)


def pick(tab_ref, base, t, row):
    value = tab_ref[base, 0:1, :]
    for s in range(SEGS):
        value = jnp.where(t >= row.ends[s], tab_ref[base + s + 1, 0:1, :], value)
    return value


def entry(tab_ref, index, rows=CHUNK):
    value = tab_ref[index]
    return jnp.broadcast_to(value[None], (rows // 8, *value.shape)).reshape(rows, value.shape[1])


def put_entry(tab_ref, index, value):
    tab_ref[index] = jnp.broadcast_to(value, tab_ref.shape[1:])


def put_table(tab_ref, base, values):
    for s in range(SEGS):
        put_entry(tab_ref, base + s, values[s])
    put_entry(tab_ref, base + SEGS, jnp.zeros_like(values[0]))


def fold(x):
    return jnp.sum(x.reshape(x.shape[0] // 8, 8, x.shape[1]), axis=0)


def add_masked_sums(acc_ref, t, row, first, second):
    for s in range(SEGS):
        inside = jnp.logical_and(t >= row.begins[s], t < row.ends[s])
        acc_ref[s] += fold(jnp.where(inside, first, 0.0))
        acc_ref[4 + s] += fold(jnp.where(inside, second, 0.0))


def put_sums(acc_ref, st_ref, msg_refs, row, r):
    for s in range(SEGS):
        for k in range(2):
            st_ref[r, pl.ds(SEGS * k + s, 1), :] = jnp.sum(acc_ref[4 * k + s], axis=0, keepdims=True)
    for k in range(2):
        value = jnp.sum(acc_ref[4 * k + row.long_at], axis=0, keepdims=True)
        for ref in msg_refs:
            ref[pl.ds(2 * r + k, 1), :] = value


def sums_of(row, r, st_ref, rx_refs, s):
    out = []
    for k in range(2):
        total = sum(ref[pl.ds(2 * r + k, 1), :] for ref in rx_refs)
        local = st_ref[r, SEGS * k + s : SEGS * k + s + 1, :]
        out.append(jnp.where(row.long_at == s, total, local))
    return out


def norm_of(row, r, st_ref, rx_ref, aff_ref, s):
    width = st_ref.shape[2]
    first, second = sums_of(row, r, st_ref, rx_ref, s)
    count = jnp.full((1, width), row.counts[s].astype(F32))
    mean = first / count
    rstd = lax.rsqrt(second / count - mean * mean + EPSILON)
    affine = aff_ref[r, s : s + 1, :]
    return mean, rstd, 1.0 + affine[:, :width], affine[:, width:], count


def put_forward(row, r, st_ref, rx_ref, aff_ref, tab_ref):
    scales, shifts = [], []
    for s in range(SEGS):
        mean, rstd, gain, beta, _ = norm_of(row, r, st_ref, rx_ref, aff_ref, s)
        scales.append(gain * rstd)
        shifts.append(beta - mean * scales[-1])
    put_table(tab_ref, 0, scales)
    put_table(tab_ref, 4, shifts)
    put_entry(tab_ref, 12, row.of_long(scales))
    put_entry(tab_ref, 13, row.of_long(shifts))


def put_backward(row, r, st_ref, rx_ref, gst_ref, grx_ref, aff_ref, tab_ref):
    parts = [[], [], []]
    for s in range(SEGS):
        mean, rstd, gain, _, count = norm_of(row, r, st_ref, rx_ref, aff_ref, s)
        if isinstance(grx_ref, (list, tuple)):
            shift, scale = sums_of(row, r, gst_ref, grx_ref, s)
            scale = rstd * (scale - mean * shift)
        else:
            width = mean.shape[1]
            total = grx_ref[pl.ds(4 * r + s, 1), : 2 * width] + grx_ref[pl.ds(4 * r + SEGS, 1), 2 * width :]
            shift, local = gst_ref[r, s : s + 1, :], gst_ref[r, SEGS + s : SEGS + s + 1, :]
            scale = jnp.where(row.long_at == s, total[:, :width], rstd * (local - mean * shift))
            shift = jnp.where(row.long_at == s, total[:, width:], shift)
        mean_g = gain * shift / count
        slope = rstd * rstd * (gain * scale / count)
        parts[0].append(gain * rstd)
        parts[1].append(-slope)
        parts[2].append(slope * mean - rstd * mean_g)
    for k in range(3):
        put_table(tab_ref, 4 * k, parts[k])
        put_entry(tab_ref, 12 + k, row.of_long(parts[k]))


def put_affine_grads(row, r, st_ref, rx_ref, gst_ref, aff_ref, out_ref, at):
    width = st_ref.shape[2]
    for s in range(SEGS):
        mean, rstd, _, _, _ = norm_of(row, r, st_ref, rx_ref, aff_ref, s)
        shift = gst_ref[r, s : s + 1, :]
        scale = rstd * (gst_ref[r, SEGS + s : SEGS + s + 1, :] - mean * shift)
        out_ref[pl.ds(4 * r + s, 1), at : at + width] = scale
        out_ref[pl.ds(4 * r + s, 1), at + width : at + 2 * width] = shift


def silu(a):
    half = 0.5 * a
    return half + half * jnp.tanh(half)


def silu_and_slope(a):
    gate = 0.5 + 0.5 * jnp.tanh(0.5 * a)
    low = a * gate
    return low, gate + low * (1.0 - gate)


def halo_tile(row, frames, width, left):
    t = frame_ids(-PAD if left else frames, PAD, width)
    near = jnp.logical_and(t >= -2, t < frames + 2)
    inside = jnp.logical_and(t >= row.long_begin, t < row.long_end)
    return t, jnp.logical_and(near, inside)


def edge_tile(rx_refs, row, r, t, at, left):
    last = len(rx_refs) - 1
    neighbour = jnp.maximum(row.z - 1, 0) if left else jnp.minimum(row.z + 1, last)
    edges = []
    for i in range(2):
        value, k = rx_refs[1][pl.ds(8 + 4 * r + at + i, 1), :], 3
        while k <= last:
            value = jnp.where((row.z ^ neighbour) == k, rx_refs[k][pl.ds(8 + 4 * r + at + i, 1), :], value)
            k = 2 * k + 1
        edges.append(value)
    second = -1 if left else row.frames + 1
    return jnp.where(t == second, edges[1], edges[0])


def stack_taps(buf_ref, xs_ref, row, frames, forward, halo, low_ref=None, r=None):
    width = buf_ref.shape[1]
    before_at, after_at = (0, 2 * width) if forward else (2 * width, 0)
    base = PAD if halo else 0
    for i in range(frames // CHUNK):
        o, d = PAD + i * CHUNK, base + i * CHUNK
        centre = buf_ref[o : o + CHUNK, :].astype(BF16)
        xs_ref[d : d + CHUNK, width : 2 * width] = centre
        xs_ref[d : d + CHUNK, before_at : before_at + width] = buf_ref[o - 1 : o - 1 + CHUNK, :].astype(BF16)
        xs_ref[d : d + CHUNK, after_at : after_at + width] = buf_ref[o + 1 : o + 1 + CHUNK, :].astype(BF16)
        if low_ref is not None:
            low_ref[r, i * CHUNK : (i + 1) * CHUNK, :] = centre
    if halo:
        end = PAD + frames
        left, right = buf_ref[0:PAD, :], buf_ref[end : end + PAD, :]
        xs_ref[0:PAD, width : 2 * width] = left.astype(BF16)
        xs_ref[end : end + PAD, width : 2 * width] = right.astype(BF16)
        xs_ref[0:PAD, before_at : before_at + width] = pltpu.roll(left, 1, 0).astype(BF16)
        xs_ref[end : end + PAD, before_at : before_at + width] = buf_ref[end - 1 : end - 1 + PAD, :].astype(BF16)
        xs_ref[0:PAD, after_at : after_at + width] = buf_ref[1 : 1 + PAD, :].astype(BF16)
        xs_ref[end : end + PAD, after_at : after_at + width] = pltpu.roll(right, PAD - 1, 0).astype(BF16)
    for end in row.ends[:2]:
        for at, t in ((before_at, end), (after_at, end - 1)):

            @pl.when(jnp.logical_and(t >= 0, t < frames))
            def _(at=at, t=t):
                tile = pl.multiple_of((t // PAD) * PAD, PAD)
                rows = pl.ds(base + tile, PAD)
                value = xs_ref[rows, at : at + width].astype(F32)
                keep = frame_ids(tile, PAD, width) != t
                xs_ref[rows, at : at + width] = jnp.where(keep, value, 0.0).astype(BF16)


class Sums:
    def __init__(self, row, width):
        self.row = row
        self.parts = [[jnp.zeros((8, width), F32)] * SEGS for _ in range(2)]

    def add(self, t0, rows, first, second):
        folded = (fold(first), fold(second))
        for s in range(SEGS):
            fills = jnp.logical_and(t0 >= self.row.begins[s], t0 + rows <= self.row.ends[s])
            weight = jnp.where(fills, 1.0, 0.0)
            for k in range(2):
                self.parts[k][s] = self.parts[k][s] + folded[k] * weight

    def put(self, acc_ref):
        for k in range(2):
            for s in range(SEGS):
                acc_ref[4 * k + s] = self.parts[k][s]


def rows_moved(ref, at, rows, step):
    if at - step < 0 or at + rows - step > ref.shape[0]:
        return pltpu.roll(ref[at : at + rows, :], step % rows, 0)
    return ref[at - step : at - step + rows, :]


def tap_sum(z_ref, row, t0, rows, first=0, last=2):
    at, t = PAD + t0, frame_ids(t0, rows, z_ref.shape[2])
    starts = functools.reduce(jnp.logical_or, [t == end for end in row.ends])
    stops = functools.reduce(jnp.logical_or, [t == end - 1 for end in row.ends])
    before = jnp.where(starts, 0.0, rows_moved(z_ref.at[first], at, rows, 1))
    after = jnp.where(stops, 0.0, rows_moved(z_ref.at[last], at, rows, -1))
    return before + z_ref[1, at : at + rows, :] + after


def put_products(x, w_ref, z_ref, transposed=False):
    width = x.shape[1]
    dims = (((1,), (1 if transposed else 0,)), ((), ()))
    for k in range(3):
        tap = w_ref[k * width : (k + 1) * width, :]
        z_ref[k] = lax.dot_general(x, tap, dims, preferred_element_type=F32)


def times_transposed(xs, w_ref, width):
    out = None
    for k in range(3):
        part = lax.dot_general(
            xs[:, k * width : (k + 1) * width],
            w_ref[k * width : (k + 1) * width, :],
            (((1,), (1,)), ((), ())),
            preferred_element_type=F32,
        )
        out = part if out is None else out + part
    return out


def for_rows(len_ref, rows, frames, body):
    def step(r, carry):
        body(r, Row(len_ref, r, frames))
        return carry

    lax.fori_loop(0, rows, step, 0)


def token_sums_kernel(len_ref, tok_hbm, og_hbm, w_hbm, tok_ref, w_ref, st_ref, msg_refs, head_ref, tail_ref, acc_ref,
                      sems, row_sems):
    rows, frames, width = tok_ref.shape

    def row_copy(r):
        return pltpu.make_async_copy(tok_hbm.at[r], tok_ref.at[r], row_sems.at[r])

    for r in range(rows):
        row_copy(r).start()
    edges = (
        pltpu.make_async_copy(og_hbm.at[:, pl.ds(0, PAD), :], head_ref, sems.at[0]),
        pltpu.make_async_copy(og_hbm.at[:, pl.ds(frames - PAD, PAD), :], tail_ref, sems.at[1]),
    )
    for copy in edges:
        copy.start()
    kernel_copy = pltpu.make_async_copy(w_hbm, w_ref, sems.at[2])
    kernel_copy.start()
    for copy in edges:
        copy.wait()

    def body(r, row):
        row_copy(r).wait()
        sums = Sums(row, width)

        def uniform(t0, s):
            v = tok_ref[r, pl.ds(t0, CHUNK), :].astype(F32)
            sums.add(t0, CHUNK, v, v * v)

        def mixed(t0):
            v = tok_ref[r, pl.ds(t0, CHUNK), :].astype(F32)
            add_masked_sums(acc_ref, frame_ids(t0, CHUNK, width), row, v, v * v)

        row.chunks(uniform, mixed, sums, acc_ref)
        put_sums(acc_ref, st_ref, msg_refs, row, r)
        for j, (head, tail) in enumerate(
            ((tok_ref[r, 0:PAD, :], tok_ref[r, frames - PAD : frames, :]), (head_ref[r], tail_ref[r]))
        ):
            first, last = head.astype(F32), tail.astype(F32)
            for i in range(2):
                to_left, to_right = first[i : i + 1, :], last[PAD - 2 + i : PAD - 1 + i, :]
                for k, ref in enumerate(msg_refs):
                    value = jnp.where(row.z < row.z ^ k, to_right, to_left)
                    ref[pl.ds(8 + 4 * r + 2 * j + i, 1), :] = value

    for_rows(len_ref, rows, frames, body)
    kernel_copy.wait()


def first_half_kernel(len_ref, tok_ref, st_ref, rx_ref, aff_ref, w_ref, og_hbm, w2_hbm, low_ref,
                      hid_ref, st2_ref, msg_ref, og_ref, w2_ref, z_ref, tab_ref, acc_ref, sems):
    rows, frames, width = tok_ref.shape
    copies = (
        pltpu.make_async_copy(og_hbm, og_ref, sems.at[0]),
        pltpu.make_async_copy(w2_hbm, w2_ref, sems.at[1]),
    )
    for copy in copies:
        copy.start()

    def body(r, row):
        put_forward(row, r, st_ref, rx_ref, aff_ref, tab_ref)

        def uniform(t0, s):
            v = tok_ref[r, pl.ds(t0, CHUNK), :].astype(F32)
            low = silu(v * entry(tab_ref, s) + entry(tab_ref, 4 + s))
            low_ref[r, pl.ds(PAD + t0, CHUNK), :] = low.astype(BF16)

        def mixed(t0):
            t = frame_ids(t0, CHUNK, width)
            v = tok_ref[r, pl.ds(t0, CHUNK), :].astype(F32)
            low = silu(v * pick(tab_ref, 0, t, row) + pick(tab_ref, 4, t, row))
            low_ref[r, pl.ds(PAD + t0, CHUNK), :] = jnp.where(t < row.ends[2], low, 0.0).astype(BF16)

        row.chunks(uniform, mixed)
        for left in (True, False):
            t, valid = halo_tile(row, frames, width, left)
            low = silu(edge_tile(rx_ref, row, r, t, 0, left) * tab_ref[12, 0:1, :] + tab_ref[13, 0:1, :])
            at = 0 if left else PAD + frames
            low_ref[r, at : at + PAD, :] = jnp.where(valid, low, 0.0).astype(BF16)
        put_products(low_ref[r], w_ref, z_ref)
        sums = Sums(row, width)
        for t0 in range(0, frames, CHUNK):
            v = tap_sum(z_ref, row, t0, CHUNK)
            hid_ref[r, PAD + t0 : PAD + t0 + CHUNK, :] = v
            sums.add(t0, CHUNK, v, v * v)
        sums.put(acc_ref)
        for t0 in (-PAD, frames):
            hid_ref[r, PAD + t0 : 2 * PAD + t0, :] = tap_sum(z_ref, row, t0, PAD)

        def mixed_sums(t0):
            v = hid_ref[r, pl.ds(PAD + t0, CHUNK), :]
            add_masked_sums(acc_ref, frame_ids(t0, CHUNK, width), row, v, v * v)

        row.mixed(mixed_sums)
        put_sums(acc_ref, st2_ref, [msg_ref], row, r)

    for_rows(len_ref, rows, frames, body)
    for copy in copies:
        copy.wait()


def branch_grad_kernel(len_ref, og_ref, rx_ref, w_ref, low_ref, hid_ref, gs_ref, q_ref, bias_ref, low_hbm, hid_hbm,
                       buf_ref, xs_ref, sems):
    rows, frames, width = og_ref.shape
    stores = (
        pltpu.make_async_copy(low_ref, low_hbm, sems.at[0]),
        pltpu.make_async_copy(hid_ref, hid_hbm, sems.at[1]),
    )
    for copy in stores:
        copy.start()
    bias_ref[...] = jnp.zeros_like(bias_ref)

    def body(r, row):
        def put(t0, g, weight):
            g = g.astype(BF16).astype(F32)
            buf_ref[pl.ds(PAD + t0, CHUNK), :] = g
            bias_ref[...] += fold(g) * weight

        def uniform(t0, s):
            scale = jnp.where(s < SEGS, ROOT_HALF, 0.0)
            g = og_ref[r, pl.ds(t0, CHUNK), :].astype(F32) * scale
            put(t0, g, jnp.where(t0 + CHUNK <= row.ends[2], 1.0, 0.0))

        def mixed(t0):
            t = frame_ids(t0, CHUNK, width)
            g = og_ref[r, pl.ds(t0, CHUNK), :].astype(F32) * ROOT_HALF
            put(t0, jnp.where(t < row.ends[2], g, 0.0), 1.0)

        row.chunks(uniform, mixed, ends=row.ends[2:])
        for left in (True, False):
            t, valid = halo_tile(row, frames, width, left)
            at = 0 if left else PAD + frames
            g = edge_tile(rx_ref, row, r, t, 2, left) * ROOT_HALF
            buf_ref[at : at + PAD, :] = jnp.where(valid, g, 0.0)
        stack_taps(buf_ref, xs_ref, row, frames, False, True)
        gs_ref[r] = xs_ref[PAD : PAD + frames, :]
        q_ref[r] = times_transposed(xs_ref[...], w_ref, width).astype(BF16)

    for_rows(len_ref, rows, frames, body)
    for copy in stores:
        copy.wait()


def second_norm_kernel(len_ref, hid_ref, q_ref, st_ref, rx_ref, aff_ref, low_ref, da_ref, gst_ref, msg_ref,
                       tab_ref, acc_ref):
    rows, padded, width = hid_ref.shape
    frames = padded - 2 * PAD

    def body(r, row):
        put_forward(row, r, st_ref, rx_ref, aff_ref, tab_ref)
        sums = Sums(row, width)

        def uniform(t0, s):
            at = pl.ds(PAD + t0, CHUNK)
            v = hid_ref[r, at, :]
            low, slope = silu_and_slope(v * entry(tab_ref, s) + entry(tab_ref, 4 + s))
            da = slope * q_ref[r, at, :].astype(F32)
            low_ref[r, at, :] = low.astype(BF16)
            da_ref[r, at, :] = da.astype(BF16)
            sums.add(t0, CHUNK, da, da * v)

        def mixed(t0):
            at = pl.ds(PAD + t0, CHUNK)
            t = frame_ids(t0, CHUNK, width)
            live = t < row.ends[2]
            v = hid_ref[r, at, :]
            low, slope = silu_and_slope(v * pick(tab_ref, 0, t, row) + pick(tab_ref, 4, t, row))
            da = slope * q_ref[r, at, :].astype(F32)
            low_ref[r, at, :] = jnp.where(live, low, 0.0).astype(BF16)
            da_ref[r, at, :] = jnp.where(live, da, 0.0).astype(BF16)
            add_masked_sums(acc_ref, t, row, da, da * v)

        row.chunks(uniform, mixed, sums, acc_ref)
        for left in (True, False):
            t, valid = halo_tile(row, frames, width, left)
            at = 0 if left else PAD + frames
            v = hid_ref[r, at : at + PAD, :]
            low, slope = silu_and_slope(v * tab_ref[12, 0:1, :] + tab_ref[13, 0:1, :])
            da = slope * q_ref[r, at : at + PAD, :].astype(F32)
            low_ref[r, at : at + PAD, :] = jnp.where(valid, low, 0.0).astype(BF16)
            da_ref[r, at : at + PAD, :] = jnp.where(valid, da, 0.0).astype(BF16)
        put_sums(acc_ref, gst_ref, [msg_ref], row, r)

    for_rows(len_ref, rows, frames, body)


class Loads:
    def __init__(self, rows, sems, whole, by_row):
        count = len(whole)
        self.whole = [pltpu.make_async_copy(a, b, sems.at[i]) for i, (a, b) in enumerate(whole)]
        self.row = lambda r: [
            pltpu.make_async_copy(a.at[r], b.at[r], sems.at[count + i * rows + r]) for i, (a, b) in enumerate(by_row)
        ]
        for copy in (*self.row(0), *self.whole):
            copy.start()
        for r in range(1, rows):
            for copy in self.row(r):
                copy.start()

    def wait(self, r):
        for copy in self.row(r):
            copy.wait()

        @pl.when(r == 0)
        def _():
            for copy in self.whole:
                copy.wait()


def block_out_kernel(len_ref, low_hbm, tok_hbm, w_hbm, bias_ref, out_hbm, low_ref, tok_ref, w_ref, z_ref, out_ref,
                     sems, row_sems):
    rows, frames, width = tok_ref.shape
    loads = Loads(rows, sems, [(w_hbm, w_ref)], [(low_hbm, low_ref), (tok_hbm, tok_ref)])

    def row_copy(r):
        return pltpu.make_async_copy(out_ref.at[r], out_hbm.at[r], row_sems.at[r])

    def body(r, row):
        loads.wait(r)
        bias = bias_ref[...].astype(F32)
        put_products(low_ref[r], w_ref, z_ref)
        for t0 in range(0, frames, CHUNK):
            live = frame_ids(t0, CHUNK, width) < row.ends[2]
            branch = tap_sum(z_ref, row, t0, CHUNK) + jnp.where(live, bias, 0.0)
            out = (tok_ref[r, t0 : t0 + CHUNK, :].astype(F32) + branch) * ROOT_HALF
            out_ref[r, t0 : t0 + CHUNK, :] = out.astype(BF16)
        row_copy(r).start()

    for_rows(len_ref, rows, frames, body)
    for r in range(rows):
        row_copy(r).wait()


def half_of_grad(low_ref, gs_ref, r, half, first_frame):
    frames, width = gs_ref.shape[1], low_ref.shape[2] // 2
    u = low_ref[r, first_frame : first_frame + frames, pl.ds(pl.multiple_of(half * width, width), width)]
    return lax.dot_general(u, gs_ref[r], (((0,), (0,)), ((), ())), preferred_element_type=F32)


def put_half(acc_ref, out_ref):
    half, width = acc_ref.shape[0], acc_ref.shape[1] // 3
    for k in range(3):
        out_ref[k * half : (k + 1) * half, :] = acc_ref[:, k * width : (k + 1) * width].astype(BF16)


def kernel_grad_kernel(own, first_frame, low_ref, gs_ref, kept_ref, out_ref, kept_hbm, acc_ref, sems):
    store = pltpu.make_async_copy(kept_ref, kept_hbm, sems.at[0])
    store.start()
    core = lax.axis_index("core")
    half = core if own else 1 - core
    acc_ref[...] = half_of_grad(low_ref, gs_ref, 0, half, first_frame)

    def step(r, carry):
        acc_ref[...] += half_of_grad(low_ref, gs_ref, r, half, first_frame)
        return carry

    lax.fori_loop(1, low_ref.shape[0], step, 0)
    put_half(acc_ref, out_ref)
    store.wait()


def hidden_grad_kernel(len_ref, low_hbm, da_hbm, hid_hbm, st_ref, rx_ref, gst_ref, grx_ref, aff_ref,
                       g_hbm, send_ref, keep_ref, part_ref, low_ref, da_ref, hid_ref, g_ref, gs_ref, buf_ref, tab_ref, acc_ref,
                       sems, row_sems):
    rows, frames, width = low_ref.shape[0], gs_ref.shape[0], low_ref.shape[2]
    loads = Loads(rows, sems, [], [(da_hbm, da_ref), (hid_hbm, hid_ref), (low_hbm, low_ref)])
    part_ref[...] = jnp.zeros_like(part_ref)
    acc_ref[...] = jnp.zeros_like(acc_ref)

    def row_copy(r):
        return pltpu.make_async_copy(g_ref.at[r], g_hbm.at[r], row_sems.at[r])

    def body(r, row):
        put_affine_grads(row, r, st_ref, rx_ref, gst_ref, aff_ref, part_ref, 0)
        put_backward(row, r, st_ref, rx_ref, gst_ref, grx_ref, aff_ref, tab_ref)
        loads.wait(r)

        def uniform(t0, s):
            at = pl.ds(PAD + t0, CHUNK)
            buf_ref[at, :] = (
                da_ref[r, at, :].astype(F32) * entry(tab_ref, s)
                + hid_ref[r, at, :] * entry(tab_ref, 4 + s)
                + entry(tab_ref, 8 + s)
            )

        def mixed(t0):
            at = pl.ds(PAD + t0, CHUNK)
            t = frame_ids(t0, CHUNK, width)
            grad = (
                da_ref[r, at, :].astype(F32) * pick(tab_ref, 0, t, row)
                + hid_ref[r, at, :] * pick(tab_ref, 4, t, row)
                + pick(tab_ref, 8, t, row)
            )
            buf_ref[at, :] = jnp.where(t < row.ends[2], grad, 0.0)

        row.chunks(uniform, mixed)
        for left in (True, False):
            t, valid = halo_tile(row, frames, width, left)
            at = 0 if left else PAD + frames
            grad = (
                da_ref[r, at : at + PAD, :].astype(F32) * tab_ref[12, 0:1, :]
                + hid_ref[r, at : at + PAD, :] * tab_ref[13, 0:1, :]
                + tab_ref[14, 0:1, :]
            )
            buf_ref[at : at + PAD, :] = jnp.where(valid, grad, 0.0)
        g_ref[r] = buf_ref[...].astype(BF16)
        stack_taps(buf_ref, gs_ref, row, frames, False, False)
        row_copy(r).start()
        acc_ref[...] += lax.dot_general(
            low_ref[r, PAD : PAD + frames, :], gs_ref[...], (((0,), (0,)), ((), ())), preferred_element_type=F32
        )

    for_rows(len_ref, rows, frames, body)
    core, half = lax.axis_index("core"), width // 2
    for ref, which in ((send_ref, 1 - core), (keep_ref, core)):
        put_half(acc_ref.at[pl.ds(pl.multiple_of(which * half, half), half), :], ref)
    for r in range(rows):
        row_copy(r).wait()


def first_norm_grad_kernel(len_ref, g_hbm, w_hbm, tok_hbm, st_ref, rx_ref, aff_ref, part2_ref, bias_ref,
                           da_hbm, gst_ref, out_ref, g_ref, w_ref, tok_ref, da_ref, q_ref, z_ref, tab_ref, acc_ref,
                           part_ref, sems, row_sems):
    rows, frames, width = tok_ref.shape
    loads = Loads(rows, sems, [(w_hbm, w_ref)], [(g_hbm, g_ref), (tok_hbm, tok_ref)])
    part_ref[:, : 2 * width] = jnp.zeros((part_ref.shape[0], 2 * width), F32)
    part_ref[:, 2 * width :] = part2_ref[...]
    part_ref[SEGS : SEGS + 1, :width] = jnp.sum(bias_ref[...], axis=0, keepdims=True)

    def row_copy(r):
        return pltpu.make_async_copy(da_ref.at[r], da_hbm.at[r], row_sems.at[r])

    def body(r, row):
        put_forward(row, r, st_ref, rx_ref, aff_ref, tab_ref)
        loads.wait(r)
        put_products(g_ref[r], w_ref, z_ref, True)
        for t0 in range(0, frames, CHUNK):
            q_ref[t0 : t0 + CHUNK, :] = tap_sum(z_ref, row, t0, CHUNK, 2, 0)
        sums = Sums(row, width)

        def uniform(t0, s):
            at = pl.ds(t0, CHUNK)
            v = tok_ref[r, at, :].astype(F32)
            _, slope = silu_and_slope(v * entry(tab_ref, s) + entry(tab_ref, 4 + s))
            da = slope * q_ref[at, :]
            da_ref[r, at, :] = da.astype(BF16)
            sums.add(t0, CHUNK, da, da * v)

        def mixed(t0):
            at = pl.ds(t0, CHUNK)
            t = frame_ids(t0, CHUNK, width)
            v = tok_ref[r, at, :].astype(F32)
            _, slope = silu_and_slope(v * pick(tab_ref, 0, t, row) + pick(tab_ref, 4, t, row))
            da = slope * q_ref[at, :]
            da_ref[r, at, :] = jnp.where(t < row.ends[2], da, 0.0).astype(BF16)
            add_masked_sums(acc_ref, t, row, da, da * v)

        row.chunks(uniform, mixed, sums, acc_ref)
        row_copy(r).start()
        put_sums(acc_ref, gst_ref, [], row, r)
        put_affine_grads(row, r, st_ref, rx_ref, gst_ref, aff_ref, part_ref, 0)
        value = part_ref[pl.ds(4 * r + row.long_at, 1), : 2 * width]
        part_ref[pl.ds(4 * r + SEGS, 1), 2 * width :] = value - value.astype(BF16).astype(F32)

    for_rows(len_ref, rows, frames, body)
    out_ref[...] = part_ref[...].astype(BF16)
    for r in range(rows):
        row_copy(r).wait()


def input_grad_kernel(len_ref, og_hbm, da_hbm, tok_hbm, st_ref, rx_ref, gst_ref, grx_ref, aff_ref, out_hbm,
                      og_ref, da_ref, tok_ref, tab_ref, out_ref, sems, row_sems):
    rows, frames, width = tok_ref.shape
    loads = Loads(rows, sems, [], [(og_hbm, og_ref), (da_hbm, da_ref), (tok_hbm, tok_ref)])

    def row_copy(r):
        return pltpu.make_async_copy(out_ref.at[r], out_hbm.at[r], row_sems.at[r])

    def body(r, row):
        put_backward(row, r, st_ref, rx_ref, gst_ref, grx_ref, aff_ref, tab_ref)
        loads.wait(r)

        def uniform(t0, s):
            at = pl.ds(t0, CHUNK)
            out = (
                og_ref[r, at, :].astype(F32) * ROOT_HALF
                + da_ref[r, at, :].astype(F32) * entry(tab_ref, s)
                + tok_ref[r, at, :].astype(F32) * entry(tab_ref, 4 + s)
                + entry(tab_ref, 8 + s)
            )
            out_ref[r, at, :] = out.astype(BF16)

        def mixed(t0):
            at = pl.ds(t0, CHUNK)
            t = frame_ids(t0, CHUNK, width)
            grad = (
                da_ref[r, at, :].astype(F32) * pick(tab_ref, 0, t, row)
                + tok_ref[r, at, :].astype(F32) * pick(tab_ref, 4, t, row)
                + pick(tab_ref, 8, t, row)
            )
            out = og_ref[r, at, :].astype(F32) * ROOT_HALF + jnp.where(t < row.ends[2], grad, 0.0)
            out_ref[r, at, :] = out.astype(BF16)

        row.chunks(uniform, mixed)
        row_copy(r).start()

    for_rows(len_ref, rows, frames, body)
    for r in range(rows):
        row_copy(r).wait()


def projection_grad_kernel(all_ref, fc1_hbm, fc2_hbm, bias1_ref, bias2_ref, conv_bias_ref, rows_ref, grad_ref, sems):
    device = lax.axis_index("chip") * 2 + lax.axis_index("core")
    width = conv_bias_ref.shape[1]
    for i in range(all_ref.shape[0] // PAD):
        block = pl.ds(pl.multiple_of((device ^ i) * PAD, PAD), PAD)
        rows_ref[i * PAD : (i + 1) * PAD, :] = all_ref[block, :]
    grads, styles = rows_ref[:, : 4 * width], rows_ref[:, 4 * width :]
    grad_ref[...] = lax.dot_general(styles, grads, (((0,), (0,)), ((), ())), preferred_element_type=F32)
    copies = [
        pltpu.make_async_copy(grad_ref.at[:, pl.ds(i * 2 * width, 2 * width)], out, sems.at[i])
        for i, out in enumerate((fc1_hbm, fc2_hbm))
    ]
    for copy in copies:
        copy.start()
    values = grads.astype(F32)
    of_segment = frame_ids(0, values.shape[0], values.shape[1]) % 4 < SEGS
    bias = jnp.sum(jnp.where(of_segment, values, 0.0), axis=0, keepdims=True)
    bias1_ref[...] = bias[:, : 2 * width]
    bias2_ref[...] = bias[:, 2 * width :]
    rest = jnp.where(of_segment[:, :width], 0.0, values[:, :width])
    conv_bias_ref[...] = jnp.sum(rest, axis=0, keepdims=True)
    for copy in copies:
        copy.wait()


def assemble_kernel(own, half_ref, *refs):
    out2_hbm, out1_hbm, buf_ref, sems = refs[-4:]
    chips, count, _, rows, width = half_ref.shape
    half = chips * count * rows // 3
    core = lax.axis_index("core")
    place = pl.ds(pl.multiple_of((core if own else 1 - core) * half, half), half)
    copies = []
    for which, out_hbm in enumerate((out2_hbm, out1_hbm)):
        for b in range(chips * count):
            for j in range(rows // PAD):
                at = b * rows + j * PAD
                tap, channel = at // half, at % half
                block = half_ref[b // count, b % count, which, j * PAD : (j + 1) * PAD]
                buf_ref[which, tap, channel : channel + PAD, :] = block.astype(F32)
        copies.append(pltpu.make_async_copy(buf_ref.at[which], out_hbm.at[:, place, :], sems.at[which]))
        copies[-1].start()
    for copy in copies:
        copy.wait()


SPACES = {"s": pltpu.SMEM, "v": pltpu.VMEM, "h": pltpu.HBM}


def call(kernel, spaces, arrays, outs, scratch, vmem_mib, flops=0, nbytes=8 << 20, aliases=()):
    arrays = [
        pltpu.with_memory_space_constraint(a, pltpu.HBM) if c == "h" else a for c, a in zip(spaces, arrays)
    ]
    letters = list(zip(spaces, [*arrays, *outs]))
    specs = [jax.tree.map(lambda _, c=c: pl.BlockSpec(memory_space=SPACES[c]), a) for c, a in letters[: len(arrays)]]

    def shape_of(c, out):
        return pltpu.HBM(*out) if c == "h" else jax.ShapeDtypeStruct(*out)

    def spec_of(c, out):
        return pl.BlockSpec(memory_space=SPACES[c])

    shapes, out_specs = (
        [[f(c, o) for o in out] if isinstance(out, list) else f(c, out) for c, out in letters[len(arrays) :]]
        for f in (shape_of, spec_of)
    )
    return pl.pallas_call(
        kernel,
        out_shape=shapes,
        in_specs=specs,
        out_specs=out_specs,
        input_output_aliases=dict(aliases),
        scratch_shapes=[pltpu.SemaphoreType.DMA(s) if len(s) == 1 else pltpu.VMEM(*s) for s in scratch],
        compiler_params=pltpu.CompilerParams(vmem_limit_bytes=vmem_mib << 20),
        cost_estimate=pl.CostEstimate(flops=flops, bytes_accessed=nbytes, transcendentals=0),
    )(*arrays)


def after(x, *others):
    return lax.optimization_barrier((x, *others))[0]


def exchange(messages):
    return [messages[0]] + [swap(m, "tm", k) for k, m in enumerate(messages) if k > 0]


def scatter_sum(blocks, axis):
    return jnp.sum(lax.all_to_all(blocks, axis, 0, 0).astype(F32), axis=0).astype(BF16)


def spread(block, axis):
    return lax.all_to_all(jnp.broadcast_to(block[None], (lax.axis_size(axis), *block.shape)), axis, 0, 0)


def swap(x, axis, bit):
    return lax.ppermute(x, axis, [(i, i ^ bit) for i in range(lax.axis_size(axis))])


def sum_over_tm(x):
    count = lax.axis_size("tm")
    parts = [x.astype(F32)] + [swap(x, "tm", k).astype(F32) for k in range(1, count)]
    while len(parts) > 1:
        half = len(parts) // 2
        parts = [a + b for a, b in zip(parts[:half], parts[half:])]
    return parts[0]


def gather_rows(x):
    steps = [("core", 1)] + [("chip", 1 << b) for b in range((lax.axis_size("chip") - 1).bit_length())]
    for axis, bit in steps:
        x = jnp.concatenate([x, swap(x, axis, bit)])
    return x


def per_device(tokens, lengths, style, fc1_weight, fc1_bias, conv1_kernel, fc2_weight, fc2_bias, conv2_kernel,
               conv2_bias, out_grad):
    rows, frames, width = tokens.shape
    count, chips = lax.axis_size("tm"), lax.axis_size("chip")
    padded = frames + 2 * PAD
    affine1 = jnp.einsum("rsk,kc->rsc", style, fc1_weight, preferred_element_type=F32) + fc1_bias.astype(F32)
    affine2 = jnp.einsum("rsk,kc->rsc", style, fc2_weight, preferred_element_type=F32) + fc2_bias.astype(F32)
    kernel1, kernel2 = (k.reshape(3 * width, width) for k in (conv1_kernel, conv2_kernel))

    own, wide = ((rows, frames, width), BF16), ((rows, padded, width), BF16)
    hid, taps, kernel = ((rows, padded, width), F32), ((rows, frames, 3 * width), BF16), ((3 * width, width), BF16)
    sums, msg, half = ((rows, 8, width), F32), ((2 * rows, width), F32), ((3 * width // 2, width), BF16)
    acc, tab = ((8, 8, width), F32), ((16, 8, width), F32)
    buf, xs = ((padded, width), F32), ((padded, 3 * width), BF16)
    products = ((3, padded, width), F32)
    flops = 2 * rows * frames * 3 * width * width

    tok, w1, st1, msg1 = call(
        token_sums_kernel, "shhh" + "vvvv", (lengths, tokens, out_grad, kernel1),
        [own, kernel, sums, [((EDGE, width), F32)] * count],
        [((rows, PAD, width), BF16), ((rows, PAD, width), BF16), acc, (3,), (rows,)], SMALL,
    )
    rx1 = exchange(msg1)
    low1, hidden, st2, msg2, og, w2 = call(
        first_half_kernel, "svvvvvhh" + "vvvvvv", (lengths, tok, st1, rx1, affine1, w1, out_grad, kernel2),
        [wide, hid, sums, msg, own, kernel], [products, tab, acc, (2,)], SMALL, flops,
    )
    rx2 = exchange([msg2] * count)
    gs2, grad_low2, bias_part, low1_hbm, hidden_hbm = call(
        branch_grad_kernel, "svvvvv" + "vvvhh", (lengths, og, rx1, w2, low1, hidden),
        [taps, wide, ((8, width), F32), wide, hid], [buf, xs, (2,)], SMALL, flops,
    )
    low2, da2, gst2, msg3 = call(
        second_norm_kernel, "svvvvv" + "vvvv", (lengths, hidden, grad_low2, st2, rx2, affine2),
        [wide, wide, sums, msg], [tab, acc], SMALL,
    )
    rx3 = exchange([msg3] * count)

    def kernel_grad(own_half, first_frame, low, gs, kept):
        return call(
            functools.partial(kernel_grad_kernel, own_half, first_frame), "vvv" + "vh", (low, gs, kept), [half, wide],
            [((width // 2, 3 * width), F32), (1,)], SMALL, flops // 2,
        )

    send2, low2_hbm = kernel_grad(False, PAD, low2, gs2, low2)
    got2 = swap(send2, "core", 1)
    keep2, da2_hbm = kernel_grad(True, PAD, low2, after(gs2, send2), da2)
    half2 = (got2.astype(F32) + after(keep2, *rx3).astype(F32)).astype(BF16)
    blocks2 = lax.all_to_all(half2.reshape(chips, -1, width), "chip", 0, 0)

    grad_hidden, send1, keep1, affine_part2 = call(
        hidden_grad_kernel, "shhhvvvvv" + "hvvv",
        (lengths, low1_hbm, after(da2_hbm, half2), hidden_hbm, st2, rx2, gst2, rx3, affine2),
        [wide, half, half, ((4 * rows, 2 * width), F32)],
        [wide, wide, hid, wide, ((frames, 3 * width), BF16), buf, tab, ((width, 3 * width), F32), (3 * rows,), (rows,)], LARGE, flops,
    )
    got1 = swap(after(send1, blocks2), "core", 1)
    part2 = jnp.sum(blocks2.astype(F32), axis=0).astype(BF16)
    half1 = (got1.astype(F32) + keep1.astype(F32)).astype(BF16)
    part1 = scatter_sum(half1.reshape(chips, -1, width), "chip")

    da1, gst1, last_part = call(
        first_norm_grad_kernel, "shhhvvvvv" + "hvv",
        (lengths, after(grad_hidden, half1), kernel1, tokens, st1, rx1, affine1, affine_part2, bias_part),
        [own, sums, ((4 * rows, 4 * width), BF16)],
        [wide, kernel, own, own, ((frames, width), F32), products, tab, acc, ((4 * rows, 4 * width), F32),
         (1 + 2 * rows,), (rows,)],
        LARGE, flops,
    )
    both = jnp.concatenate([part2.reshape(count, -1, width), part1.reshape(count, -1, width)], axis=1)
    both = after(both, da1)
    last_part = after(last_part, both)
    both = scatter_sum(both, "tm")
    (block_out,) = call(
        block_out_kernel, "shhhv" + "h", (lengths, low2_hbm, after(tokens, both), kernel2, conv2_bias.reshape(1, width)), [own],
        [wide, own, kernel, products, own, (1 + 2 * rows,), (rows,)], LARGE, flops,
    )
    last = sum_over_tm(last_part)
    affine_grads = after(last, both).astype(BF16)
    both = spread(both, "tm")
    (input_grad,) = call(
        input_grad_kernel, "shhhvvvvv" + "h", (lengths, out_grad, after(da1, both), tokens, st1, rx1, gst1, last, affine1), [own],
        [own, own, own, tab, own, (3 * rows,), (rows,)], LARGE,
    )
    mine = affine_grads.reshape(rows, 4, 4 * width)[:, :SEGS].reshape(rows * SEGS, 4 * width)
    style_grad = lax.dot_general(
        mine[:, : 2 * width], fc1_weight, (((1,), (1,)), ((), ())), preferred_element_type=F32
    ) + lax.dot_general(mine[:, 2 * width :], fc2_weight, (((1,), (1,)), ((), ())), preferred_element_type=F32)
    style_grad = style_grad.reshape(style.shape)
    style_pad = jnp.pad(style, ((0, 0), (0, 1), (0, 0))).reshape(rows * 4, -1)
    gathered = gather_rows(jnp.concatenate([affine_grads, style_pad], axis=1))
    both = spread(after(both, block_out, gathered), "chip")
    fc_shape, bias_shape = ((style.shape[2], 2 * width), F32), ((1, 2 * width), F32)
    fc1_grad, fc2_grad, fc1_bias_grad, fc2_bias_grad, conv2_bias_grad = call(
        projection_grad_kernel, "v" + "hhvvv", (gathered,), [fc_shape, fc_shape, bias_shape, bias_shape, ((1, width), F32)],
        [(gathered.shape, BF16), ((style.shape[2], 4 * width), F32), (2,)], SMALL,
    )
    fc1_bias_grad, fc2_bias_grad, conv2_bias_grad = (
        b.reshape(b.shape[1]) for b in (fc1_bias_grad, fc2_bias_grad, conv2_bias_grad)
    )

    both = both.reshape(chips, count, 2, -1, width)
    both, input_grad, *small = lax.optimization_barrier(
        (both, input_grad, style_grad, fc1_grad, fc2_grad, fc1_bias_grad, fc2_bias_grad, conv2_bias_grad)
    )
    style_grad, fc1_grad, fc2_grad, fc1_bias_grad, fc2_bias_grad, conv2_bias_grad = small
    other = swap(both, "core", 1)
    if both.shape[3] % PAD == 0:
        conv_shape = ((3, width, width), F32)
        buffers = [((2, 3, width // 2, width), F32), (2,)]
        sums_own = call(
            functools.partial(assemble_kernel, True), "v" + "hh", (both,), [conv_shape, conv_shape], buffers, SMALL,
        )
        conv2_sum, conv1_sum = call(
            functools.partial(assemble_kernel, False), "vhh" + "hh", (other, *sums_own), [conv_shape, conv_shape], buffers,
            SMALL, aliases=((1, 0), (2, 1)),
        )
    else:
        first = lax.axis_index("core") == 0
        halves = [jnp.where(first, both, other), jnp.where(first, other, both)]
        halves = [jnp.moveaxis(h, 2, 0).reshape(2, 3, width // 2, width) for h in halves]
        conv2_sum, conv1_sum = jnp.concatenate(halves, axis=2).astype(F32)
    return (
        block_out, input_grad, style_grad, fc1_grad, fc1_bias_grad, conv1_sum, fc2_grad, fc2_bias_grad, conv2_sum,
        conv2_bias_grad,
    )


def solution(mesh):
    chips = mesh.shape["dp"] // 2
    mesh = Mesh(mesh.devices.reshape(chips, 2, mesh.shape["tm"]), ("chip", "core", "tm"))
    dp = ("chip", "core")
    return jax.shard_map(
        per_device,
        mesh=mesh,
        in_specs=(
            P(dp, "tm", None),
            P(dp, None),
            P(dp, None, None),
            P(),
            P(),
            P(),
            P(),
            P(),
            P(),
            P(),
            P(dp, "tm", None),
        ),
        out_specs=(
            P(dp, "tm", None),
            P(dp, "tm", None),
            P(dp, None, None),
            P(),
            P(),
            P(),
            P(),
            P(),
            P(),
            P(),
        ),
        check_vma=False,
    )
```

```python
import functools

import jax
import jax.numpy as jnp
from jax import lax
from jax.experimental import pallas as pl
from jax.experimental.pallas import tpu as pltpu
from jax.sharding import Mesh, PartitionSpec as P

EPSILON = 1e-05
ROOT_HALF = 0.7071067811865476
SEGS = 3
PAD = 16
CHUNK = 32
EDGE = 8 + 16
F32 = jnp.float32
BF16 = jnp.bfloat16
SMALL, LARGE = 20, 30


class Row:
    def __init__(self, len_ref, r, frames):
        self.frames = frames
        self.z = lax.axis_index("tm")
        self.counts = [len_ref[r, s] for s in range(SEGS)]
        l0, l1, l2 = self.counts
        start = -self.z * frames
        e0 = start + l0
        e1 = e0 + l1
        e2 = e1 + l2
        self.begins = [start, e0, e1]
        self.ends = [e0, e1, e2]
        self.long_at = jnp.where(l0 >= jnp.maximum(l1, l2), 0, jnp.where(l1 >= l2, 1, 2))
        self.long_begin = self.of_long(self.begins)
        self.long_end = self.of_long(self.ends)

    def of_long(self, values):
        return jnp.where(
            self.long_at == 0, values[0], jnp.where(self.long_at == 1, values[1], values[2])
        )

    def segment(self, t):
        return sum((t >= e).astype(jnp.int32) for e in self.ends)

    def chunks(self, uniform_fn, mixed_fn, sums=None, acc_ref=None, ends=None):
        for t0 in range(0, self.frames, CHUNK):
            uniform_fn(t0, self.segment(t0))
        if sums is not None:
            sums.put(acc_ref)
        self.mixed(mixed_fn, ends)

    def mixed(self, fn, ends=None):
        for end in ends or self.ends:

            @pl.when(jnp.logical_and(jnp.logical_and(end > 0, end < self.frames), end % CHUNK != 0))
            def _(end=end):
                fn(pl.multiple_of((end // CHUNK) * CHUNK, CHUNK))


def frame_ids(t0, rows, width):
    return t0 + lax.broadcasted_iota(jnp.int32, (rows, width), 0)


def pick(tab_ref, base, t, row):
    value = tab_ref[base, 0:1, :]
    for s in range(SEGS):
        value = jnp.where(t >= row.ends[s], tab_ref[base + s + 1, 0:1, :], value)
    return value


def entry(tab_ref, index, rows=CHUNK):
    value = tab_ref[index]
    return jnp.broadcast_to(value[None], (rows // 8, *value.shape)).reshape(rows, value.shape[1])


def put_entry(tab_ref, index, value):
    tab_ref[index] = jnp.broadcast_to(value, tab_ref.shape[1:])


def put_table(tab_ref, base, values):
    for s in range(SEGS):
        put_entry(tab_ref, base + s, values[s])
    put_entry(tab_ref, base + SEGS, jnp.zeros_like(values[0]))


def fold(x):
    return jnp.sum(x.reshape(x.shape[0] // 8, 8, x.shape[1]), axis=0)


def add_masked_sums(acc_ref, t, row, first, second):
    for s in range(SEGS):
        inside = jnp.logical_and(t >= row.begins[s], t < row.ends[s])
        acc_ref[s] += fold(jnp.where(inside, first, 0.0))
        acc_ref[4 + s] += fold(jnp.where(inside, second, 0.0))


def put_sums(acc_ref, st_ref, msg_refs, row, r):
    for s in range(SEGS):
        for k in range(2):
            st_ref[r, pl.ds(SEGS * k + s, 1), :] = jnp.sum(acc_ref[4 * k + s], axis=0, keepdims=True)
    for k in range(2):
        value = jnp.sum(acc_ref[4 * k + row.long_at], axis=0, keepdims=True)
        for ref in msg_refs:
            ref[pl.ds(2 * r + k, 1), :] = value


def sums_of(row, r, st_ref, rx_refs, s):
    out = []
    for k in range(2):
        total = sum(ref[pl.ds(2 * r + k, 1), :] for ref in rx_refs)
        local = st_ref[r, SEGS * k + s : SEGS * k + s + 1, :]
        out.append(jnp.where(row.long_at == s, total, local))
    return out


def norm_of(row, r, st_ref, rx_ref, aff_ref, s):
    width = st_ref.shape[2]
    first, second = sums_of(row, r, st_ref, rx_ref, s)
    count = jnp.full((1, width), row.counts[s].astype(F32))
    mean = first / count
    rstd = lax.rsqrt(second / count - mean * mean + EPSILON)
    affine = aff_ref[r, s : s + 1, :]
    return mean, rstd, 1.0 + affine[:, :width], affine[:, width:], count


def put_forward(row, r, st_ref, rx_ref, aff_ref, tab_ref):
    scales, shifts = [], []
    for s in range(SEGS):
        mean, rstd, gain, beta, _ = norm_of(row, r, st_ref, rx_ref, aff_ref, s)
        scales.append(gain * rstd)
        shifts.append(beta - mean * scales[-1])
    put_table(tab_ref, 0, scales)
    put_table(tab_ref, 4, shifts)
    put_entry(tab_ref, 12, row.of_long(scales))
    put_entry(tab_ref, 13, row.of_long(shifts))


def put_backward(row, r, st_ref, rx_ref, gst_ref, grx_ref, aff_ref, tab_ref):
    parts = [[], [], []]
    for s in range(SEGS):
        mean, rstd, gain, _, count = norm_of(row, r, st_ref, rx_ref, aff_ref, s)
        if isinstance(grx_ref, (list, tuple)):
            shift, scale = sums_of(row, r, gst_ref, grx_ref, s)
            scale = rstd * (scale - mean * shift)
        else:
            width = mean.shape[1]
            total = grx_ref[pl.ds(4 * r + s, 1), : 2 * width] + grx_ref[pl.ds(4 * r + SEGS, 1), 2 * width :]
            shift, local = gst_ref[r, s : s + 1, :], gst_ref[r, SEGS + s : SEGS + s + 1, :]
            scale = jnp.where(row.long_at == s, total[:, :width], rstd * (local - mean * shift))
            shift = jnp.where(row.long_at == s, total[:, width:], shift)
        mean_g = gain * shift / count
        slope = rstd * rstd * (gain * scale / count)
        parts[0].append(gain * rstd)
        parts[1].append(-slope)
        parts[2].append(slope * mean - rstd * mean_g)
    for k in range(3):
        put_table(tab_ref, 4 * k, parts[k])
        put_entry(tab_ref, 12 + k, row.of_long(parts[k]))


def put_affine_grads(row, r, st_ref, rx_ref, gst_ref, aff_ref, out_ref, at):
    width = st_ref.shape[2]
    for s in range(SEGS):
        mean, rstd, _, _, _ = norm_of(row, r, st_ref, rx_ref, aff_ref, s)
        shift = gst_ref[r, s : s + 1, :]
        scale = rstd * (gst_ref[r, SEGS + s : SEGS + s + 1, :] - mean * shift)
        out_ref[pl.ds(4 * r + s, 1), at : at + width] = scale
        out_ref[pl.ds(4 * r + s, 1), at + width : at + 2 * width] = shift


def silu(a):
    half = 0.5 * a
    return half + half * jnp.tanh(half)


def silu_and_slope(a):
    gate = 0.5 + 0.5 * jnp.tanh(0.5 * a)
    low = a * gate
    return low, gate + low * (1.0 - gate)


def halo_tile(row, frames, width, left):
    t = frame_ids(-PAD if left else frames, PAD, width)
    near = jnp.logical_and(t >= -2, t < frames + 2)
    inside = jnp.logical_and(t >= row.long_begin, t < row.long_end)
    return t, jnp.logical_and(near, inside)


def edge_tile(rx_refs, row, r, t, at, left):
    last = len(rx_refs) - 1
    neighbour = jnp.maximum(row.z - 1, 0) if left else jnp.minimum(row.z + 1, last)
    edges = []
    for i in range(2):
        value, k = rx_refs[1][pl.ds(8 + 4 * r + at + i, 1), :], 3
        while k <= last:
            value = jnp.where((row.z ^ neighbour) == k, rx_refs[k][pl.ds(8 + 4 * r + at + i, 1), :], value)
            k = 2 * k + 1
        edges.append(value)
    second = -1 if left else row.frames + 1
    return jnp.where(t == second, edges[1], edges[0])


def stack_taps(buf_ref, xs_ref, row, frames, forward, halo, low_ref=None, r=None):
    width = buf_ref.shape[1]
    before_at, after_at = (0, 2 * width) if forward else (2 * width, 0)
    base = PAD if halo else 0
    for i in range(frames // CHUNK):
        o, d = PAD + i * CHUNK, base + i * CHUNK
        centre = buf_ref[o : o + CHUNK, :].astype(BF16)
        xs_ref[d : d + CHUNK, width : 2 * width] = centre
        xs_ref[d : d + CHUNK, before_at : before_at + width] = buf_ref[o - 1 : o - 1 + CHUNK, :].astype(BF16)
        xs_ref[d : d + CHUNK, after_at : after_at + width] = buf_ref[o + 1 : o + 1 + CHUNK, :].astype(BF16)
        if low_ref is not None:
            low_ref[r, i * CHUNK : (i + 1) * CHUNK, :] = centre
    if halo:
        end = PAD + frames
        left, right = buf_ref[0:PAD, :], buf_ref[end : end + PAD, :]
        xs_ref[0:PAD, width : 2 * width] = left.astype(BF16)
        xs_ref[end : end + PAD, width : 2 * width] = right.astype(BF16)
        xs_ref[0:PAD, before_at : before_at + width] = pltpu.roll(left, 1, 0).astype(BF16)
        xs_ref[end : end + PAD, before_at : before_at + width] = buf_ref[end - 1 : end - 1 + PAD, :].astype(BF16)
        xs_ref[0:PAD, after_at : after_at + width] = buf_ref[1 : 1 + PAD, :].astype(BF16)
        xs_ref[end : end + PAD, after_at : after_at + width] = pltpu.roll(right, PAD - 1, 0).astype(BF16)
    for end in row.ends[:2]:
        for at, t in ((before_at, end), (after_at, end - 1)):

            @pl.when(jnp.logical_and(t >= 0, t < frames))
            def _(at=at, t=t):
                tile = pl.multiple_of((t // PAD) * PAD, PAD)
                rows = pl.ds(base + tile, PAD)
                value = xs_ref[rows, at : at + width].astype(F32)
                keep = frame_ids(tile, PAD, width) != t
                xs_ref[rows, at : at + width] = jnp.where(keep, value, 0.0).astype(BF16)


class Sums:
    def __init__(self, row, width):
        self.row = row
        self.parts = [[jnp.zeros((8, width), F32)] * SEGS for _ in range(2)]

    def add(self, t0, rows, first, second):
        folded = (fold(first), fold(second))
        for s in range(SEGS):
            fills = jnp.logical_and(t0 >= self.row.begins[s], t0 + rows <= self.row.ends[s])
            weight = jnp.where(fills, 1.0, 0.0)
            for k in range(2):
                self.parts[k][s] = self.parts[k][s] + folded[k] * weight

    def put(self, acc_ref):
        for k in range(2):
            for s in range(SEGS):
                acc_ref[4 * k + s] = self.parts[k][s]


def rows_moved(ref, at, rows, step):
    if at - step < 0 or at + rows - step > ref.shape[0]:
        return pltpu.roll(ref[at : at + rows, :], step % rows, 0)
    return ref[at - step : at - step + rows, :]


def tap_sum(z_ref, row, t0, rows, first=0, last=2):
    at, t = PAD + t0, frame_ids(t0, rows, z_ref.shape[2])
    starts = functools.reduce(jnp.logical_or, [t == end for end in row.ends])
    stops = functools.reduce(jnp.logical_or, [t == end - 1 for end in row.ends])
    before = jnp.where(starts, 0.0, rows_moved(z_ref.at[first], at, rows, 1))
    after = jnp.where(stops, 0.0, rows_moved(z_ref.at[last], at, rows, -1))
    return before + z_ref[1, at : at + rows, :] + after


def put_products(x, w_ref, z_ref, transposed=False):
    width = x.shape[1]
    dims = (((1,), (1 if transposed else 0,)), ((), ()))
    for k in range(3):
        tap = w_ref[k * width : (k + 1) * width, :]
        z_ref[k] = lax.dot_general(x, tap, dims, preferred_element_type=F32)


def times_transposed(xs, w_ref, width):
    out = None
    for k in range(3):
        part = lax.dot_general(
            xs[:, k * width : (k + 1) * width],
            w_ref[k * width : (k + 1) * width, :],
            (((1,), (1,)), ((), ())),
            preferred_element_type=F32,
        )
        out = part if out is None else out + part
    return out


def for_rows(len_ref, rows, frames, body):
    def step(r, carry):
        body(r, Row(len_ref, r, frames))
        return carry

    lax.fori_loop(0, rows, step, 0)


def token_sums_kernel(len_ref, tok_hbm, og_hbm, w_hbm, tok_ref, w_ref, st_ref, msg_refs, head_ref, tail_ref, acc_ref,
                      sems, row_sems):
    rows, frames, width = tok_ref.shape

    def row_copy(r):
        return pltpu.make_async_copy(tok_hbm.at[r], tok_ref.at[r], row_sems.at[r])

    for r in range(rows):
        row_copy(r).start()
    edges = (
        pltpu.make_async_copy(og_hbm.at[:, pl.ds(0, PAD), :], head_ref, sems.at[0]),
        pltpu.make_async_copy(og_hbm.at[:, pl.ds(frames - PAD, PAD), :], tail_ref, sems.at[1]),
    )
    for copy in edges:
        copy.start()
    kernel_copy = pltpu.make_async_copy(w_hbm, w_ref, sems.at[2])
    kernel_copy.start()
    for copy in edges:
        copy.wait()

    def body(r, row):
        row_copy(r).wait()
        sums = Sums(row, width)

        def uniform(t0, s):
            v = tok_ref[r, pl.ds(t0, CHUNK), :].astype(F32)
            sums.add(t0, CHUNK, v, v * v)

        def mixed(t0):
            v = tok_ref[r, pl.ds(t0, CHUNK), :].astype(F32)
            add_masked_sums(acc_ref, frame_ids(t0, CHUNK, width), row, v, v * v)

        row.chunks(uniform, mixed, sums, acc_ref)
        put_sums(acc_ref, st_ref, msg_refs, row, r)
        for j, (head, tail) in enumerate(
            ((tok_ref[r, 0:PAD, :], tok_ref[r, frames - PAD : frames, :]), (head_ref[r], tail_ref[r]))
        ):
            first, last = head.astype(F32), tail.astype(F32)
            for i in range(2):
                to_left, to_right = first[i : i + 1, :], last[PAD - 2 + i : PAD - 1 + i, :]
                for k, ref in enumerate(msg_refs):
                    value = jnp.where(row.z < row.z ^ k, to_right, to_left)
                    ref[pl.ds(8 + 4 * r + 2 * j + i, 1), :] = value

    for_rows(len_ref, rows, frames, body)
    kernel_copy.wait()


def first_half_kernel(len_ref, tok_ref, st_ref, rx_ref, aff_ref, w_ref, og_hbm, w2_hbm, low_ref,
                      hid_ref, st2_ref, msg_ref, og_ref, w2_ref, z_ref, tab_ref, acc_ref, sems):
    rows, frames, width = tok_ref.shape
    copies = (
        pltpu.make_async_copy(og_hbm, og_ref, sems.at[0]),
        pltpu.make_async_copy(w2_hbm, w2_ref, sems.at[1]),
    )
    for copy in copies:
        copy.start()

    def body(r, row):
        put_forward(row, r, st_ref, rx_ref, aff_ref, tab_ref)

        def uniform(t0, s):
            v = tok_ref[r, pl.ds(t0, CHUNK), :].astype(F32)
            low = silu(v * entry(tab_ref, s) + entry(tab_ref, 4 + s))
            low_ref[r, pl.ds(PAD + t0, CHUNK), :] = low.astype(BF16)

        def mixed(t0):
            t = frame_ids(t0, CHUNK, width)
            v = tok_ref[r, pl.ds(t0, CHUNK), :].astype(F32)
            low = silu(v * pick(tab_ref, 0, t, row) + pick(tab_ref, 4, t, row))
            low_ref[r, pl.ds(PAD + t0, CHUNK), :] = jnp.where(t < row.ends[2], low, 0.0).astype(BF16)

        row.chunks(uniform, mixed)
        for left in (True, False):
            t, valid = halo_tile(row, frames, width, left)
            low = silu(edge_tile(rx_ref, row, r, t, 0, left) * tab_ref[12, 0:1, :] + tab_ref[13, 0:1, :])
            at = 0 if left else PAD + frames
            low_ref[r, at : at + PAD, :] = jnp.where(valid, low, 0.0).astype(BF16)
        put_products(low_ref[r], w_ref, z_ref)
        sums = Sums(row, width)
        for t0 in range(0, frames, CHUNK):
            v = tap_sum(z_ref, row, t0, CHUNK)
            hid_ref[r, PAD + t0 : PAD + t0 + CHUNK, :] = v
            sums.add(t0, CHUNK, v, v * v)
        sums.put(acc_ref)
        for t0 in (-PAD, frames):
            hid_ref[r, PAD + t0 : 2 * PAD + t0, :] = tap_sum(z_ref, row, t0, PAD)

        def mixed_sums(t0):
            v = hid_ref[r, pl.ds(PAD + t0, CHUNK), :]
            add_masked_sums(acc_ref, frame_ids(t0, CHUNK, width), row, v, v * v)

        row.mixed(mixed_sums)
        put_sums(acc_ref, st2_ref, [msg_ref], row, r)

    for_rows(len_ref, rows, frames, body)
    for copy in copies:
        copy.wait()


def branch_grad_kernel(len_ref, og_ref, rx_ref, w_ref, gs_ref, q_ref, bias_ref, buf_ref, xs_ref):
    rows, frames, width = og_ref.shape
    bias_ref[...] = jnp.zeros_like(bias_ref)

    def body(r, row):
        def put(t0, g, weight):
            g = g.astype(BF16).astype(F32)
            buf_ref[pl.ds(PAD + t0, CHUNK), :] = g
            bias_ref[...] += fold(g) * weight

        def uniform(t0, s):
            scale = jnp.where(s < SEGS, ROOT_HALF, 0.0)
            g = og_ref[r, pl.ds(t0, CHUNK), :].astype(F32) * scale
            put(t0, g, jnp.where(t0 + CHUNK <= row.ends[2], 1.0, 0.0))

        def mixed(t0):
            t = frame_ids(t0, CHUNK, width)
            g = og_ref[r, pl.ds(t0, CHUNK), :].astype(F32) * ROOT_HALF
            put(t0, jnp.where(t < row.ends[2], g, 0.0), 1.0)

        row.chunks(uniform, mixed, ends=row.ends[2:])
        for left in (True, False):
            t, valid = halo_tile(row, frames, width, left)
            at = 0 if left else PAD + frames
            g = edge_tile(rx_ref, row, r, t, 2, left) * ROOT_HALF
            buf_ref[at : at + PAD, :] = jnp.where(valid, g, 0.0)
        stack_taps(buf_ref, xs_ref, row, frames, False, True)
        gs_ref[r] = xs_ref[PAD : PAD + frames, :]
        q_ref[r] = times_transposed(xs_ref[...], w_ref, width).astype(BF16)

    for_rows(len_ref, rows, frames, body)


def second_norm_kernel(len_ref, hid_ref, q_ref, st_ref, rx_ref, aff_ref, low_ref, da_ref, gst_ref, msg_ref,
                       tab_ref, acc_ref):
    rows, padded, width = hid_ref.shape
    frames = padded - 2 * PAD

    def body(r, row):
        put_forward(row, r, st_ref, rx_ref, aff_ref, tab_ref)
        sums = Sums(row, width)

        def uniform(t0, s):
            at = pl.ds(PAD + t0, CHUNK)
            v = hid_ref[r, at, :]
            low, slope = silu_and_slope(v * entry(tab_ref, s) + entry(tab_ref, 4 + s))
            da = slope * q_ref[r, at, :].astype(F32)
            low_ref[r, at, :] = low.astype(BF16)
            da_ref[r, at, :] = da.astype(BF16)
            sums.add(t0, CHUNK, da, da * v)

        def mixed(t0):
            at = pl.ds(PAD + t0, CHUNK)
            t = frame_ids(t0, CHUNK, width)
            live = t < row.ends[2]
            v = hid_ref[r, at, :]
            low, slope = silu_and_slope(v * pick(tab_ref, 0, t, row) + pick(tab_ref, 4, t, row))
            da = slope * q_ref[r, at, :].astype(F32)
            low_ref[r, at, :] = jnp.where(live, low, 0.0).astype(BF16)
            da_ref[r, at, :] = jnp.where(live, da, 0.0).astype(BF16)
            add_masked_sums(acc_ref, t, row, da, da * v)

        row.chunks(uniform, mixed, sums, acc_ref)
        for left in (True, False):
            t, valid = halo_tile(row, frames, width, left)
            at = 0 if left else PAD + frames
            v = hid_ref[r, at : at + PAD, :]
            low, slope = silu_and_slope(v * tab_ref[12, 0:1, :] + tab_ref[13, 0:1, :])
            da = slope * q_ref[r, at : at + PAD, :].astype(F32)
            low_ref[r, at : at + PAD, :] = jnp.where(valid, low, 0.0).astype(BF16)
            da_ref[r, at : at + PAD, :] = jnp.where(valid, da, 0.0).astype(BF16)
        put_sums(acc_ref, gst_ref, [msg_ref], row, r)

    for_rows(len_ref, rows, frames, body)


class Loads:
    def __init__(self, rows, sems, whole, by_row):
        count = len(whole)
        self.whole = [pltpu.make_async_copy(a, b, sems.at[i]) for i, (a, b) in enumerate(whole)]
        self.row = lambda r: [
            pltpu.make_async_copy(a.at[r], b.at[r], sems.at[count + i * rows + r]) for i, (a, b) in enumerate(by_row)
        ]
        for copy in (*self.row(0), *self.whole):
            copy.start()
        for r in range(1, rows):
            for copy in self.row(r):
                copy.start()

    def wait(self, r):
        for copy in self.row(r):
            copy.wait()

        @pl.when(r == 0)
        def _():
            for copy in self.whole:
                copy.wait()


def block_out_kernel(len_ref, low_hbm, tok_hbm, w_hbm, bias_ref, out_hbm, low_ref, tok_ref, w_ref, z_ref, out_ref,
                     sems, row_sems):
    rows, frames, width = tok_ref.shape
    loads = Loads(rows, sems, [(w_hbm, w_ref)], [(low_hbm, low_ref), (tok_hbm, tok_ref)])

    def row_copy(r):
        return pltpu.make_async_copy(out_ref.at[r], out_hbm.at[r], row_sems.at[r])

    def body(r, row):
        loads.wait(r)
        bias = bias_ref[...].astype(F32)
        put_products(low_ref[r], w_ref, z_ref)
        for t0 in range(0, frames, CHUNK):
            live = frame_ids(t0, CHUNK, width) < row.ends[2]
            branch = tap_sum(z_ref, row, t0, CHUNK) + jnp.where(live, bias, 0.0)
            out = (tok_ref[r, t0 : t0 + CHUNK, :].astype(F32) + branch) * ROOT_HALF
            out_ref[r, t0 : t0 + CHUNK, :] = out.astype(BF16)
        row_copy(r).start()

    for_rows(len_ref, rows, frames, body)
    for r in range(rows):
        row_copy(r).wait()


def half_of_grad(low_ref, gs_ref, r, half, first_frame):
    frames, width = gs_ref.shape[1], low_ref.shape[2] // 2
    u = low_ref[r, first_frame : first_frame + frames, pl.ds(pl.multiple_of(half * width, width), width)]
    return lax.dot_general(u, gs_ref[r], (((0,), (0,)), ((), ())), preferred_element_type=F32)


def put_half(acc_ref, out_ref):
    half, width = acc_ref.shape[0], acc_ref.shape[1] // 3
    for k in range(3):
        out_ref[k * half : (k + 1) * half, :] = acc_ref[:, k * width : (k + 1) * width].astype(BF16)


def kernel_grad_kernel(own, first_frame, low_ref, gs_ref, out_ref, *refs):
    acc_ref = refs[-1] if own else refs[1]
    if not own:
        store = pltpu.make_async_copy(low_ref, refs[0], refs[2].at[0])
        store.start()
    core = lax.axis_index("core")
    half = core if own else 1 - core
    acc_ref[...] = half_of_grad(low_ref, gs_ref, 0, half, first_frame)

    def step(r, carry):
        acc_ref[...] += half_of_grad(low_ref, gs_ref, r, half, first_frame)
        return carry

    lax.fori_loop(1, low_ref.shape[0], step, 0)
    put_half(acc_ref, out_ref)
    if not own:
        store.wait()


def hidden_grad_kernel(len_ref, low_ref, da_ref, hid_ref, st_ref, rx_ref, gst_ref, grx_ref, aff_ref,
                       g_hbm, gs_ref, send_ref, part_ref, g_ref, buf_ref, tab_ref, acc_ref, row_sems):
    rows, frames, width = low_ref.shape[0], gs_ref.shape[1], low_ref.shape[2]
    part_ref[...] = jnp.zeros_like(part_ref)
    acc_ref[...] = jnp.zeros_like(acc_ref)

    def row_copy(r):
        return pltpu.make_async_copy(g_ref.at[r], g_hbm.at[r], row_sems.at[r])

    def body(r, row):
        put_affine_grads(row, r, st_ref, rx_ref, gst_ref, aff_ref, part_ref, 0)
        put_backward(row, r, st_ref, rx_ref, gst_ref, grx_ref, aff_ref, tab_ref)

        def uniform(t0, s):
            at = pl.ds(PAD + t0, CHUNK)
            buf_ref[at, :] = (
                da_ref[r, at, :].astype(F32) * entry(tab_ref, s)
                + hid_ref[r, at, :] * entry(tab_ref, 4 + s)
                + entry(tab_ref, 8 + s)
            )

        def mixed(t0):
            at = pl.ds(PAD + t0, CHUNK)
            t = frame_ids(t0, CHUNK, width)
            grad = (
                da_ref[r, at, :].astype(F32) * pick(tab_ref, 0, t, row)
                + hid_ref[r, at, :] * pick(tab_ref, 4, t, row)
                + pick(tab_ref, 8, t, row)
            )
            buf_ref[at, :] = jnp.where(t < row.ends[2], grad, 0.0)

        row.chunks(uniform, mixed)
        for left in (True, False):
            t, valid = halo_tile(row, frames, width, left)
            at = 0 if left else PAD + frames
            grad = (
                da_ref[r, at : at + PAD, :].astype(F32) * tab_ref[12, 0:1, :]
                + hid_ref[r, at : at + PAD, :] * tab_ref[13, 0:1, :]
                + tab_ref[14, 0:1, :]
            )
            buf_ref[at : at + PAD, :] = jnp.where(valid, grad, 0.0)
        g_ref[r] = buf_ref[...].astype(BF16)
        stack_taps(buf_ref, gs_ref.at[r], row, frames, False, False)
        row_copy(r).start()
        acc_ref[...] += half_of_grad(low_ref, gs_ref, r, 1 - lax.axis_index("core"), PAD)

    for_rows(len_ref, rows, frames, body)
    put_half(acc_ref, send_ref)
    for r in range(rows):
        row_copy(r).wait()


def first_norm_grad_kernel(len_ref, g_hbm, w_hbm, tok_hbm, st_ref, rx_ref, aff_ref, part2_ref, bias_ref,
                           da_hbm, gst_ref, out_ref, g_ref, w_ref, tok_ref, da_ref, q_ref, z_ref, tab_ref, acc_ref,
                           part_ref, sems, row_sems):
    rows, frames, width = tok_ref.shape
    loads = Loads(rows, sems, [(w_hbm, w_ref)], [(g_hbm, g_ref), (tok_hbm, tok_ref)])
    part_ref[:, : 2 * width] = jnp.zeros((part_ref.shape[0], 2 * width), F32)
    part_ref[:, 2 * width :] = part2_ref[...]
    part_ref[SEGS : SEGS + 1, :width] = jnp.sum(bias_ref[...], axis=0, keepdims=True)

    def row_copy(r):
        return pltpu.make_async_copy(da_ref.at[r], da_hbm.at[r], row_sems.at[r])

    def body(r, row):
        put_forward(row, r, st_ref, rx_ref, aff_ref, tab_ref)
        loads.wait(r)
        put_products(g_ref[r], w_ref, z_ref, True)
        for t0 in range(0, frames, CHUNK):
            q_ref[t0 : t0 + CHUNK, :] = tap_sum(z_ref, row, t0, CHUNK, 2, 0)
        sums = Sums(row, width)

        def uniform(t0, s):
            at = pl.ds(t0, CHUNK)
            v = tok_ref[r, at, :].astype(F32)
            _, slope = silu_and_slope(v * entry(tab_ref, s) + entry(tab_ref, 4 + s))
            da = slope * q_ref[at, :]
            da_ref[r, at, :] = da.astype(BF16)
            sums.add(t0, CHUNK, da, da * v)

        def mixed(t0):
            at = pl.ds(t0, CHUNK)
            t = frame_ids(t0, CHUNK, width)
            v = tok_ref[r, at, :].astype(F32)
            _, slope = silu_and_slope(v * pick(tab_ref, 0, t, row) + pick(tab_ref, 4, t, row))
            da = slope * q_ref[at, :]
            da_ref[r, at, :] = jnp.where(t < row.ends[2], da, 0.0).astype(BF16)
            add_masked_sums(acc_ref, t, row, da, da * v)

        row.chunks(uniform, mixed, sums, acc_ref)
        row_copy(r).start()
        put_sums(acc_ref, gst_ref, [], row, r)
        put_affine_grads(row, r, st_ref, rx_ref, gst_ref, aff_ref, part_ref, 0)
        value = part_ref[pl.ds(4 * r + row.long_at, 1), : 2 * width]
        part_ref[pl.ds(4 * r + SEGS, 1), 2 * width :] = value - value.astype(BF16).astype(F32)

    for_rows(len_ref, rows, frames, body)
    out_ref[...] = part_ref[...].astype(BF16)
    for r in range(rows):
        row_copy(r).wait()


def input_grad_kernel(len_ref, og_hbm, da_hbm, tok_hbm, st_ref, rx_ref, gst_ref, grx_ref, aff_ref, out_hbm,
                      og_ref, da_ref, tok_ref, tab_ref, out_ref, sems, row_sems):
    rows, frames, width = tok_ref.shape
    loads = Loads(rows, sems, [], [(og_hbm, og_ref), (da_hbm, da_ref), (tok_hbm, tok_ref)])

    def row_copy(r):
        return pltpu.make_async_copy(out_ref.at[r], out_hbm.at[r], row_sems.at[r])

    def body(r, row):
        put_backward(row, r, st_ref, rx_ref, gst_ref, grx_ref, aff_ref, tab_ref)
        loads.wait(r)

        def uniform(t0, s):
            at = pl.ds(t0, CHUNK)
            out = (
                og_ref[r, at, :].astype(F32) * ROOT_HALF
                + da_ref[r, at, :].astype(F32) * entry(tab_ref, s)
                + tok_ref[r, at, :].astype(F32) * entry(tab_ref, 4 + s)
                + entry(tab_ref, 8 + s)
            )
            out_ref[r, at, :] = out.astype(BF16)

        def mixed(t0):
            at = pl.ds(t0, CHUNK)
            t = frame_ids(t0, CHUNK, width)
            grad = (
                da_ref[r, at, :].astype(F32) * pick(tab_ref, 0, t, row)
                + tok_ref[r, at, :].astype(F32) * pick(tab_ref, 4, t, row)
                + pick(tab_ref, 8, t, row)
            )
            out = og_ref[r, at, :].astype(F32) * ROOT_HALF + jnp.where(t < row.ends[2], grad, 0.0)
            out_ref[r, at, :] = out.astype(BF16)

        row.chunks(uniform, mixed)
        row_copy(r).start()

    for_rows(len_ref, rows, frames, body)
    for r in range(rows):
        row_copy(r).wait()


def projection_grad_kernel(all_ref, fc1_hbm, fc2_hbm, bias1_ref, bias2_ref, conv_bias_ref, rows_ref, grad_ref, sems):
    device = lax.axis_index("chip") * 2 + lax.axis_index("core")
    width = conv_bias_ref.shape[1]
    for i in range(all_ref.shape[0] // PAD):
        block = pl.ds(pl.multiple_of((device ^ i) * PAD, PAD), PAD)
        rows_ref[i * PAD : (i + 1) * PAD, :] = all_ref[block, :]
    grads, styles = rows_ref[:, : 4 * width], rows_ref[:, 4 * width :]
    grad_ref[...] = lax.dot_general(styles, grads, (((0,), (0,)), ((), ())), preferred_element_type=F32)
    copies = [
        pltpu.make_async_copy(grad_ref.at[:, pl.ds(i * 2 * width, 2 * width)], out, sems.at[i])
        for i, out in enumerate((fc1_hbm, fc2_hbm))
    ]
    for copy in copies:
        copy.start()
    values = grads.astype(F32)
    of_segment = frame_ids(0, values.shape[0], values.shape[1]) % 4 < SEGS
    bias = jnp.sum(jnp.where(of_segment, values, 0.0), axis=0, keepdims=True)
    bias1_ref[...] = bias[:, : 2 * width]
    bias2_ref[...] = bias[:, 2 * width :]
    rest = jnp.where(of_segment[:, :width], 0.0, values[:, :width])
    conv_bias_ref[...] = jnp.sum(rest, axis=0, keepdims=True)
    for copy in copies:
        copy.wait()


def assemble_kernel(own, half_ref, *refs):
    out2_hbm, out1_hbm, buf_ref, sems = refs[-4:]
    chips, count, _, rows, width = half_ref.shape
    half = chips * count * rows // 3
    core = lax.axis_index("core")
    place = pl.ds(pl.multiple_of((core if own else 1 - core) * half, half), half)
    copies = []
    for which, out_hbm in enumerate((out2_hbm, out1_hbm)):
        for b in range(chips * count):
            for j in range(rows // PAD):
                at = b * rows + j * PAD
                tap, channel = at // half, at % half
                block = half_ref[b // count, b % count, which, j * PAD : (j + 1) * PAD]
                buf_ref[which, tap, channel : channel + PAD, :] = block.astype(F32)
        copies.append(pltpu.make_async_copy(buf_ref.at[which], out_hbm.at[:, place, :], sems.at[which]))
        copies[-1].start()
    for copy in copies:
        copy.wait()


SPACES = {"s": pltpu.SMEM, "v": pltpu.VMEM, "h": pltpu.HBM}


def call(kernel, spaces, arrays, outs, scratch, vmem_mib, flops=0, nbytes=8 << 20, aliases=()):
    arrays = [
        pltpu.with_memory_space_constraint(a, pltpu.HBM) if c == "h" else a for c, a in zip(spaces, arrays)
    ]
    letters = list(zip(spaces, [*arrays, *outs]))
    specs = [jax.tree.map(lambda _, c=c: pl.BlockSpec(memory_space=SPACES[c]), a) for c, a in letters[: len(arrays)]]

    def shape_of(c, out):
        return pltpu.HBM(*out) if c == "h" else jax.ShapeDtypeStruct(*out)

    def spec_of(c, out):
        return pl.BlockSpec(memory_space=SPACES[c])

    shapes, out_specs = (
        [[f(c, o) for o in out] if isinstance(out, list) else f(c, out) for c, out in letters[len(arrays) :]]
        for f in (shape_of, spec_of)
    )
    return pl.pallas_call(
        kernel,
        out_shape=shapes,
        in_specs=specs,
        out_specs=out_specs,
        input_output_aliases=dict(aliases),
        scratch_shapes=[pltpu.SemaphoreType.DMA(s) if len(s) == 1 else pltpu.VMEM(*s) for s in scratch],
        compiler_params=pltpu.CompilerParams(vmem_limit_bytes=vmem_mib << 20),
        cost_estimate=pl.CostEstimate(flops=flops, bytes_accessed=nbytes, transcendentals=0),
    )(*arrays)


def after(x, *others):
    return lax.optimization_barrier((x, *others))[0]


def exchange(messages):
    return [messages[0]] + [swap(m, "tm", k) for k, m in enumerate(messages) if k > 0]


def scatter_sum(blocks, axis):
    return jnp.sum(lax.all_to_all(blocks, axis, 0, 0).astype(F32), axis=0).astype(BF16)


def spread(block, axis):
    return lax.all_to_all(jnp.broadcast_to(block[None], (lax.axis_size(axis), *block.shape)), axis, 0, 0)


def swap(x, axis, bit):
    return lax.ppermute(x, axis, [(i, i ^ bit) for i in range(lax.axis_size(axis))])


def sum_over_tm(x):
    count = lax.axis_size("tm")
    parts = [x.astype(F32)] + [swap(x, "tm", k).astype(F32) for k in range(1, count)]
    while len(parts) > 1:
        half = len(parts) // 2
        parts = [a + b for a, b in zip(parts[:half], parts[half:])]
    return parts[0]


def gather_rows(x, first, rest):
    x = jnp.concatenate([x, swap(x, "core", 1)])
    for b in range((lax.axis_size("chip") - 1).bit_length()):
        x = after(x, first if b == 0 else rest)
        x = jnp.concatenate([x, swap(x, "chip", 1 << b)])
    return x


def per_device(tokens, lengths, style, fc1_weight, fc1_bias, conv1_kernel, fc2_weight, fc2_bias, conv2_kernel,
               conv2_bias, out_grad):
    rows, frames, width = tokens.shape
    count, chips = lax.axis_size("tm"), lax.axis_size("chip")
    padded = frames + 2 * PAD
    affine1 = jnp.einsum("rsk,kc->rsc", style, fc1_weight, preferred_element_type=F32) + fc1_bias.astype(F32)
    affine2 = jnp.einsum("rsk,kc->rsc", style, fc2_weight, preferred_element_type=F32) + fc2_bias.astype(F32)
    kernel1, kernel2 = (k.reshape(3 * width, width) for k in (conv1_kernel, conv2_kernel))

    own, wide = ((rows, frames, width), BF16), ((rows, padded, width), BF16)
    hid, taps, kernel = ((rows, padded, width), F32), ((rows, frames, 3 * width), BF16), ((3 * width, width), BF16)
    sums, msg, half = ((rows, 8, width), F32), ((2 * rows, width), F32), ((3 * width // 2, width), BF16)
    acc, tab = ((8, 8, width), F32), ((16, 8, width), F32)
    buf, xs = ((padded, width), F32), ((padded, 3 * width), BF16)
    products = ((3, padded, width), F32)
    flops = 2 * rows * frames * 3 * width * width

    tok, w1, st1, msg1 = call(
        token_sums_kernel, "shhh" + "vvvv", (lengths, tokens, out_grad, kernel1),
        [own, kernel, sums, [((EDGE, width), F32)] * count],
        [((rows, PAD, width), BF16), ((rows, PAD, width), BF16), acc, (3,), (rows,)], SMALL,
    )
    rx1 = exchange(msg1)
    low1, hidden, st2, msg2, og, w2 = call(
        first_half_kernel, "svvvvvhh" + "vvvvvv", (lengths, tok, st1, rx1, affine1, w1, out_grad, kernel2),
        [wide, hid, sums, msg, own, kernel], [products, tab, acc, (2,)], SMALL, flops,
    )
    rx2 = exchange([msg2] * count)
    gs2, grad_low2, bias_part = call(
        branch_grad_kernel, "svvv" + "vvv", (lengths, og, rx1, w2), [taps, wide, ((8, width), F32)], [buf, xs], SMALL, flops,
    )
    low2, da2, gst2, msg3 = call(
        second_norm_kernel, "svvvvv" + "vvvv", (lengths, hidden, grad_low2, st2, rx2, affine2),
        [wide, wide, sums, msg], [tab, acc], SMALL,
    )
    rx3 = exchange([msg3] * count)

    half_acc = ((width // 2, 3 * width), F32)
    send2, low2_hbm = call(
        functools.partial(kernel_grad_kernel, False, PAD), "vv" + "vh", (low2, gs2), [half, wide], [half_acc, (1,)], SMALL,
    )
    got2 = swap(send2, "core", 1)
    (keep2,) = call(
        functools.partial(kernel_grad_kernel, True, PAD), "vv" + "v", (low2, after(gs2, send2)), [half], [half_acc], SMALL,
    )
    half2 = (got2.astype(F32) + after(keep2, *rx3).astype(F32)).astype(BF16)
    grad_hidden, gs1, send1, affine_part2 = call(
        hidden_grad_kernel, "svvvvvvvv" + "hvvv",
        (lengths, low1, after(da2, half2), hidden, st2, rx2, gst2, rx3, affine2),
        [wide, taps, half, ((4 * rows, 2 * width), F32)], [wide, buf, tab, half_acc, (rows,)], SMALL, flops,
    )
    got1 = swap(send1, "core", 1)
    (keep1,) = call(
        functools.partial(kernel_grad_kernel, True, PAD), "vv" + "v", (low1, after(gs1, send1)), [half], [half_acc], SMALL,
    )
    half1 = (got1.astype(F32) + keep1.astype(F32)).astype(BF16)
    both = jnp.concatenate([h.reshape(chips, count, 1, -1, width) for h in (half2, half1)], axis=2)
    both = both.reshape(chips, -1, width)
    grad_hidden = after(grad_hidden, both)
    both = scatter_sum(both, "chip").reshape(count, -1, width)

    da1, gst1, last_part = call(
        first_norm_grad_kernel, "shhhvvvvv" + "hvv",
        (lengths, grad_hidden, kernel1, tokens, st1, rx1, affine1, affine_part2, bias_part),
        [own, sums, ((4 * rows, 4 * width), BF16)],
        [wide, kernel, own, own, ((frames, width), F32), products, tab, acc, ((4 * rows, 4 * width), F32),
         (1 + 2 * rows,), (rows,)],
        LARGE, flops,
    )
    last = sum_over_tm(last_part)
    both = after(both, da1, last)
    affine_grads, unscattered = last.astype(BF16), both
    both = scatter_sum(both, "tm")
    scattered = both
    (block_out,) = call(
        block_out_kernel, "shhhv" + "h", (lengths, low2_hbm, after(tokens, both), kernel2, conv2_bias.reshape(1, width)), [own],
        [wide, own, kernel, products, own, (1 + 2 * rows,), (rows,)], LARGE, flops,
    )
    both = spread(both, "tm")
    (input_grad,) = call(
        input_grad_kernel, "shhhvvvvv" + "h", (lengths, out_grad, after(da1, both), tokens, st1, rx1, gst1, last, affine1), [own],
        [own, own, own, tab, own, (3 * rows,), (rows,)], LARGE,
    )
    mine = affine_grads.reshape(rows, 4, 4 * width)[:, :SEGS].reshape(rows * SEGS, 4 * width)
    style_grad = lax.dot_general(
        mine[:, : 2 * width], fc1_weight, (((1,), (1,)), ((), ())), preferred_element_type=F32
    ) + lax.dot_general(mine[:, 2 * width :], fc2_weight, (((1,), (1,)), ((), ())), preferred_element_type=F32)
    style_grad = style_grad.reshape(style.shape)
    style_pad = jnp.pad(style, ((0, 0), (0, 1), (0, 0))).reshape(rows * 4, -1)
    gathered = gather_rows(jnp.concatenate([affine_grads, style_pad], axis=1), unscattered, scattered)
    both = spread(after(both, block_out, gathered), "chip")
    fc_shape, bias_shape = ((style.shape[2], 2 * width), F32), ((1, 2 * width), F32)
    fc1_grad, fc2_grad, fc1_bias_grad, fc2_bias_grad, conv2_bias_grad = call(
        projection_grad_kernel, "v" + "hhvvv", (gathered,), [fc_shape, fc_shape, bias_shape, bias_shape, ((1, width), F32)],
        [(gathered.shape, BF16), ((style.shape[2], 4 * width), F32), (2,)], SMALL,
    )
    fc1_bias_grad, fc2_bias_grad, conv2_bias_grad = (
        b.reshape(b.shape[1]) for b in (fc1_bias_grad, fc2_bias_grad, conv2_bias_grad)
    )

    both = both.reshape(chips, count, 2, -1, width)
    both, input_grad, *small = lax.optimization_barrier(
        (both, input_grad, style_grad, fc1_grad, fc2_grad, fc1_bias_grad, fc2_bias_grad, conv2_bias_grad)
    )
    style_grad, fc1_grad, fc2_grad, fc1_bias_grad, fc2_bias_grad, conv2_bias_grad = small
    other = swap(both, "core", 1)
    if both.shape[3] % PAD == 0:
        conv_shape = ((3, width, width), F32)
        buffers = [((2, 3, width // 2, width), F32), (2,)]
        sums_own = call(
            functools.partial(assemble_kernel, True), "v" + "hh", (both,), [conv_shape, conv_shape], buffers, SMALL,
        )
        conv2_sum, conv1_sum = call(
            functools.partial(assemble_kernel, False), "vhh" + "hh", (other, *sums_own), [conv_shape, conv_shape], buffers,
            SMALL, aliases=((1, 0), (2, 1)),
        )
    else:
        first = lax.axis_index("core") == 0
        halves = [jnp.where(first, both, other), jnp.where(first, other, both)]
        halves = [jnp.moveaxis(h, 2, 0).reshape(2, 3, width // 2, width) for h in halves]
        conv2_sum, conv1_sum = jnp.concatenate(halves, axis=2).astype(F32)
    return (
        block_out, input_grad, style_grad, fc1_grad, fc1_bias_grad, conv1_sum, fc2_grad, fc2_bias_grad, conv2_sum,
        conv2_bias_grad,
    )


def solution(mesh):
    chips = mesh.shape["dp"] // 2
    mesh = Mesh(mesh.devices.reshape(chips, 2, mesh.shape["tm"]), ("chip", "core", "tm"))
    dp = ("chip", "core")
    return jax.shard_map(
        per_device,
        mesh=mesh,
        in_specs=(
            P(dp, "tm", None),
            P(dp, None),
            P(dp, None, None),
            P(),
            P(),
            P(),
            P(),
            P(),
            P(),
            P(),
            P(dp, "tm", None),
        ),
        out_specs=(
            P(dp, "tm", None),
            P(dp, "tm", None),
            P(dp, None, None),
            P(),
            P(),
            P(),
            P(),
            P(),
            P(),
            P(),
        ),
        check_vma=False,
    )
```

```python
import functools

import jax
import jax.numpy as jnp
from jax import lax
from jax.experimental import pallas as pl
from jax.experimental.pallas import tpu as pltpu
from jax.sharding import Mesh, PartitionSpec as P

EPSILON = 1e-05
ROOT_HALF = 0.7071067811865476
SEGS = 3
PAD = 16
CHUNK = 32
EDGE = 8 + 16
F32 = jnp.float32
BF16 = jnp.bfloat16
SMALL, LARGE = 20, 30


class Row:
    def __init__(self, len_ref, r, frames):
        self.frames = frames
        self.z = lax.axis_index("tm")
        self.counts = [len_ref[r, s] for s in range(SEGS)]
        l0, l1, l2 = self.counts
        start = -self.z * frames
        e0 = start + l0
        e1 = e0 + l1
        e2 = e1 + l2
        self.begins = [start, e0, e1]
        self.ends = [e0, e1, e2]
        self.long_at = jnp.where(l0 >= jnp.maximum(l1, l2), 0, jnp.where(l1 >= l2, 1, 2))
        self.long_begin = self.of_long(self.begins)
        self.long_end = self.of_long(self.ends)

    def of_long(self, values):
        return jnp.where(
            self.long_at == 0, values[0], jnp.where(self.long_at == 1, values[1], values[2])
        )

    def segment(self, t):
        return sum((t >= e).astype(jnp.int32) for e in self.ends)

    def chunks(self, uniform_fn, mixed_fn, sums=None, acc_ref=None, ends=None):
        for t0 in range(0, self.frames, CHUNK):
            uniform_fn(t0, self.segment(t0))
        if sums is not None:
            sums.put(acc_ref)
        self.mixed(mixed_fn, ends)

    def mixed(self, fn, ends=None):
        for end in ends or self.ends:

            @pl.when(jnp.logical_and(jnp.logical_and(end > 0, end < self.frames), end % CHUNK != 0))
            def _(end=end):
                fn(pl.multiple_of((end // CHUNK) * CHUNK, CHUNK))


def frame_ids(t0, rows, width):
    return t0 + lax.broadcasted_iota(jnp.int32, (rows, width), 0)


def pick(tab_ref, base, t, row):
    value = tab_ref[base, 0:1, :]
    for s in range(SEGS):
        value = jnp.where(t >= row.ends[s], tab_ref[base + s + 1, 0:1, :], value)
    return value


def entry(tab_ref, index, rows=CHUNK):
    value = tab_ref[index]
    return jnp.broadcast_to(value[None], (rows // 8, *value.shape)).reshape(rows, value.shape[1])


def put_entry(tab_ref, index, value):
    tab_ref[index] = jnp.broadcast_to(value, tab_ref.shape[1:])


def put_table(tab_ref, base, values):
    for s in range(SEGS):
        put_entry(tab_ref, base + s, values[s])
    put_entry(tab_ref, base + SEGS, jnp.zeros_like(values[0]))


def fold(x):
    return jnp.sum(x.reshape(x.shape[0] // 8, 8, x.shape[1]), axis=0)


def add_masked_sums(acc_ref, t, row, first, second):
    for s in range(SEGS):
        inside = jnp.logical_and(t >= row.begins[s], t < row.ends[s])
        acc_ref[s] += fold(jnp.where(inside, first, 0.0))
        acc_ref[4 + s] += fold(jnp.where(inside, second, 0.0))


def put_sums(acc_ref, st_ref, msg_refs, row, r):
    for s in range(SEGS):
        for k in range(2):
            st_ref[r, pl.ds(SEGS * k + s, 1), :] = jnp.sum(acc_ref[4 * k + s], axis=0, keepdims=True)
    for k in range(2):
        value = jnp.sum(acc_ref[4 * k + row.long_at], axis=0, keepdims=True)
        for ref in msg_refs:
            ref[pl.ds(2 * r + k, 1), :] = value


def sums_of(row, r, st_ref, rx_refs, s):
    out = []
    for k in range(2):
        total = sum(ref[pl.ds(2 * r + k, 1), :] for ref in rx_refs)
        local = st_ref[r, SEGS * k + s : SEGS * k + s + 1, :]
        out.append(jnp.where(row.long_at == s, total, local))
    return out


def norm_of(row, r, st_ref, rx_ref, aff_ref, s):
    width = st_ref.shape[2]
    first, second = sums_of(row, r, st_ref, rx_ref, s)
    count = jnp.full((1, width), row.counts[s].astype(F32))
    mean = first / count
    rstd = lax.rsqrt(second / count - mean * mean + EPSILON)
    affine = aff_ref[r, s : s + 1, :]
    return mean, rstd, 1.0 + affine[:, :width], affine[:, width:], count


def put_forward(row, r, st_ref, rx_ref, aff_ref, tab_ref):
    scales, shifts = [], []
    for s in range(SEGS):
        mean, rstd, gain, beta, _ = norm_of(row, r, st_ref, rx_ref, aff_ref, s)
        scales.append(gain * rstd)
        shifts.append(beta - mean * scales[-1])
    put_table(tab_ref, 0, scales)
    put_table(tab_ref, 4, shifts)
    put_entry(tab_ref, 12, row.of_long(scales))
    put_entry(tab_ref, 13, row.of_long(shifts))


def put_backward(row, r, st_ref, rx_ref, gst_ref, grx_ref, aff_ref, tab_ref):
    parts = [[], [], []]
    for s in range(SEGS):
        mean, rstd, gain, _, count = norm_of(row, r, st_ref, rx_ref, aff_ref, s)
        if isinstance(grx_ref, (list, tuple)):
            shift, scale = sums_of(row, r, gst_ref, grx_ref, s)
            scale = rstd * (scale - mean * shift)
        else:
            width = mean.shape[1]
            total = grx_ref[pl.ds(4 * r + s, 1), : 2 * width] + grx_ref[pl.ds(4 * r + SEGS, 1), 2 * width :]
            shift, local = gst_ref[r, s : s + 1, :], gst_ref[r, SEGS + s : SEGS + s + 1, :]
            scale = jnp.where(row.long_at == s, total[:, :width], rstd * (local - mean * shift))
            shift = jnp.where(row.long_at == s, total[:, width:], shift)
        mean_g = gain * shift / count
        slope = rstd * rstd * (gain * scale / count)
        parts[0].append(gain * rstd)
        parts[1].append(-slope)
        parts[2].append(slope * mean - rstd * mean_g)
    for k in range(3):
        put_table(tab_ref, 4 * k, parts[k])
        put_entry(tab_ref, 12 + k, row.of_long(parts[k]))


def put_affine_grads(row, r, st_ref, rx_ref, gst_ref, aff_ref, out_ref, at):
    width = st_ref.shape[2]
    for s in range(SEGS):
        mean, rstd, _, _, _ = norm_of(row, r, st_ref, rx_ref, aff_ref, s)
        shift = gst_ref[r, s : s + 1, :]
        scale = rstd * (gst_ref[r, SEGS + s : SEGS + s + 1, :] - mean * shift)
        out_ref[pl.ds(4 * r + s, 1), at : at + width] = scale
        out_ref[pl.ds(4 * r + s, 1), at + width : at + 2 * width] = shift


def silu(a):
    half = 0.5 * a
    return half + half * jnp.tanh(half)


def silu_and_slope(a):
    gate = 0.5 + 0.5 * jnp.tanh(0.5 * a)
    low = a * gate
    return low, gate + low * (1.0 - gate)


def halo_tile(row, frames, width, left):
    t = frame_ids(-PAD if left else frames, PAD, width)
    near = jnp.logical_and(t >= -2, t < frames + 2)
    inside = jnp.logical_and(t >= row.long_begin, t < row.long_end)
    return t, jnp.logical_and(near, inside)


def edge_tile(rx_refs, row, r, t, at, left):
    last = len(rx_refs) - 1
    neighbour = jnp.maximum(row.z - 1, 0) if left else jnp.minimum(row.z + 1, last)
    edges = []
    for i in range(2):
        value, k = rx_refs[1][pl.ds(8 + 4 * r + at + i, 1), :], 3
        while k <= last:
            value = jnp.where((row.z ^ neighbour) == k, rx_refs[k][pl.ds(8 + 4 * r + at + i, 1), :], value)
            k = 2 * k + 1
        edges.append(value)
    second = -1 if left else row.frames + 1
    return jnp.where(t == second, edges[1], edges[0])


def stack_taps(buf_ref, xs_ref, row, frames, forward, halo, low_ref=None, r=None):
    width = buf_ref.shape[1]
    before_at, after_at = (0, 2 * width) if forward else (2 * width, 0)
    base = PAD if halo else 0
    for i in range(frames // CHUNK):
        o, d = PAD + i * CHUNK, base + i * CHUNK
        centre = buf_ref[o : o + CHUNK, :].astype(BF16)
        xs_ref[d : d + CHUNK, width : 2 * width] = centre
        xs_ref[d : d + CHUNK, before_at : before_at + width] = buf_ref[o - 1 : o - 1 + CHUNK, :].astype(BF16)
        xs_ref[d : d + CHUNK, after_at : after_at + width] = buf_ref[o + 1 : o + 1 + CHUNK, :].astype(BF16)
        if low_ref is not None:
            low_ref[r, i * CHUNK : (i + 1) * CHUNK, :] = centre
    if halo:
        end = PAD + frames
        left, right = buf_ref[0:PAD, :], buf_ref[end : end + PAD, :]
        xs_ref[0:PAD, width : 2 * width] = left.astype(BF16)
        xs_ref[end : end + PAD, width : 2 * width] = right.astype(BF16)
        xs_ref[0:PAD, before_at : before_at + width] = pltpu.roll(left, 1, 0).astype(BF16)
        xs_ref[end : end + PAD, before_at : before_at + width] = buf_ref[end - 1 : end - 1 + PAD, :].astype(BF16)
        xs_ref[0:PAD, after_at : after_at + width] = buf_ref[1 : 1 + PAD, :].astype(BF16)
        xs_ref[end : end + PAD, after_at : after_at + width] = pltpu.roll(right, PAD - 1, 0).astype(BF16)
    for end in row.ends[:2]:
        for at, t in ((before_at, end), (after_at, end - 1)):

            @pl.when(jnp.logical_and(t >= 0, t < frames))
            def _(at=at, t=t):
                tile = pl.multiple_of((t // PAD) * PAD, PAD)
                rows = pl.ds(base + tile, PAD)
                value = xs_ref[rows, at : at + width].astype(F32)
                keep = frame_ids(tile, PAD, width) != t
                xs_ref[rows, at : at + width] = jnp.where(keep, value, 0.0).astype(BF16)


class Sums:
    def __init__(self, row, width):
        self.row = row
        self.parts = [[jnp.zeros((8, width), F32)] * SEGS for _ in range(2)]

    def add(self, t0, rows, first, second):
        folded = (fold(first), fold(second))
        for s in range(SEGS):
            fills = jnp.logical_and(t0 >= self.row.begins[s], t0 + rows <= self.row.ends[s])
            weight = jnp.where(fills, 1.0, 0.0)
            for k in range(2):
                self.parts[k][s] = self.parts[k][s] + folded[k] * weight

    def put(self, acc_ref):
        for k in range(2):
            for s in range(SEGS):
                acc_ref[4 * k + s] = self.parts[k][s]


def rows_moved(ref, at, rows, step):
    if at - step < 0 or at + rows - step > ref.shape[0]:
        return pltpu.roll(ref[at : at + rows, :], step % rows, 0)
    return ref[at - step : at - step + rows, :]


def tap_sum(z_ref, row, t0, rows, first=0, last=2):
    at, t = PAD + t0, frame_ids(t0, rows, z_ref.shape[2])
    starts = functools.reduce(jnp.logical_or, [t == end for end in row.ends])
    stops = functools.reduce(jnp.logical_or, [t == end - 1 for end in row.ends])
    before = jnp.where(starts, 0.0, rows_moved(z_ref.at[first], at, rows, 1))
    after = jnp.where(stops, 0.0, rows_moved(z_ref.at[last], at, rows, -1))
    return before + z_ref[1, at : at + rows, :] + after


def put_products(x, w_ref, z_ref, transposed=False):
    width = x.shape[1]
    dims = (((1,), (1 if transposed else 0,)), ((), ()))
    for k in range(3):
        tap = w_ref[k * width : (k + 1) * width, :]
        z_ref[k] = lax.dot_general(x, tap, dims, preferred_element_type=F32)


def times_transposed(xs, w_ref, width):
    out = None
    for k in range(3):
        part = lax.dot_general(
            xs[:, k * width : (k + 1) * width],
            w_ref[k * width : (k + 1) * width, :],
            (((1,), (1,)), ((), ())),
            preferred_element_type=F32,
        )
        out = part if out is None else out + part
    return out


def for_rows(len_ref, rows, frames, body):
    def step(r, carry):
        body(r, Row(len_ref, r, frames))
        return carry

    lax.fori_loop(0, rows, step, 0)


def token_sums_kernel(len_ref, tok_hbm, og_hbm, w_hbm, tok_ref, w_ref, st_ref, msg_refs, head_ref, tail_ref, acc_ref,
                      sems, row_sems):
    rows, frames, width = tok_ref.shape

    def row_copy(r):
        return pltpu.make_async_copy(tok_hbm.at[r], tok_ref.at[r], row_sems.at[r])

    for r in range(rows):
        row_copy(r).start()
    edges = (
        pltpu.make_async_copy(og_hbm.at[:, pl.ds(0, PAD), :], head_ref, sems.at[0]),
        pltpu.make_async_copy(og_hbm.at[:, pl.ds(frames - PAD, PAD), :], tail_ref, sems.at[1]),
    )
    for copy in edges:
        copy.start()
    kernel_copy = pltpu.make_async_copy(w_hbm, w_ref, sems.at[2])
    kernel_copy.start()
    for copy in edges:
        copy.wait()

    def body(r, row):
        row_copy(r).wait()
        sums = Sums(row, width)

        def uniform(t0, s):
            v = tok_ref[r, pl.ds(t0, CHUNK), :].astype(F32)
            sums.add(t0, CHUNK, v, v * v)

        def mixed(t0):
            v = tok_ref[r, pl.ds(t0, CHUNK), :].astype(F32)
            add_masked_sums(acc_ref, frame_ids(t0, CHUNK, width), row, v, v * v)

        row.chunks(uniform, mixed, sums, acc_ref)
        put_sums(acc_ref, st_ref, msg_refs, row, r)
        for j, (head, tail) in enumerate(
            ((tok_ref[r, 0:PAD, :], tok_ref[r, frames - PAD : frames, :]), (head_ref[r], tail_ref[r]))
        ):
            first, last = head.astype(F32), tail.astype(F32)
            for i in range(2):
                to_left, to_right = first[i : i + 1, :], last[PAD - 2 + i : PAD - 1 + i, :]
                for k, ref in enumerate(msg_refs):
                    value = jnp.where(row.z < row.z ^ k, to_right, to_left)
                    ref[pl.ds(8 + 4 * r + 2 * j + i, 1), :] = value

    for_rows(len_ref, rows, frames, body)
    kernel_copy.wait()


def first_half_kernel(len_ref, tok_ref, st_ref, rx_ref, aff_ref, w_ref, og_hbm, w2_hbm, low_ref,
                      hid_ref, st2_ref, msg_ref, og_ref, w2_ref, z_ref, tab_ref, acc_ref, sems):
    rows, frames, width = tok_ref.shape
    copies = (
        pltpu.make_async_copy(og_hbm, og_ref, sems.at[0]),
        pltpu.make_async_copy(w2_hbm, w2_ref, sems.at[1]),
    )
    for copy in copies:
        copy.start()

    def body(r, row):
        put_forward(row, r, st_ref, rx_ref, aff_ref, tab_ref)

        def uniform(t0, s):
            v = tok_ref[r, pl.ds(t0, CHUNK), :].astype(F32)
            low = silu(v * entry(tab_ref, s) + entry(tab_ref, 4 + s))
            low_ref[r, pl.ds(PAD + t0, CHUNK), :] = low.astype(BF16)

        def mixed(t0):
            t = frame_ids(t0, CHUNK, width)
            v = tok_ref[r, pl.ds(t0, CHUNK), :].astype(F32)
            low = silu(v * pick(tab_ref, 0, t, row) + pick(tab_ref, 4, t, row))
            low_ref[r, pl.ds(PAD + t0, CHUNK), :] = jnp.where(t < row.ends[2], low, 0.0).astype(BF16)

        row.chunks(uniform, mixed)
        for left in (True, False):
            t, valid = halo_tile(row, frames, width, left)
            low = silu(edge_tile(rx_ref, row, r, t, 0, left) * tab_ref[12, 0:1, :] + tab_ref[13, 0:1, :])
            at = 0 if left else PAD + frames
            low_ref[r, at : at + PAD, :] = jnp.where(valid, low, 0.0).astype(BF16)
        put_products(low_ref[r], w_ref, z_ref)
        sums = Sums(row, width)
        for t0 in range(0, frames, CHUNK):
            v = tap_sum(z_ref, row, t0, CHUNK)
            hid_ref[r, PAD + t0 : PAD + t0 + CHUNK, :] = v
            sums.add(t0, CHUNK, v, v * v)
        sums.put(acc_ref)
        for t0 in (-PAD, frames):
            hid_ref[r, PAD + t0 : 2 * PAD + t0, :] = tap_sum(z_ref, row, t0, PAD)

        def mixed_sums(t0):
            v = hid_ref[r, pl.ds(PAD + t0, CHUNK), :]
            add_masked_sums(acc_ref, frame_ids(t0, CHUNK, width), row, v, v * v)

        row.mixed(mixed_sums)
        put_sums(acc_ref, st2_ref, [msg_ref], row, r)

    for_rows(len_ref, rows, frames, body)
    for copy in copies:
        copy.wait()


def branch_grad_kernel(len_ref, og_ref, rx_ref, w_ref, gs_ref, q_ref, bias_ref, buf_ref, xs_ref):
    rows, frames, width = og_ref.shape
    bias_ref[...] = jnp.zeros_like(bias_ref)

    def body(r, row):
        def put(t0, g, weight):
            g = g.astype(BF16).astype(F32)
            buf_ref[pl.ds(PAD + t0, CHUNK), :] = g
            bias_ref[...] += fold(g) * weight

        def uniform(t0, s):
            scale = jnp.where(s < SEGS, ROOT_HALF, 0.0)
            g = og_ref[r, pl.ds(t0, CHUNK), :].astype(F32) * scale
            put(t0, g, jnp.where(t0 + CHUNK <= row.ends[2], 1.0, 0.0))

        def mixed(t0):
            t = frame_ids(t0, CHUNK, width)
            g = og_ref[r, pl.ds(t0, CHUNK), :].astype(F32) * ROOT_HALF
            put(t0, jnp.where(t < row.ends[2], g, 0.0), 1.0)

        row.chunks(uniform, mixed, ends=row.ends[2:])
        for left in (True, False):
            t, valid = halo_tile(row, frames, width, left)
            at = 0 if left else PAD + frames
            g = edge_tile(rx_ref, row, r, t, 2, left) * ROOT_HALF
            buf_ref[at : at + PAD, :] = jnp.where(valid, g, 0.0)
        stack_taps(buf_ref, xs_ref, row, frames, False, True)
        gs_ref[r] = xs_ref[PAD : PAD + frames, :]
        q_ref[r] = times_transposed(xs_ref[...], w_ref, width).astype(BF16)

    for_rows(len_ref, rows, frames, body)


def second_norm_kernel(len_ref, hid_ref, q_ref, st_ref, rx_ref, aff_ref, low_ref, da_ref, gst_ref, msg_ref,
                       tab_ref, acc_ref):
    rows, padded, width = hid_ref.shape
    frames = padded - 2 * PAD

    def body(r, row):
        put_forward(row, r, st_ref, rx_ref, aff_ref, tab_ref)
        sums = Sums(row, width)

        def uniform(t0, s):
            at = pl.ds(PAD + t0, CHUNK)
            v = hid_ref[r, at, :]
            low, slope = silu_and_slope(v * entry(tab_ref, s) + entry(tab_ref, 4 + s))
            da = slope * q_ref[r, at, :].astype(F32)
            low_ref[r, at, :] = low.astype(BF16)
            da_ref[r, at, :] = da.astype(BF16)
            sums.add(t0, CHUNK, da, da * v)

        def mixed(t0):
            at = pl.ds(PAD + t0, CHUNK)
            t = frame_ids(t0, CHUNK, width)
            live = t < row.ends[2]
            v = hid_ref[r, at, :]
            low, slope = silu_and_slope(v * pick(tab_ref, 0, t, row) + pick(tab_ref, 4, t, row))
            da = slope * q_ref[r, at, :].astype(F32)
            low_ref[r, at, :] = jnp.where(live, low, 0.0).astype(BF16)
            da_ref[r, at, :] = jnp.where(live, da, 0.0).astype(BF16)
            add_masked_sums(acc_ref, t, row, da, da * v)

        row.chunks(uniform, mixed, sums, acc_ref)
        for left in (True, False):
            t, valid = halo_tile(row, frames, width, left)
            at = 0 if left else PAD + frames
            v = hid_ref[r, at : at + PAD, :]
            low, slope = silu_and_slope(v * tab_ref[12, 0:1, :] + tab_ref[13, 0:1, :])
            da = slope * q_ref[r, at : at + PAD, :].astype(F32)
            low_ref[r, at : at + PAD, :] = jnp.where(valid, low, 0.0).astype(BF16)
            da_ref[r, at : at + PAD, :] = jnp.where(valid, da, 0.0).astype(BF16)
        put_sums(acc_ref, gst_ref, [msg_ref], row, r)

    for_rows(len_ref, rows, frames, body)


class Loads:
    def __init__(self, rows, sems, whole, by_row):
        count = len(whole)
        self.whole = [pltpu.make_async_copy(a, b, sems.at[i]) for i, (a, b) in enumerate(whole)]
        self.row = lambda r: [
            pltpu.make_async_copy(a.at[r], b.at[r], sems.at[count + i * rows + r]) for i, (a, b) in enumerate(by_row)
        ]
        for copy in (*self.row(0), *self.whole):
            copy.start()
        for r in range(1, rows):
            for copy in self.row(r):
                copy.start()

    def wait(self, r):
        for copy in self.row(r):
            copy.wait()

        @pl.when(r == 0)
        def _():
            for copy in self.whole:
                copy.wait()


def block_out_kernel(len_ref, low_hbm, tok_hbm, w_hbm, bias_ref, out_hbm, low_ref, tok_ref, w_ref, z_ref, out_ref,
                     sems, row_sems):
    rows, frames, width = tok_ref.shape
    loads = Loads(rows, sems, [(w_hbm, w_ref)], [(low_hbm, low_ref), (tok_hbm, tok_ref)])

    def row_copy(r):
        return pltpu.make_async_copy(out_ref.at[r], out_hbm.at[r], row_sems.at[r])

    def body(r, row):
        loads.wait(r)
        bias = bias_ref[...].astype(F32)
        put_products(low_ref[r], w_ref, z_ref)
        for t0 in range(0, frames, CHUNK):
            live = frame_ids(t0, CHUNK, width) < row.ends[2]
            branch = tap_sum(z_ref, row, t0, CHUNK) + jnp.where(live, bias, 0.0)
            out = (tok_ref[r, t0 : t0 + CHUNK, :].astype(F32) + branch) * ROOT_HALF
            out_ref[r, t0 : t0 + CHUNK, :] = out.astype(BF16)
        row_copy(r).start()

    for_rows(len_ref, rows, frames, body)
    for r in range(rows):
        row_copy(r).wait()


def half_of_grad(low_ref, gs_ref, r, half, first_frame):
    frames, width = gs_ref.shape[1], low_ref.shape[2] // 2
    u = low_ref[r, first_frame : first_frame + frames, pl.ds(pl.multiple_of(half * width, width), width)]
    return lax.dot_general(u, gs_ref[r], (((0,), (0,)), ((), ())), preferred_element_type=F32)


def put_half(acc_ref, out_ref):
    half, width = acc_ref.shape[0], acc_ref.shape[1] // 3
    for k in range(3):
        out_ref[k * half : (k + 1) * half, :] = acc_ref[:, k * width : (k + 1) * width].astype(BF16)


def kernel_grad_kernel(own, first_frame, low_ref, gs_ref, out_ref, *refs):
    acc_ref = refs[-1] if own else refs[1]
    if not own:
        store = pltpu.make_async_copy(low_ref, refs[0], refs[2].at[0])
        store.start()
    core = lax.axis_index("core")
    half = core if own else 1 - core
    acc_ref[...] = half_of_grad(low_ref, gs_ref, 0, half, first_frame)

    def step(r, carry):
        acc_ref[...] += half_of_grad(low_ref, gs_ref, r, half, first_frame)
        return carry

    lax.fori_loop(1, low_ref.shape[0], step, 0)
    put_half(acc_ref, out_ref)
    if not own:
        store.wait()


def hidden_grad_kernel(len_ref, low_ref, da_ref, hid_ref, st_ref, rx_ref, gst_ref, grx_ref, aff_ref,
                       g_hbm, gs_ref, send_ref, part_ref, g_ref, buf_ref, tab_ref, acc_ref, row_sems):
    rows, frames, width = low_ref.shape[0], gs_ref.shape[1], low_ref.shape[2]
    part_ref[...] = jnp.zeros_like(part_ref)
    acc_ref[...] = jnp.zeros_like(acc_ref)

    def row_copy(r):
        return pltpu.make_async_copy(g_ref.at[r], g_hbm.at[r], row_sems.at[r])

    def body(r, row):
        put_affine_grads(row, r, st_ref, rx_ref, gst_ref, aff_ref, part_ref, 0)
        put_backward(row, r, st_ref, rx_ref, gst_ref, grx_ref, aff_ref, tab_ref)

        def uniform(t0, s):
            at = pl.ds(PAD + t0, CHUNK)
            buf_ref[at, :] = (
                da_ref[r, at, :].astype(F32) * entry(tab_ref, s)
                + hid_ref[r, at, :] * entry(tab_ref, 4 + s)
                + entry(tab_ref, 8 + s)
            )

        def mixed(t0):
            at = pl.ds(PAD + t0, CHUNK)
            t = frame_ids(t0, CHUNK, width)
            grad = (
                da_ref[r, at, :].astype(F32) * pick(tab_ref, 0, t, row)
                + hid_ref[r, at, :] * pick(tab_ref, 4, t, row)
                + pick(tab_ref, 8, t, row)
            )
            buf_ref[at, :] = jnp.where(t < row.ends[2], grad, 0.0)

        row.chunks(uniform, mixed)
        for left in (True, False):
            t, valid = halo_tile(row, frames, width, left)
            at = 0 if left else PAD + frames
            grad = (
                da_ref[r, at : at + PAD, :].astype(F32) * tab_ref[12, 0:1, :]
                + hid_ref[r, at : at + PAD, :] * tab_ref[13, 0:1, :]
                + tab_ref[14, 0:1, :]
            )
            buf_ref[at : at + PAD, :] = jnp.where(valid, grad, 0.0)
        g_ref[r] = buf_ref[...].astype(BF16)
        stack_taps(buf_ref, gs_ref.at[r], row, frames, False, False)
        row_copy(r).start()
        acc_ref[...] += half_of_grad(low_ref, gs_ref, r, 1 - lax.axis_index("core"), PAD)

    for_rows(len_ref, rows, frames, body)
    put_half(acc_ref, send_ref)
    for r in range(rows):
        row_copy(r).wait()


def first_norm_grad_kernel(len_ref, g_hbm, w_hbm, tok_hbm, st_ref, rx_ref, aff_ref, part2_ref, bias_ref,
                           da_hbm, gst_ref, out_ref, g_ref, w_ref, tok_ref, da_ref, q_ref, z_ref, tab_ref, acc_ref,
                           part_ref, sems, row_sems):
    rows, frames, width = tok_ref.shape
    loads = Loads(rows, sems, [(w_hbm, w_ref)], [(g_hbm, g_ref), (tok_hbm, tok_ref)])
    part_ref[:, : 2 * width] = jnp.zeros((part_ref.shape[0], 2 * width), F32)
    part_ref[:, 2 * width :] = part2_ref[...]
    part_ref[SEGS : SEGS + 1, :width] = jnp.sum(bias_ref[...], axis=0, keepdims=True)

    def row_copy(r):
        return pltpu.make_async_copy(da_ref.at[r], da_hbm.at[r], row_sems.at[r])

    def body(r, row):
        put_forward(row, r, st_ref, rx_ref, aff_ref, tab_ref)
        loads.wait(r)
        put_products(g_ref[r], w_ref, z_ref, True)
        for t0 in range(0, frames, CHUNK):
            q_ref[t0 : t0 + CHUNK, :] = tap_sum(z_ref, row, t0, CHUNK, 2, 0)
        sums = Sums(row, width)

        def uniform(t0, s):
            at = pl.ds(t0, CHUNK)
            v = tok_ref[r, at, :].astype(F32)
            _, slope = silu_and_slope(v * entry(tab_ref, s) + entry(tab_ref, 4 + s))
            da = slope * q_ref[at, :]
            da_ref[r, at, :] = da.astype(BF16)
            sums.add(t0, CHUNK, da, da * v)

        def mixed(t0):
            at = pl.ds(t0, CHUNK)
            t = frame_ids(t0, CHUNK, width)
            v = tok_ref[r, at, :].astype(F32)
            _, slope = silu_and_slope(v * pick(tab_ref, 0, t, row) + pick(tab_ref, 4, t, row))
            da = slope * q_ref[at, :]
            da_ref[r, at, :] = jnp.where(t < row.ends[2], da, 0.0).astype(BF16)
            add_masked_sums(acc_ref, t, row, da, da * v)

        row.chunks(uniform, mixed, sums, acc_ref)
        row_copy(r).start()
        put_sums(acc_ref, gst_ref, [], row, r)
        put_affine_grads(row, r, st_ref, rx_ref, gst_ref, aff_ref, part_ref, 0)
        value = part_ref[pl.ds(4 * r + row.long_at, 1), : 2 * width]
        part_ref[pl.ds(4 * r + SEGS, 1), 2 * width :] = value - value.astype(BF16).astype(F32)

    for_rows(len_ref, rows, frames, body)
    out_ref[...] = part_ref[...].astype(BF16)
    for r in range(rows):
        row_copy(r).wait()


def input_grad_kernel(len_ref, og_hbm, da_hbm, tok_hbm, st_ref, rx_ref, gst_ref, grx_ref, aff_ref, out_hbm,
                      og_ref, da_ref, tok_ref, tab_ref, out_ref, sems, row_sems):
    rows, frames, width = tok_ref.shape
    loads = Loads(rows, sems, [], [(og_hbm, og_ref), (da_hbm, da_ref), (tok_hbm, tok_ref)])

    def row_copy(r):
        return pltpu.make_async_copy(out_ref.at[r], out_hbm.at[r], row_sems.at[r])

    def body(r, row):
        put_backward(row, r, st_ref, rx_ref, gst_ref, grx_ref, aff_ref, tab_ref)
        loads.wait(r)

        def uniform(t0, s):
            at = pl.ds(t0, CHUNK)
            out = (
                og_ref[r, at, :].astype(F32) * ROOT_HALF
                + da_ref[r, at, :].astype(F32) * entry(tab_ref, s)
                + tok_ref[r, at, :].astype(F32) * entry(tab_ref, 4 + s)
                + entry(tab_ref, 8 + s)
            )
            out_ref[r, at, :] = out.astype(BF16)

        def mixed(t0):
            at = pl.ds(t0, CHUNK)
            t = frame_ids(t0, CHUNK, width)
            grad = (
                da_ref[r, at, :].astype(F32) * pick(tab_ref, 0, t, row)
                + tok_ref[r, at, :].astype(F32) * pick(tab_ref, 4, t, row)
                + pick(tab_ref, 8, t, row)
            )
            out = og_ref[r, at, :].astype(F32) * ROOT_HALF + jnp.where(t < row.ends[2], grad, 0.0)
            out_ref[r, at, :] = out.astype(BF16)

        row.chunks(uniform, mixed)
        row_copy(r).start()

    for_rows(len_ref, rows, frames, body)
    for r in range(rows):
        row_copy(r).wait()


def projection_grad_kernel(all_ref, fc1_hbm, fc2_hbm, bias1_ref, bias2_ref, conv_bias_ref, rows_ref, grad_ref, sems):
    device = lax.axis_index("chip") * 2 + lax.axis_index("core")
    width = conv_bias_ref.shape[1]
    for i in range(all_ref.shape[0] // PAD):
        block = pl.ds(pl.multiple_of((device ^ i) * PAD, PAD), PAD)
        rows_ref[i * PAD : (i + 1) * PAD, :] = all_ref[block, :]
    grads, styles = rows_ref[:, : 4 * width], rows_ref[:, 4 * width :]
    grad_ref[...] = lax.dot_general(styles, grads, (((0,), (0,)), ((), ())), preferred_element_type=F32)
    copies = [
        pltpu.make_async_copy(grad_ref.at[:, pl.ds(i * 2 * width, 2 * width)], out, sems.at[i])
        for i, out in enumerate((fc1_hbm, fc2_hbm))
    ]
    for copy in copies:
        copy.start()
    values = grads.astype(F32)
    of_segment = frame_ids(0, values.shape[0], values.shape[1]) % 4 < SEGS
    bias = jnp.sum(jnp.where(of_segment, values, 0.0), axis=0, keepdims=True)
    bias1_ref[...] = bias[:, : 2 * width]
    bias2_ref[...] = bias[:, 2 * width :]
    rest = jnp.where(of_segment[:, :width], 0.0, values[:, :width])
    conv_bias_ref[...] = jnp.sum(rest, axis=0, keepdims=True)
    for copy in copies:
        copy.wait()


def assemble_kernel(own, half_ref, *refs):
    out2_hbm, out1_hbm, buf_ref, sems = refs[-4:]
    chips, count, _, rows, width = half_ref.shape
    half = chips * count * rows // 3
    core = lax.axis_index("core")
    place = pl.ds(pl.multiple_of((core if own else 1 - core) * half, half), half)
    copies = []
    for which, out_hbm in enumerate((out2_hbm, out1_hbm)):
        for b in range(chips * count):
            for j in range(rows // PAD):
                at = b * rows + j * PAD
                tap, channel = at // half, at % half
                block = half_ref[b // count, b % count, which, j * PAD : (j + 1) * PAD]
                buf_ref[which, tap, channel : channel + PAD, :] = block.astype(F32)
        copies.append(pltpu.make_async_copy(buf_ref.at[which], out_hbm.at[:, place, :], sems.at[which]))
        copies[-1].start()
    for copy in copies:
        copy.wait()


SPACES = {"s": pltpu.SMEM, "v": pltpu.VMEM, "h": pltpu.HBM}


def call(kernel, spaces, arrays, outs, scratch, vmem_mib, flops=0, nbytes=8 << 20, aliases=()):
    arrays = [
        pltpu.with_memory_space_constraint(a, pltpu.HBM) if c == "h" else a for c, a in zip(spaces, arrays)
    ]
    letters = list(zip(spaces, [*arrays, *outs]))
    specs = [jax.tree.map(lambda _, c=c: pl.BlockSpec(memory_space=SPACES[c]), a) for c, a in letters[: len(arrays)]]

    def shape_of(c, out):
        return pltpu.HBM(*out) if c == "h" else jax.ShapeDtypeStruct(*out)

    def spec_of(c, out):
        return pl.BlockSpec(memory_space=SPACES[c])

    shapes, out_specs = (
        [[f(c, o) for o in out] if isinstance(out, list) else f(c, out) for c, out in letters[len(arrays) :]]
        for f in (shape_of, spec_of)
    )
    return pl.pallas_call(
        kernel,
        out_shape=shapes,
        in_specs=specs,
        out_specs=out_specs,
        input_output_aliases=dict(aliases),
        scratch_shapes=[pltpu.SemaphoreType.DMA(s) if len(s) == 1 else pltpu.VMEM(*s) for s in scratch],
        compiler_params=pltpu.CompilerParams(vmem_limit_bytes=vmem_mib << 20),
        cost_estimate=pl.CostEstimate(flops=flops, bytes_accessed=nbytes, transcendentals=0),
    )(*arrays)


def after(x, *others):
    return lax.optimization_barrier((x, *others))[0]


def exchange(messages):
    return [messages[0]] + [swap(m, "tm", k) for k, m in enumerate(messages) if k > 0]


def scatter_sum(blocks, axis):
    return jnp.sum(lax.all_to_all(blocks, axis, 0, 0).astype(F32), axis=0).astype(BF16)


def spread(block, axis):
    return lax.all_to_all(jnp.broadcast_to(block[None], (lax.axis_size(axis), *block.shape)), axis, 0, 0)


def swap(x, axis, bit):
    return lax.ppermute(x, axis, [(i, i ^ bit) for i in range(lax.axis_size(axis))])


def sum_over_tm(x):
    count = lax.axis_size("tm")
    parts = [x.astype(F32)] + [swap(x, "tm", k).astype(F32) for k in range(1, count)]
    while len(parts) > 1:
        half = len(parts) // 2
        parts = [a + b for a, b in zip(parts[:half], parts[half:])]
    return parts[0]


def gather_rows(x, first, rest):
    x = jnp.concatenate([x, swap(x, "core", 1)])
    for b in range((lax.axis_size("chip") - 1).bit_length()):
        x = after(x, first if b == 0 else rest)
        x = jnp.concatenate([x, swap(x, "chip", 1 << b)])
    return x


def per_device(tokens, lengths, style, fc1_weight, fc1_bias, conv1_kernel, fc2_weight, fc2_bias, conv2_kernel,
               conv2_bias, out_grad):
    rows, frames, width = tokens.shape
    count, chips = lax.axis_size("tm"), lax.axis_size("chip")
    padded = frames + 2 * PAD
    affine1 = jnp.einsum("rsk,kc->rsc", style, fc1_weight, preferred_element_type=F32) + fc1_bias.astype(F32)
    affine2 = jnp.einsum("rsk,kc->rsc", style, fc2_weight, preferred_element_type=F32) + fc2_bias.astype(F32)
    kernel1, kernel2 = (k.reshape(3 * width, width) for k in (conv1_kernel, conv2_kernel))

    own, wide = ((rows, frames, width), BF16), ((rows, padded, width), BF16)
    hid, taps, kernel = ((rows, padded, width), F32), ((rows, frames, 3 * width), BF16), ((3 * width, width), BF16)
    sums, msg, half = ((rows, 8, width), F32), ((2 * rows, width), F32), ((3 * width // 2, width), BF16)
    acc, tab = ((8, 8, width), F32), ((16, 8, width), F32)
    buf, xs = ((padded, width), F32), ((padded, 3 * width), BF16)
    products = ((3, padded, width), F32)
    flops = 2 * rows * frames * 3 * width * width

    tok, w1, st1, msg1 = call(
        token_sums_kernel, "shhh" + "vvvv", (pltpu.with_memory_space_constraint(lengths, pltpu.HBM), tokens, out_grad, kernel1),
        [own, kernel, sums, [((EDGE, width), F32)] * count],
        [((rows, PAD, width), BF16), ((rows, PAD, width), BF16), acc, (3,), (rows,)], SMALL,
    )
    rx1 = exchange(msg1)
    low1, hidden, st2, msg2, og, w2 = call(
        first_half_kernel, "svvvvvhh" + "vvvvvv", (lengths, tok, st1, rx1, affine1, w1, out_grad, kernel2),
        [wide, hid, sums, msg, own, kernel], [products, tab, acc, (2,)], SMALL, flops,
    )
    rx2 = exchange([msg2] * count)
    gs2, grad_low2, bias_part = call(
        branch_grad_kernel, "svvv" + "vvv", (lengths, og, rx1, w2), [taps, wide, ((8, width), F32)], [buf, xs], SMALL, flops,
    )
    low2, da2, gst2, msg3 = call(
        second_norm_kernel, "svvvvv" + "vvvv", (lengths, hidden, grad_low2, st2, rx2, affine2),
        [wide, wide, sums, msg], [tab, acc], SMALL,
    )
    rx3 = exchange([msg3] * count)

    half_acc = ((width // 2, 3 * width), F32)
    send2, low2_hbm = call(
        functools.partial(kernel_grad_kernel, False, PAD), "vv" + "vh", (low2, gs2), [half, wide], [half_acc, (1,)], SMALL,
    )
    got2 = swap(send2, "core", 1)
    (keep2,) = call(
        functools.partial(kernel_grad_kernel, True, PAD), "vv" + "v", (low2, after(gs2, send2)), [half], [half_acc], SMALL,
    )
    half2 = (got2.astype(F32) + after(keep2, *rx3).astype(F32)).astype(BF16)
    grad_hidden, gs1, send1, affine_part2 = call(
        hidden_grad_kernel, "svvvvvvvv" + "hvvv",
        (lengths, low1, after(da2, half2), hidden, st2, rx2, gst2, rx3, affine2),
        [wide, taps, half, ((4 * rows, 2 * width), F32)], [wide, buf, tab, half_acc, (rows,)], SMALL, flops,
    )
    got1 = swap(send1, "core", 1)
    (keep1,) = call(
        functools.partial(kernel_grad_kernel, True, PAD), "vv" + "v", (low1, after(gs1, send1)), [half], [half_acc], SMALL,
    )
    half1 = (got1.astype(F32) + keep1.astype(F32)).astype(BF16)
    both = jnp.concatenate([h.reshape(chips, count, 1, -1, width) for h in (half2, half1)], axis=2)
    both = both.reshape(chips, -1, width)
    grad_hidden = after(grad_hidden, both)
    both = scatter_sum(both, "chip").reshape(count, -1, width)

    da1, gst1, last_part = call(
        first_norm_grad_kernel, "shhhvvvvv" + "hvv",
        (lengths, grad_hidden, kernel1, tokens, st1, rx1, affine1, affine_part2, bias_part),
        [own, sums, ((4 * rows, 4 * width), BF16)],
        [wide, kernel, own, own, ((frames, width), F32), products, tab, acc, ((4 * rows, 4 * width), F32),
         (1 + 2 * rows,), (rows,)],
        LARGE, flops,
    )
    last = sum_over_tm(last_part)
    both = after(both, da1, last)
    affine_grads, unscattered = last.astype(BF16), both
    both = scatter_sum(both, "tm")
    scattered = both
    (block_out,) = call(
        block_out_kernel, "shhhv" + "h", (lengths, low2_hbm, after(tokens, both), kernel2, conv2_bias.reshape(1, width)), [own],
        [wide, own, kernel, products, own, (1 + 2 * rows,), (rows,)], LARGE, flops,
    )
    both = spread(both, "tm")
    (input_grad,) = call(
        input_grad_kernel, "shhhvvvvv" + "h", (lengths, out_grad, after(da1, both), tokens, st1, rx1, gst1, last, affine1), [own],
        [own, own, own, tab, own, (3 * rows,), (rows,)], LARGE,
    )
    mine = affine_grads.reshape(rows, 4, 4 * width)[:, :SEGS].reshape(rows * SEGS, 4 * width)
    style_grad = lax.dot_general(
        mine[:, : 2 * width], fc1_weight, (((1,), (1,)), ((), ())), preferred_element_type=F32
    ) + lax.dot_general(mine[:, 2 * width :], fc2_weight, (((1,), (1,)), ((), ())), preferred_element_type=F32)
    style_grad = style_grad.reshape(style.shape)
    style_pad = jnp.pad(style, ((0, 0), (0, 1), (0, 0))).reshape(rows * 4, -1)
    gathered = gather_rows(jnp.concatenate([affine_grads, style_pad], axis=1), unscattered, scattered)
    both = spread(after(both, block_out, gathered), "chip")
    fc_shape, bias_shape = ((style.shape[2], 2 * width), F32), ((1, 2 * width), F32)
    fc1_grad, fc2_grad, fc1_bias_grad, fc2_bias_grad, conv2_bias_grad = call(
        projection_grad_kernel, "v" + "hhvvv", (gathered,), [fc_shape, fc_shape, bias_shape, bias_shape, ((1, width), F32)],
        [(gathered.shape, BF16), ((style.shape[2], 4 * width), F32), (2,)], SMALL,
    )
    fc1_bias_grad, fc2_bias_grad, conv2_bias_grad = (
        b.reshape(b.shape[1]) for b in (fc1_bias_grad, fc2_bias_grad, conv2_bias_grad)
    )

    both = both.reshape(chips, count, 2, -1, width)
    both, input_grad, *small = lax.optimization_barrier(
        (both, input_grad, style_grad, fc1_grad, fc2_grad, fc1_bias_grad, fc2_bias_grad, conv2_bias_grad)
    )
    style_grad, fc1_grad, fc2_grad, fc1_bias_grad, fc2_bias_grad, conv2_bias_grad = small
    other = swap(both, "core", 1)
    if both.shape[3] % PAD == 0:
        conv_shape = ((3, width, width), F32)
        buffers = [((2, 3, width // 2, width), F32), (2,)]
        sums_own = call(
            functools.partial(assemble_kernel, True), "v" + "hh", (both,), [conv_shape, conv_shape], buffers, SMALL,
        )
        conv2_sum, conv1_sum = call(
            functools.partial(assemble_kernel, False), "vhh" + "hh", (other, *sums_own), [conv_shape, conv_shape], buffers,
            SMALL, aliases=((1, 0), (2, 1)),
        )
    else:
        first = lax.axis_index("core") == 0
        halves = [jnp.where(first, both, other), jnp.where(first, other, both)]
        halves = [jnp.moveaxis(h, 2, 0).reshape(2, 3, width // 2, width) for h in halves]
        conv2_sum, conv1_sum = jnp.concatenate(halves, axis=2).astype(F32)
    return (
        block_out, input_grad, style_grad, fc1_grad, fc1_bias_grad, conv1_sum, fc2_grad, fc2_bias_grad, conv2_sum,
        conv2_bias_grad,
    )


def solution(mesh):
    chips = mesh.shape["dp"] // 2
    mesh = Mesh(mesh.devices.reshape(chips, 2, mesh.shape["tm"]), ("chip", "core", "tm"))
    dp = ("chip", "core")
    return jax.shard_map(
        per_device,
        mesh=mesh,
        in_specs=(
            P(dp, "tm", None),
            P(dp, None),
            P(dp, None, None),
            P(),
            P(),
            P(),
            P(),
            P(),
            P(),
            P(),
            P(dp, "tm", None),
        ),
        out_specs=(
            P(dp, "tm", None),
            P(dp, "tm", None),
            P(dp, None, None),
            P(),
            P(),
            P(),
            P(),
            P(),
            P(),
            P(),
        ),
        check_vma=False,
    )
```
